32 devices in a mesh: grp: 4 (over z), exp: 8 (over y, x, core).
Axes of the slice: x: 2, y: 2, z: 4, core: 2. Of those that a mesh axis runs over, the one named last changes fastest.
Arguments:
- tokens: bfloat16 [32768, 1024], P(('grp', 'exp')), may hold values from -6 to 6
- cotangent: bfloat16 [32768, 1024], P(('grp', 'exp')), may hold values from -6 to 6
- arrival: int32 [32, 1024], P(('grp', 'exp')), may hold values from 0 to 1023, each once within a row
- seq_length: int32 [32], P(('grp', 'exp')), may hold values from 256 to 1024, as said below
- w_q: bfloat16 [1024, 1024], P(('grp', 'exp')), may hold values from -0.1875 to 0.1875
- w_k: bfloat16 [1024, 1024], P(('grp', 'exp')), may hold values from -0.1875 to 0.1875
- w_v: bfloat16 [1024, 1024], P(('grp', 'exp')), may hold values from -0.1875 to 0.1875
- w_o: bfloat16 [1024, 1024], P(('grp', 'exp')), may hold values from -1.5 to 1.5
- ln1_gain: bfloat16 [1024], P(('grp', 'exp')), may hold values from 0.5 to 1.5
- ln1_bias: bfloat16 [1024], P(('grp', 'exp')), may hold values from -1 to 1
- ln2_gain: bfloat16 [1024], P(('grp', 'exp')), may hold values from 0.5 to 1.5
- ln2_bias: bfloat16 [1024], P(('grp', 'exp')), may hold values from -1 to 1
- w_in: bfloat16 [8, 1024, 4096], P('exp'), may hold values from -0.1875 to 0.1875
- w_out: bfloat16 [8, 1024, 4096], P('exp'), may hold values from -0.09375 to 0.09375
Outputs:
- output: bfloat16 [32768, 1024], P(('grp', 'exp'))
- grad_x: bfloat16 [32768, 1024], P(('grp', 'exp'))
- grad_w_q: float32 [1024, 1024], P(('grp', 'exp'))
- grad_w_k: float32 [1024, 1024], P(('grp', 'exp'))
- grad_w_v: float32 [1024, 1024], P(('grp', 'exp'))
- grad_w_o: float32 [1024, 1024], P(('grp', 'exp'))
- grad_ln1_gain: float32 [1024], P(('grp', 'exp'))
- grad_ln1_bias: float32 [1024], P(('grp', 'exp'))
- grad_ln2_gain: float32 [1024], P(('grp', 'exp'))
- grad_ln2_bias: float32 [1024], P(('grp', 'exp'))
- grad_w_in: float32 [8, 1024, 4096], P('exp', None, 'grp')
- grad_w_out: float32 [8, 1024, 4096], P('exp', None, 'grp')
The draws below stay inside these ranges and needn't reach their ends.
Inputs may be any that keep to these rules, and one draw needn't show every extreme that they name: `seq_length`: each entry is 256 or 1024; every group has slots of both kinds.
All inputs are finite; a program needn't handle non-finite values.
Results may differ from the reference program's by a relative error of at most 0.013.
Values may be sent and summed in bfloat16 or wider, within the bound.
No kernel may reach another device: no remote copies, remote signals or barrier semaphores. Data moves between devices by JAX's collectives and lax.ppermute only.
A program may use at most 320 MiB of HBM per device.

```python
import jax
import jax.numpy as jnp
from jax import lax

D = 1024
HEADS = 16
HDIM = 64
FF = 4096
TOK_DEV = 1024
SHORT = 256
SLOT = 128
EXPERTS = 8
TOKENS = 32768
N_GRP = 4
N_EXP = 8
DEVICES = 32


def draw_seq_length(key, part):
    key = jax.random.fold_in(key, 11)
    flag_key, pick_key = jax.random.split(key)
    flags = jax.random.randint(flag_key, (N_GRP, N_EXP), 0, 2)
    picked = jax.random.randint(pick_key, (N_GRP, 1), 0, N_EXP)
    column = jnp.arange(N_EXP)[None, :]
    flags = jnp.where(column == picked, 1, flags)
    flags = jnp.where(column == (picked + 1) % N_EXP, 0, flags)
    return jnp.where(flags == 1, TOK_DEV, SHORT).reshape(N_GRP * N_EXP).astype(jnp.int32)


def block_scale(key, extent, cuts, low, high):
    def one(dim, blocks):
        steps = jax.random.uniform(jax.random.fold_in(jax.random.fold_in(key, 6), dim), (blocks,), jnp.float32, low / len(cuts), high / len(cuts))
        return jnp.repeat(jnp.exp(steps), extent[dim] // blocks).reshape((-1,) + (1,) * (len(extent) - dim - 1))

    level = one(*cuts[0])
    for cut in cuts[1:]:
        level = level * one(*cut)
    return level


def gaussian(own_key, extent, width, most, pieces=(), kind=jnp.bfloat16):
    drawn = jax.random.normal(own_key, extent, jnp.float32) * width
    if len(pieces) > 0:
        drawn = block_scale(own_key, extent, pieces, -0.22, 0.18) * drawn
    return jnp.clip(drawn, min=-most, max=most).astype(kind)


def setup_inputs(seed: int = 0) -> dict:
    arg_keys = jax.random.split(jax.random.key(seed), 15)
    tokens = gaussian(arg_keys[0], (TOKENS, D), 1.0, 6.0, ((0, 32),))
    cotangent = gaussian(arg_keys[1], (TOKENS, D), 1.0, 6.0, ((0, 32),))
    arrival = jax.vmap(lambda own: jax.random.permutation(own, TOK_DEV))(jax.random.split(arg_keys[2], DEVICES)).reshape((DEVICES, TOK_DEV)).astype(jnp.int32)
    seq_length = draw_seq_length(jax.random.fold_in(arg_keys[14], 71), 0)
    w_q = gaussian(arg_keys[4], (D, D), D ** -0.5, 0.1875, ((0, 32),))
    w_k = gaussian(arg_keys[5], (D, D), D ** -0.5, 0.1875, ((0, 32),))
    w_v = gaussian(arg_keys[6], (D, D), D ** -0.5, 0.1875, ((0, 32),))
    w_o = gaussian(arg_keys[7], (D, D), (D // 64) ** -0.5, 1.5, ((0, 32),))
    ln1_gain = jnp.clip(1.0 + 0.1 * jax.random.normal(arg_keys[8], (D,), jnp.float32), 0.5, 1.5).astype(jnp.bfloat16)
    ln1_bias = gaussian(arg_keys[9], (D,), 0.2, 1.0, ((0, 32),))
    ln2_gain = jnp.clip(1.0 + 0.1 * jax.random.normal(arg_keys[10], (D,), jnp.float32), 0.5, 1.5).astype(jnp.bfloat16)
    ln2_bias = gaussian(arg_keys[11], (D,), 0.2, 1.0, ((0, 32),))
    w_in = gaussian(arg_keys[12], (EXPERTS, D, FF), D ** -0.5, 0.1875, ((0, 8),))
    w_out = gaussian(arg_keys[13], (EXPERTS, D, FF), FF ** -0.5, 0.09375, ((0, 8),))
    return dict(tokens=tokens, cotangent=cotangent, arrival=arrival, seq_length=seq_length, w_q=w_q, w_k=w_k, w_v=w_v, w_o=w_o, ln1_gain=ln1_gain, ln1_bias=ln1_bias, ln2_gain=ln2_gain, ln2_bias=ln2_bias, w_in=w_in, w_out=w_out)


HIGHEST = lax.Precision.HIGHEST
EPSILON = 1e-05
NEG_FILL = -1e+30

@jax.custom_vjp
def low(v):
    return lax.optimization_barrier(v.astype(jnp.bfloat16)).astype(jnp.float32)

@jax.custom_vjp
def low_back(v):
    return v

def low_keep(v):
    return (low(v), None)

def low_pass(kept, grad):
    return (grad,)

def back_keep(v):
    return (v, None)

def back_low(kept, grad):
    return (low(grad),)
low.defvjp(low_keep, low_pass)
low_back.defvjp(back_keep, back_low)

def product(left_mat, right_mat):
    return jnp.dot(left_mat, right_mat, precision=HIGHEST, preferred_element_type=jnp.float32)

def product_t(left_mat, right_mat):
    return lax.dot_general(left_mat, right_mat, (((1,), (1,)), ((), ())), precision=HIGHEST, preferred_element_type=jnp.float32)

def layer_norm(inputs, scaling, offset):
    average = lax.optimization_barrier(jnp.mean(inputs, -1, keepdims=True))
    centred = inputs - average
    return centred * lax.rsqrt(lax.optimization_barrier(jnp.mean(centred * centred, -1, keepdims=True)) + EPSILON) * scaling + offset

def to_sequence(tok_rows, arrival):
    grouped = tok_rows.reshape(N_GRP, N_EXP, N_EXP, SLOT, D).transpose(0, 2, 1, 3, 4).reshape(N_GRP * N_EXP, TOK_DEV, D)
    return jnp.take_along_axis(grouped, arrival[:, :, None], axis=1)

def to_expert(seq_rows, arrival):
    lookup = jnp.argsort(arrival, axis=-1).astype(jnp.int32)
    placed = jnp.take_along_axis(seq_rows, lookup[:, :, None], axis=1)
    return placed.reshape(N_GRP, N_EXP, N_EXP, SLOT, D).transpose(0, 2, 1, 3, 4).reshape(N_GRP, N_EXP, TOK_DEV, D)

def attend(slot_rows, seq_len, params):
    w_query, w_key, w_value, w_output, gain_one, bias_one = params
    ln_one = low(layer_norm(slot_rows, gain_one, bias_one))
    queries = low(low_back(product(ln_one, w_query))).reshape(TOK_DEV, HEADS, HDIM)
    keys_all = low(low_back(product(ln_one, w_key))).reshape(TOK_DEV, HEADS, HDIM)
    values_all = low(low_back(product(ln_one, w_value))).reshape(TOK_DEV, HEADS, HDIM)
    scores = low_back(jnp.einsum('phd,thd->hpt', queries, keys_all, precision=HIGHEST) * HDIM ** (-0.5))
    places = jnp.arange(TOK_DEV, dtype=jnp.int32)
    allowed = (places[None, :] <= places[:, None]) & (places[None, :] // seq_len == places[:, None] // seq_len)
    scores = jnp.where(allowed[None], scores, NEG_FILL)
    row_max = lax.optimization_barrier(jnp.max(scores, -1, keepdims=True))
    exp_scores = jnp.exp(scores - row_max)
    soft_probs = low(exp_scores / lax.optimization_barrier(jnp.sum(exp_scores, -1, keepdims=True)))
    attn_rows = jnp.einsum('hpt,thd->phd', soft_probs, values_all, precision=HIGHEST).reshape(TOK_DEV, D)
    attn_low = low(low_back(attn_rows))
    return slot_rows + product(attn_low, w_output)

def forward(tok_float, w_query, w_key, w_value, w_output, gain_one, bias_one, gain_two, bias_two, w_first, w_second, arrival, seq_length):
    seq_in = low_back(to_sequence(tok_float, arrival))
    params = (w_query, w_key, w_value, w_output, gain_one, bias_one)

    def one_slot(pair_in):
        return attend(pair_in[0], pair_in[1], params)
    mixed_rows = lax.map(jax.checkpoint(one_slot), (seq_in, seq_length))
    sent_rows = low(low_back(mixed_rows))
    expert_in = to_expert(sent_rows, arrival).transpose(1, 0, 2, 3).reshape(N_EXP, N_GRP * TOK_DEV, D)

    def one_expert(triple):
        block_rows, first_mat, second_mat = triple
        ln_two = low(layer_norm(block_rows, gain_two, bias_two))
        pre_act = low_back(product(ln_two, first_mat))
        act_low = low(jax.nn.gelu(pre_act))
        return block_rows + product_t(act_low, second_mat)
    result = lax.map(jax.checkpoint(one_expert), (expert_in, w_first, w_second))
    return result.reshape(N_EXP, N_GRP, TOK_DEV, D).transpose(1, 0, 2, 3).reshape(N_GRP * N_EXP * TOK_DEV, D)

def reference(tokens, cotangent, arrival, seq_length, w_q, w_k, w_v, w_o, ln1_gain, ln1_bias, ln2_gain, ln2_bias, w_in, w_out):
    floats = tuple((entry.astype(jnp.float32) for entry in (tokens, w_q, w_k, w_v, w_o, ln1_gain, ln1_bias, ln2_gain, ln2_bias, w_in, w_out)))

    def runner(*entries):
        return forward(*entries, arrival, seq_length)
    result, pullback = jax.vjp(runner, *floats)
    grads = pullback(cotangent.astype(jnp.float32))
    return (result.astype(jnp.bfloat16), grads[0].astype(jnp.bfloat16), grads[1], grads[2], grads[3], grads[4], grads[5], grads[6], grads[7], grads[8], grads[9], grads[10])
```

```python
from functools import partial

import jax
import jax.numpy as jnp
from jax import lax
from jax.experimental import pallas as pl
from jax.experimental.pallas import tpu as pltpu
from jax.sharding import PartitionSpec as P

HDIM = 64
QB = 256
EPSILON = 1e-05
NEG_FILL = -1e30
GELU_A = 0.7978845608028654
GELU_B = 0.044715
BF = jnp.bfloat16
F32 = jnp.float32
MIB = 1024 * 1024


def dot_nn(left, right):
    return lax.dot_general(left, right, (((1,), (0,)), ((), ())), preferred_element_type=F32)


def dot_nt(left, right):
    return lax.dot_general(left, right, (((1,), (1,)), ((), ())), preferred_element_type=F32)


def norm_rows(x):
    centred = x - jnp.mean(x, -1, keepdims=True)
    inverse = lax.rsqrt(jnp.mean(centred * centred, -1, keepdims=True) + EPSILON)
    return centred * inverse, inverse


def norm_back(grad, normed, inverse, gain):
    scaled = grad * gain
    return inverse * (
        scaled
        - jnp.mean(scaled, -1, keepdims=True)
        - normed * jnp.mean(scaled * normed, -1, keepdims=True)
    )


def gelu_both(u):
    sq = u * u
    t = jnp.tanh(GELU_A * u * (1.0 + GELU_B * sq))
    half = 0.5 * (1.0 + t)
    return u * half, half + (0.5 * u) * (1.0 - t * t) * (GELU_A + (3.0 * GELU_A * GELU_B) * sq)


def params(limit):
    return pltpu.CompilerParams(vmem_limit_bytes=limit * MIB)


def cost(gflop, mbytes):
    return pl.CostEstimate(
        flops=int(gflop * 1e9), bytes_accessed=int(mbytes * 1e6), transcendentals=0
    )


def whole(shape):
    return pl.BlockSpec(shape, lambda *_: (0,) * len(shape), pipeline_mode=pl.Buffered(1))


def one_hot(ids, other):
    return jnp.where(ids == other, 1.0, 0.0).astype(BF)


def seq_kernel(parts, rel_ref, gain_ref, bias_ref, *refs):
    chunks, (seq_ref, ln_ref, lnt_ref, rows) = refs[:parts], refs[parts:]
    size = chunks[0].shape[0]
    for k in range(parts):
        rows[k * size : (k + 1) * size] = chunks[k][...]
    total = rows.shape[0]
    for r in range(0, total, QB):
        lanes = lax.broadcasted_iota(jnp.int32, (QB, total), 1)
        x = dot_nn(one_hot(rel_ref[r : r + QB], lanes), rows[...])
        seq_ref[r : r + QB] = x.astype(BF)
        normed, _ = norm_rows(x)
        ln = (normed * gain_ref[...] + bias_ref[...]).astype(BF)
        ln_ref[r : r + QB] = ln
        lnt_ref[:, r : r + QB] = jnp.transpose(ln)


def seq_norm(rel_col, gain, bias, chunks):
    parts, (size, width) = len(chunks), chunks[0].shape
    total = parts * size
    return pl.pallas_call(
        partial(seq_kernel, parts),
        out_shape=[
            jax.ShapeDtypeStruct((total, width), BF),
            jax.ShapeDtypeStruct((total, width), BF),
            jax.ShapeDtypeStruct((width, total), BF),
        ],
        scratch_shapes=[pltpu.VMEM((total, width), BF)],
        compiler_params=params(32),
        cost_estimate=cost(3, 8),
    )(rel_col, gain, bias, *chunks)


def place(meta, refs, full, pick, step):
    groups, experts = full.shape[0], full.shape[1]
    for r in range(experts):
        for z in range(groups):
            row = lax.rem(meta[1] + (groups - z), groups)
            full[row, r ^ meta[0]] = refs[r][z, pick * step : (pick + 1) * step]


def proj_kernel(experts, pick, meta, ln_ref, *refs):
    pieces, (out_ref, full_ref) = refs[:experts], refs[experts:]
    step = full_ref.shape[2]
    place(meta, pieces, full_ref, pick, step)
    width = ln_ref.shape[1]
    out_ref[...] = dot_nn(ln_ref[...], full_ref[...].reshape(width, width)).astype(BF)


def project(meta, ln, pieces, pick):
    experts, groups = len(pieces), pieces[0].shape[0]
    total, width = ln.shape
    step = width // (experts * groups)
    full = (groups, experts, step, width)
    out, mat = pl.pallas_call(
        partial(proj_kernel, experts, pick),
        grid_spec=pltpu.PrefetchScalarGridSpec(
            num_scalar_prefetch=1,
            grid=(1,),
            in_specs=[whole((total, width))] + [whole(p.shape) for p in pieces],
            out_specs=[whole((total, width)), whole(full)],
        ),
        out_shape=[jax.ShapeDtypeStruct((total, width), BF), jax.ShapeDtypeStruct(full, BF)],
        compiler_params=params(32),
        cost_estimate=cost(2.2, 8),
    )(meta, ln, *pieces)
    return out, mat.reshape(width, width)


def attend_kernel(flag, q_ref, k_ref, v_ref, o_ref, lse_ref, lse_cols):
    total = q_ref.shape[0]
    low = lax.broadcasted_iota(jnp.int32, (1, 2 * HDIM), 1) < HDIM
    causal = lax.broadcasted_iota(jnp.int32, (QB, QB), 1) <= lax.broadcasted_iota(
        jnp.int32, (QB, QB), 0
    )

    def run(long):
        for a in range(0, total, QB):
            b = a + QB
            q = q_ref[a:b]
            outs, logs = [], []
            for keep in (low, ~low):
                qh = jnp.where(keep, q, jnp.zeros_like(q)) * BF(HDIM**-0.5)
                near = jnp.where(causal, dot_nt(qh, k_ref[a:b]), NEG_FILL)
                top = jnp.max(near, 1, keepdims=True)
                if long and a > 0:
                    far = dot_nt(qh, k_ref[0:a])
                    top = jnp.maximum(top, jnp.max(far, 1, keepdims=True))
                near = jnp.exp(near - top)
                mass = jnp.sum(near, 1, keepdims=True)
                o = dot_nn(near.astype(BF), v_ref[a:b])
                if long and a > 0:
                    far = jnp.exp(far - top)
                    mass = mass + jnp.sum(far, 1, keepdims=True)
                    o = o + dot_nn(far.astype(BF), v_ref[0:a])
                outs.append(o * (1.0 / mass))
                logs.append(top + jnp.log(mass))
            o_ref[a:b] = jnp.where(low, outs[0], outs[1]).astype(BF)
            lse_cols[a:b] = jnp.where(low, logs[0], logs[1])

    @pl.when(flag[0] > QB)
    def _():
        run(True)

    @pl.when(flag[0] <= QB)
    def _():
        run(False)

    turned = jnp.transpose(lse_cols[...])
    lse_ref[0, 0:1] = turned[0:1]
    lse_ref[0, 1:2] = turned[HDIM : HDIM + 1]


def attend(flag, q, k, v):
    total, width = q.shape
    pair = 2 * HDIM
    block = pl.BlockSpec((total, pair), lambda j, *_: (0, j))
    stat = pl.BlockSpec((1, 8, total), lambda j, *_: (j, 0, 0))
    return pl.pallas_call(
        attend_kernel,
        grid_spec=pltpu.PrefetchScalarGridSpec(
            num_scalar_prefetch=1,
            grid=(width // pair,),
            in_specs=[block] * 3,
            out_specs=[block, stat],
            scratch_shapes=[pltpu.VMEM((total, pair), F32)],
        ),
        out_shape=[
            jax.ShapeDtypeStruct((total, width), BF),
            jax.ShapeDtypeStruct((width // pair, 8, total), F32),
        ],
        compiler_params=params(32),
        cost_estimate=cost(24, 9),
    )(flag, q, k, v)


def attend_back_kernel(
    flag, q_ref, k_ref, v_ref, o_ref, g_ref, lse_ref, dq_ref, dk_ref, dv_ref, dq_turned
):
    total = q_ref.shape[0]
    low = lax.broadcasted_iota(jnp.int32, (1, 2 * HDIM), 1) < HDIM
    causal = lax.broadcasted_iota(jnp.int32, (QB, QB), 0) <= lax.broadcasted_iota(
        jnp.int32, (QB, QB), 1
    )
    prod = jnp.transpose(g_ref[...].astype(F32) * o_ref[...].astype(F32))
    delta = [jnp.sum(prod[h * HDIM : (h + 1) * HDIM], 0, keepdims=True) for h in range(2)]
    k_turned = jnp.transpose(k_ref[...])

    def run(long):
        for a in range(0, total, QB):
            b = a + QB
            ks, vs = k_ref[a:b], v_ref[a:b]
            dks, dvs = [], []
            for h, keep in enumerate((low, ~low)):
                kh = jnp.where(keep, ks, jnp.zeros_like(ks)) * BF(HDIM**-0.5)
                vh = jnp.where(keep, vs, jnp.zeros_like(vs))
                kth = k_turned[h * HDIM : (h + 1) * HDIM, a:b]
                spans = [(a, b)]
                if long and b < total:
                    spans.append((b, total))
                dk = dv = None
                for lo, hi in spans:
                    qs, gs = q_ref[lo:hi], g_ref[lo:hi]
                    probs = jnp.exp(dot_nt(kh, qs) - lse_ref[0, h : h + 1, lo:hi])
                    if lo == a:
                        probs = jnp.where(causal, probs, 0.0)
                    dp = dot_nt(vh, gs)
                    ds = (probs * (dp - delta[h][:, lo:hi])).astype(BF)
                    dv_part, dk_part = dot_nn(probs.astype(BF), gs), dot_nn(ds, qs)
                    dk = dk_part if dk is None else dk + dk_part
                    dv = dv_part if dv is None else dv + dv_part
                    rows = slice(h * HDIM, (h + 1) * HDIM)
                    if a == 0 or not long:
                        dq_turned[rows, lo:hi] = dot_nn(kth, ds)
                    else:
                        dq_turned[rows, lo:hi] += dot_nn(kth, ds)
                dks.append(dk)
                dvs.append(dv)
            dk_ref[a:b] = (jnp.where(low, dks[0], dks[1]) * HDIM**-0.5).astype(BF)
            dv_ref[a:b] = jnp.where(low, dvs[0], dvs[1]).astype(BF)

    @pl.when(flag[0] > QB)
    def _():
        run(True)

    @pl.when(flag[0] <= QB)
    def _():
        run(False)

    dq_ref[...] = (jnp.transpose(dq_turned[...]) * HDIM**-0.5).astype(BF)


def attend_back(flag, q, k, v, o, g, lse):
    total, width = q.shape
    pair = 2 * HDIM
    block = pl.BlockSpec((total, pair), lambda j, *_: (0, j))
    stat = pl.BlockSpec((1, 8, total), lambda j, *_: (j, 0, 0))
    return pl.pallas_call(
        attend_back_kernel,
        grid_spec=pltpu.PrefetchScalarGridSpec(
            num_scalar_prefetch=1,
            grid=(width // pair,),
            in_specs=[block] * 5 + [stat],
            out_specs=[block] * 3,
            scratch_shapes=[pltpu.VMEM((pair, total), F32)],
        ),
        out_shape=[jax.ShapeDtypeStruct((total, width), BF)] * 3,
        compiler_params=params(32),
        cost_estimate=cost(32, 16),
    )(flag, q, k, v, o, g, lse)


def mix_kernel(experts, meta, attn_ref, seq_ref, rel_ref, *refs):
    pieces, rest = refs[:experts], refs[experts:]
    full_ref, outs, mixed = rest[0], rest[1 : 1 + experts], rest[1 + experts]
    step = full_ref.shape[2]
    place(meta, pieces, full_ref, 1, step)
    total, width = mixed.shape
    mat = full_ref[...].reshape(width, width)
    for r in range(0, total, QB):
        x = seq_ref[r : r + QB].astype(F32) + dot_nn(attn_ref[r : r + QB], mat)
        mixed[r : r + QB] = x.astype(BF)
    to_parts(rel_ref, mixed, outs)


def to_parts(rel_ref, rows, outs):
    total, size = rows.shape[0], outs[0].shape[0]
    per = max(1, QB // size)
    for k in range(0, len(outs), per):
        ids = lax.broadcasted_iota(jnp.int32, (per * size, total), 0) + k * size
        moved = dot_nn(one_hot(ids, rel_ref[...]), rows[...]).astype(BF)
        for j in range(per):
            outs[k + j][...] = moved[j * size : (j + 1) * size]


def mix(meta, attn, seq, rel_row, pieces):
    experts, groups = len(pieces), pieces[0].shape[0]
    total, width = attn.shape
    step = width // (experts * groups)
    full = (groups, experts, step, width)
    part = (total // experts, width)
    res = pl.pallas_call(
        partial(mix_kernel, experts),
        grid_spec=pltpu.PrefetchScalarGridSpec(
            num_scalar_prefetch=1,
            grid=(1,),
            in_specs=[whole((total, width))] * 2
            + [whole((1, total))]
            + [whole(p.shape) for p in pieces],
            out_specs=[whole(full)] + [whole(part)] * experts,
            scratch_shapes=[pltpu.VMEM((total, width), BF)],
        ),
        out_shape=[jax.ShapeDtypeStruct(full, BF)] + [jax.ShapeDtypeStruct(part, BF)] * experts,
        compiler_params=params(40),
        cost_estimate=cost(5, 12),
    )(meta, attn, seq, rel_row, *pieces)
    return res[0].reshape(width, width), list(res[1:])


def expert_kernel(parts, steps, meta, *refs):
    chunks = refs[:parts]
    cot_ref, gain_ref, bias_ref, wi_ref, wo_ref = refs[parts : parts + 5]
    out_ref, x_ref = refs[parts + 5 : parts + 7]
    dx_refs = refs[parts + 7 : 2 * parts + 7]
    sums_ref, ln, out_acc, in_acc = refs[2 * parts + 7 :]
    f = pl.program_id(0)
    size = chunks[0].shape[0]
    total, width = ln.shape

    @pl.when(f == 0)
    def _():
        for k in range(parts):
            x = chunks[k][...]
            rows = slice(k * size, (k + 1) * size)
            x_ref[rows] = x
            normed, _ = norm_rows(x.astype(F32))
            ln[rows] = (normed * gain_ref[...] + bias_ref[...]).astype(BF)

    def body(first):
        for r in range(0, total, 512):
            rows = slice(r, r + 512)
            pre = dot_nn(ln[rows], wi_ref[...])
            grad = dot_nn(cot_ref[rows], wo_ref[...])
            act, slope = gelu_both(pre)
            back = (grad * slope).astype(BF)
            o, d = dot_nt(act.astype(BF), wo_ref[...]), dot_nt(back, wi_ref[...])
            if first:
                out_acc[rows], in_acc[rows] = o, d
            else:
                out_acc[rows] += o
                in_acc[rows] += d

    @pl.when(f == 0)
    def _():
        body(True)

    @pl.when(f > 0)
    def _():
        body(False)

    @pl.when(f == steps - 1)
    def _():
        gain_sum = jnp.zeros((1, width), F32)
        bias_sum = gain_sum
        for k in range(parts):
            rows = slice(k * size, (k + 1) * size)
            x = chunks[k][...].astype(F32)
            normed, inverse = norm_rows(x)
            out_ref[k ^ meta[0]] = (x + out_acc[rows]).astype(BF)
            d = in_acc[rows]
            gain_sum = gain_sum + jnp.sum(d * normed, 0, keepdims=True)
            bias_sum = bias_sum + jnp.sum(d, 0, keepdims=True)
            back = norm_back(d, normed, inverse, gain_ref[...])
            dx_refs[k][...] = (cot_ref[rows].astype(F32) + back).astype(BF)
        sums_ref[0:1] = gain_sum
        sums_ref[1:2] = bias_sum


def expert(meta, chunks, cot, gain, bias, w_in, w_out):
    parts, (size, width) = len(chunks), chunks[0].shape
    total, hidden = parts * size, w_in.shape[1]
    tile = 512
    steps = hidden // tile
    cols = pl.BlockSpec((width, tile), lambda f, *_: (0, f))
    res = pl.pallas_call(
        partial(expert_kernel, parts, steps),
        grid_spec=pltpu.PrefetchScalarGridSpec(
            num_scalar_prefetch=1,
            grid=(steps,),
            in_specs=[whole((size, width))] * parts
            + [whole((total, width)), whole((1, width)), whole((1, width)), cols, cols],
            out_specs=[whole((parts, size, width)), whole((total, width))]
            + [whole((size, width))] * parts
            + [whole((8, width))],
            scratch_shapes=[
                pltpu.VMEM((total, width), BF),
                pltpu.VMEM((total, width), F32),
                pltpu.VMEM((total, width), F32),
            ],
        ),
        out_shape=[
            jax.ShapeDtypeStruct((parts, size, width), BF),
            jax.ShapeDtypeStruct((total, width), BF),
        ]
        + [jax.ShapeDtypeStruct((size, width), BF)] * parts
        + [jax.ShapeDtypeStruct((8, width), F32)],
        compiler_params=params(52),
        cost_estimate=cost(40, 28),
    )(meta, *chunks, cot, gain, bias, w_in, w_out)
    return res[0], res[1], list(res[2 : 2 + parts]), res[-1]


def slice_kernel(count, first, last, flags, *refs):
    xs, cots = refs[:count], refs[count : 2 * count]
    gain_ref, bias_ref, wi_ref, wo_ref = refs[2 * count : 2 * count + 4]
    rest = refs[2 * count + 4 :]
    if not first:
        in_prev, out_prev = rest[:2]
        rest = rest[2:]
    in_ref, out_ref, in_acc, out_acc = rest[:4]
    lns = rest[4:]
    f = pl.program_id(0)
    total = xs[0].shape[0]
    if first:
        in_acc[...] = jnp.zeros_like(in_acc)
        out_acc[...] = jnp.zeros_like(out_acc)
    else:
        in_acc[...] = in_prev[...]
        out_acc[...] = out_prev[...]
    for n in range(count):

        @pl.when(flags[n] > 0)
        def _(n=n):
            @pl.when(f == 0)
            def _():
                for r in range(0, total, QB):
                    normed, _ = norm_rows(xs[n][r : r + QB].astype(F32))
                    lns[n][r : r + QB] = (normed * gain_ref[...] + bias_ref[...]).astype(BF)

            pre = dot_nt(wi_ref[...], lns[n][...])
            grad = dot_nt(wo_ref[...], cots[n][...])
            act, slope = gelu_both(pre)
            back = (grad * slope).astype(BF)
            in_acc[...] += dot_nn(back, lns[n][...])
            out_acc[...] += dot_nn(act.astype(BF), cots[n][...])

    if last:
        in_ref[...] = jnp.transpose(in_acc[...])
        out_ref[...] = jnp.transpose(out_acc[...])
    else:
        in_ref[...] = in_acc[...]
        out_ref[...] = out_acc[...]


def slice_grads(flags, xs, cots, gain, bias, wi_turned, wo_turned, prev, last):
    count = len(xs)
    total, width = xs[0].shape
    hidden = wi_turned.shape[0]
    tile = min(256, hidden)
    rows = pl.BlockSpec((tile, width), lambda f, *_: (f, 0))
    cols = pl.BlockSpec((width, tile), lambda f, *_: (0, f))
    first = prev is None
    shape = (width, hidden) if last else (hidden, width)
    return pl.pallas_call(
        partial(slice_kernel, count, first, last),
        grid_spec=pltpu.PrefetchScalarGridSpec(
            num_scalar_prefetch=1,
            grid=(hidden // tile,),
            in_specs=[whole((total, width))] * (2 * count)
            + [whole((1, width))] * 2
            + [rows] * (2 if first else 4),
            out_specs=[cols if last else rows] * 2,
            scratch_shapes=[pltpu.VMEM((tile, width), F32)] * 2
            + [pltpu.VMEM((total, width), BF)] * count,
        ),
        out_shape=[jax.ShapeDtypeStruct(shape, F32)] * 2,
        compiler_params=params(48),
        cost_estimate=cost(10 * count, 8 + 4 * count),
    )(flags, *xs, *cots, gain, bias, wi_turned, wo_turned, *(() if first else prev))


def back_kernel(parts, rel_ref, mat_ref, *refs):
    chunks, (dmix_ref, dattn_ref, rows) = refs[:parts], refs[parts:]
    size = chunks[0].shape[0]
    for k in range(parts):
        rows[k * size : (k + 1) * size] = chunks[k][...]
    total = rows.shape[0]
    for r in range(0, total, QB):
        lanes = lax.broadcasted_iota(jnp.int32, (QB, total), 1)
        x = dot_nn(one_hot(rel_ref[r : r + QB], lanes), rows[...]).astype(BF)
        dmix_ref[r : r + QB] = x
        dattn_ref[r : r + QB] = dot_nt(x, mat_ref[...]).astype(BF)


def back_in(rel_col, mat, chunks):
    parts, (size, width) = len(chunks), chunks[0].shape
    total = parts * size
    return pl.pallas_call(
        partial(back_kernel, parts),
        out_shape=[jax.ShapeDtypeStruct((total, width), BF)] * 2,
        scratch_shapes=[pltpu.VMEM((total, width), BF)],
        compiler_params=params(32),
        cost_estimate=cost(5, 8),
    )(rel_col, mat, *chunks)


def shared_kernel(turn, splits, meta, left_ref, *refs):
    count = len(splits)
    rights, outs, sums = refs[:count], refs[count:-1], refs[-1]
    left = jnp.transpose(left_ref[...]) if turn else left_ref[...]
    for n in range(count):
        size = rights[n].shape[1]
        sums[:, :size] = dot_nn(left, rights[n][...])
        at, cols = splits[n]
        send, keep = outs[2 * at], outs[2 * at + 1]
        half, step = send.shape[0], send.shape[2]
        for r in range(2 * half):
            start = pl.multiple_of((r ^ meta[0]) * step, step)
            ref = send if r % 2 else keep
            ref[r // 2, 0, :, cols : cols + size] = sums[pl.ds(start, step), :size].astype(BF)


def shared_grads(meta, left, rights, splits, widths, experts, groups, turn):
    total, width = rights[0].shape
    features = left.shape[1] if turn else left.shape[0]
    step = features // (experts * groups)
    block = features // groups
    if turn:
        left_spec = pl.BlockSpec((total, block), lambda g, *_: (0, g))
    else:
        left_spec = pl.BlockSpec((block, total), lambda g, *_: (g, 0))
    shapes = [(experts // 2, groups, step, w) for w in widths for _ in range(2)]
    out_specs = [pl.BlockSpec((s[0], 1, s[2], s[3]), lambda g, *_: (0, g, 0, 0)) for s in shapes]
    res = pl.pallas_call(
        partial(shared_kernel, turn, splits),
        grid_spec=pltpu.PrefetchScalarGridSpec(
            num_scalar_prefetch=1,
            grid=(groups,),
            in_specs=[left_spec] + [whole(r.shape) for r in rights],
            out_specs=out_specs,
            scratch_shapes=[pltpu.VMEM((block, width), F32)],
        ),
        out_shape=[jax.ShapeDtypeStruct(s, BF) for s in shapes],
        compiler_params=params(40),
        cost_estimate=cost(2.2 * sum(widths) / 1024, 4 + 4 * sum(widths) / 1024),
    )(meta, left, *rights)
    return [(res[2 * n], res[2 * n + 1]) for n in range(len(widths))]


def first_kernel(steps, parts, *refs):
    dq_ref, dk_ref, dv_ref, wq_ref, wk_ref, wv_ref, seq_ref, dmix_ref, gain_ref, rel_ref = refs[:10]
    outs, sums_ref, rows = refs[10 : 10 + parts], refs[10 + parts], refs[11 + parts]
    r = pl.program_id(0)
    size = dq_ref.shape[0]
    grad = dot_nt(dq_ref[...], wq_ref[...])
    grad = grad + dot_nt(dk_ref[...], wk_ref[...])
    grad = grad + dot_nt(dv_ref[...], wv_ref[...])
    normed, inverse = norm_rows(seq_ref[...].astype(F32))
    gain_sum = jnp.sum(grad * normed, 0, keepdims=True)
    bias_sum = jnp.sum(grad, 0, keepdims=True)

    @pl.when(r == 0)
    def _():
        sums_ref[0:1] = gain_sum
        sums_ref[1:2] = bias_sum

    @pl.when(r > 0)
    def _():
        sums_ref[0:1] += gain_sum
        sums_ref[1:2] += bias_sum

    back = dmix_ref[...].astype(F32) + norm_back(grad, normed, inverse, gain_ref[...])
    rows[pl.ds(pl.multiple_of(r * size, size), size)] = back.astype(BF)

    @pl.when(r == steps - 1)
    def _():
        to_parts(rel_ref, rows, outs)


def first_back(dq, dk, dv, mats, seq, dmix, gain, rel_row, parts):
    total, width = dq.shape
    steps = total // QB
    block = pl.BlockSpec((QB, width), lambda r: (r, 0))
    part = (total // parts, width)
    res = pl.pallas_call(
        partial(first_kernel, steps, parts),
        grid=(steps,),
        in_specs=[block] * 3
        + [whole((width, width))] * 3
        + [block] * 2
        + [whole((1, width)), whole((1, total))],
        out_specs=[whole(part)] * parts + [whole((8, width))],
        out_shape=[jax.ShapeDtypeStruct(part, BF)] * parts + [jax.ShapeDtypeStruct((8, width), F32)],
        scratch_shapes=[pltpu.VMEM((total, width), BF)],
        compiler_params=params(40),
        cost_estimate=cost(9, 20),
    )(dq, dk, dv, *mats, seq, dmix, gain, rel_row)
    return list(res[:parts]), res[-1]


def order_kernel(parts, meta, *refs):
    for k in range(parts):
        refs[parts][k ^ meta[0]] = refs[k][...]


def to_order(meta, chunks):
    parts, (size, width) = len(chunks), chunks[0].shape
    return pl.pallas_call(
        partial(order_kernel, parts),
        grid_spec=pltpu.PrefetchScalarGridSpec(
            num_scalar_prefetch=1,
            grid=(1,),
            in_specs=[whole((size, width))] * parts,
            out_specs=whole((parts, size, width)),
        ),
        out_shape=jax.ShapeDtypeStruct((parts, size, width), BF),
        compiler_params=params(16),
        cost_estimate=cost(0.1, 4),
    )(meta, *chunks)


def local(
    n_grp,
    n_exp,
    tokens,
    cotangent,
    arrival,
    seq_length,
    w_q,
    w_k,
    w_v,
    w_o,
    ln1_gain,
    ln1_bias,
    ln2_gain,
    ln2_bias,
    w_in,
    w_out,
):
    me, grp = lax.axis_index("exp"), lax.axis_index("grp")
    meta = jnp.stack([me, grp]).astype(jnp.int32)
    total, width = tokens.shape
    size = total // n_exp
    step = w_q.shape[0]
    hidden = w_in.shape[2] // n_grp

    def swap(a, k):
        return lax.ppermute(a, "exp", [(i, i ^ k) for i in range(n_exp)])

    def shift(a, k):
        return lax.ppermute(a, "grp", [(i, (i + k) % n_grp) for i in range(n_grp)])

    def exchange(chunks):
        return [chunks[0]] + [swap(chunks[k], k) for k in range(1, n_exp)]

    bits = []
    while 2 ** len(bits) < n_exp:
        bits.append(2 ** len(bits))

    def gather_grp(a):
        return jnp.stack([a] + [shift(a, k) for k in range(1, n_grp)])

    def gather_exp(own, order):
        have = {0: own}
        for b in order:
            have.update({r ^ b: swap(a, b) for r, a in list(have.items())})
        return [have[r] for r in range(n_exp)]

    def line(a):
        ups, downs, up, down = [], [], a, a
        for t in range(1, n_grp):
            up = lax.ppermute(up, "grp", [(i, i + 1) for i in range(t - 1, n_grp - 1)])
            down = lax.ppermute(down, "grp", [(i + 1, i) for i in range(n_grp - t)])
            ups.append(up)
            downs.append(down)
        return ups, downs

    ids = arrival[0]
    rel = ((ids // size) ^ me) * size + ids % size
    rel_row, rel_col = rel[None, :], rel[:, None]
    flag = seq_length

    tok3 = tokens.reshape(n_exp, size, width)
    tok_chunks = [lax.dynamic_index_in_dim(tok3, me ^ k, 0, False) for k in range(n_exp)]
    arrived = exchange(tok_chunks)

    gains = jnp.concatenate([ln1_gain, ln1_bias, ln2_gain, ln2_bias])[None]
    gains = gather_exp(gather_grp(gains), bits[::-1])
    gains = jnp.stack(gains)[:, :, 0]
    gains = jnp.take(gains, jnp.arange(n_exp) ^ me, axis=0)
    gains = jnp.take(gains, (grp - jnp.arange(n_grp)) % n_grp, axis=1)
    gains = gains.reshape(n_exp, n_grp, 4, step).transpose(2, 1, 0, 3).reshape(4, 1, width)
    gains = gains.astype(F32)

    pair_qk = gather_grp(jnp.concatenate([w_q, w_k]))
    pair_vo = gather_grp(jnp.concatenate([w_v, w_o]))
    cot3 = cotangent.reshape(n_exp, size, width)
    cot_chunks = [lax.dynamic_index_in_dim(cot3, me ^ k, 0, False) for k in range(n_exp)]
    cot = jnp.concatenate(cot_chunks)
    pieces_qk = gather_exp(pair_qk, bits[:0:-1] + bits[:1])
    pieces_vo = gather_exp(pair_vo, bits[1:] + bits[:1])

    halves = [cot[: total // 2], cot[total // 2 :]]
    halves, pair_vo = lax.optimization_barrier((halves, pair_vo))
    cot_lines = [line(h) for h in halves]

    w_first, w_second = w_in[0], w_out[0]
    wi_turned = lax.dynamic_slice_in_dim(w_first, grp * hidden, hidden, 1).T
    wo_turned = lax.dynamic_slice_in_dim(w_second, grp * hidden, hidden, 1).T

    seq, ln_one, ln_turned = seq_norm(rel_col, gains[0], gains[1], arrived)
    q, mat_q = project(meta, ln_one, pieces_qk, 0)
    k, mat_k = project(meta, ln_one, pieces_qk, 1)
    v, mat_v = project(meta, ln_one, pieces_vo, 0)
    attn, lse = attend(flag, q, k, v)
    mat_o, leaving = mix(meta, attn, seq, rel_row, pieces_vo)
    x_chunks = exchange(leaving)

    out, x_all, dx_chunks, sums_two = expert(
        meta, x_chunks, cot, gains[2], gains[3], w_first, w_second
    )
    output = out.reshape(total, width)
    half = n_exp // 2
    x_lines = [line(jnp.concatenate(x_chunks[:half])), line(jnp.concatenate(x_chunks[half:]))]

    back = exchange(dx_chunks)
    dmix, dattn = back_in(rel_col, mat_o, back)

    def reduce_exp(pair, order):
        send, keep = pair
        got = swap(send, 1)
        tail = send.shape[1:]
        dims = [2] * (len(bits) - 1)
        keep, got = keep.reshape(dims + list(tail)), got.reshape(dims + list(tail))
        left = list(bits[:0:-1])
        for b in order:
            axis = left.index(b)
            left.remove(b)
            pick = lambda a, n: lax.index_in_dim(a, n, axis, False)
            send = (pick(keep, 1).astype(F32) + pick(got, 1).astype(F32)).astype(BF)
            keep = (pick(keep, 0).astype(F32) + pick(got, 0).astype(F32)).astype(BF)
            got = swap(send, b)
        return keep, got

    def reduce_grp(keep, got):
        both = keep.astype(F32) + got.astype(F32)
        low = both.astype(BF)
        acc = lax.dynamic_index_in_dim(both, grp, 0, False)
        for s in range(1, n_grp):
            sent = lax.dynamic_index_in_dim(low, (grp + s) % n_grp, 0, False)
            acc = acc + shift(sent, s).astype(F32)
        return acc

    def reduce_all(pairs):
        orders = [bits[1:], bits[:0:-1]]
        return jnp.concatenate(
            [reduce_grp(*reduce_exp(pair, orders[n])) for n, pair in enumerate(pairs)], -1
        )

    mid = width // 2
    grad_o = shared_grads(
        meta,
        attn,
        [dmix[:, :mid], dmix[:, mid:]],
        ((0, 0), (1, 0)),
        (mid, mid),
        n_exp,
        n_grp,
        True,
    )
    grad_w_o = reduce_all(grad_o)

    ones = jnp.ones((), jnp.int32)
    sums = None
    for t in range(n_grp):
        if t == 0:
            xs, cots, flags = [x_all], [cot], [ones]
        else:
            xs, cots, flags = [], [], []
            for way in range(2):
                xs.append(jnp.concatenate([p[way][t - 1] for p in x_lines]))
                cots.append(jnp.concatenate([p[way][t - 1] for p in cot_lines]))
                flags.append((grp >= t if way == 0 else grp + t < n_grp).astype(jnp.int32))
        sums = slice_grads(
            jnp.stack(flags),
            xs,
            cots,
            gains[2],
            gains[3],
            wi_turned,
            wo_turned,
            sums,
            t == n_grp - 1,
        )
    grad_w_in, grad_w_out = sums

    dq, dk, dv = attend_back(flag, q, k, v, attn, dattn, lse)
    dx_first, sums_one = first_back(
        dq, dk, dv, (mat_q, mat_k, mat_v), seq, dmix, gains[0], rel_row, n_exp
    )
    grad_x = to_order(meta, exchange(dx_first)).reshape(total, width)
    grads_qkv = shared_grads(
        meta,
        ln_turned,
        [dq, dk[:, :mid], dk[:, mid:], dv],
        ((0, 0), (0, width), (1, 0), (1, mid)),
        (width + mid, width + mid),
        n_exp,
        n_grp,
        False,
    )
    grad_qkv = reduce_all(grads_qkv)

    small = jnp.concatenate([sums_one[:2], sums_two[:2]]).reshape(4, n_grp, n_exp, step)
    small = small.transpose(2, 1, 0, 3).reshape(n_exp, n_grp, 4 * step)
    small = jnp.take(small, jnp.arange(n_exp) ^ me, axis=0)
    for b in bits[::-1]:
        small = small[:b] + swap(small[b:], b)
    small = small[0]
    acc = lax.dynamic_index_in_dim(small, grp, 0, True)
    for s in range(1, n_grp):
        acc = acc + shift(lax.dynamic_index_in_dim(small, (grp + s) % n_grp, 0, True), s)
    small = acc.reshape(4, step)

    return (
        output,
        grad_x,
        grad_qkv[:, :width],
        grad_qkv[:, width : 2 * width],
        grad_qkv[:, 2 * width :],
        grad_w_o,
        small[0],
        small[1],
        small[2],
        small[3],
        grad_w_in[None],
        grad_w_out[None],
    )


def solution(mesh):
    both = ("grp", "exp")
    rows, flat, mats = P(both, None), P(both), P("exp", None, None)
    split = P("exp", None, "grp")
    return jax.shard_map(
        partial(local, mesh.shape["grp"], mesh.shape["exp"]),
        mesh=mesh,
        in_specs=(rows, rows, rows, flat) + (rows,) * 4 + (flat,) * 4 + (mats, mats),
        out_specs=(rows,) * 6 + (flat,) * 4 + (split, split),
        check_vma=False,
    )
```

```python
from functools import partial

import jax
import jax.numpy as jnp
from jax import lax
from jax.experimental import pallas as pl
from jax.experimental.pallas import tpu as pltpu
from jax.sharding import PartitionSpec as P

HDIM = 64
QB = 256
EPSILON = 1e-05
NEG_FILL = -1e30
GELU_A = 0.7978845608028654
GELU_B = 0.044715
BF = jnp.bfloat16
F32 = jnp.float32
MIB = 1024 * 1024


def dot_nn(left, right):
    return lax.dot_general(left, right, (((1,), (0,)), ((), ())), preferred_element_type=F32)


def dot_nt(left, right):
    return lax.dot_general(left, right, (((1,), (1,)), ((), ())), preferred_element_type=F32)


def norm_rows(x):
    centred = x - jnp.mean(x, -1, keepdims=True)
    inverse = lax.rsqrt(jnp.mean(centred * centred, -1, keepdims=True) + EPSILON)
    return centred * inverse, inverse


def norm_back(grad, normed, inverse, gain):
    scaled = grad * gain
    return inverse * (
        scaled
        - jnp.mean(scaled, -1, keepdims=True)
        - normed * jnp.mean(scaled * normed, -1, keepdims=True)
    )


def gelu_both(u):
    sq = u * u
    t = jnp.tanh(GELU_A * u * (1.0 + GELU_B * sq))
    half = 0.5 * (1.0 + t)
    return u * half, half + (0.5 * u) * (1.0 - t * t) * (GELU_A + (3.0 * GELU_A * GELU_B) * sq)


def run(
    kernel,
    args,
    out_shape,
    deps=(),
    scalars=(),
    grid=(1,),
    specs=None,
    outs=None,
    scratch=(),
    micros=5,
    gates=(),
):
    specs = [whole(a.shape) for a in args] if specs is None else specs
    outs = [whole(o.shape) for o in out_shape] if outs is None else outs
    gates, deps = jax.tree.leaves(gates), jax.tree.leaves(deps)
    first, count, results = len(scalars) + len(args), len(deps) + len(gates), len(out_shape)

    def body(*refs):
        last = first + count + results
        kernel(*refs[:first], *refs[first + count : last], *refs[last + len(gates) :])

    anywhere = pl.BlockSpec(memory_space=pl.ANY)
    res = pl.pallas_call(
        body,
        grid_spec=pltpu.PrefetchScalarGridSpec(
            num_scalar_prefetch=len(scalars),
            grid=grid,
            in_specs=list(specs) + [anywhere] * count,
            out_specs=list(outs) + [anywhere] * len(gates),
            scratch_shapes=list(scratch),
        ),
        out_shape=list(out_shape) + [shaped(g.shape, g.dtype) for g in gates],
        input_output_aliases={first + len(deps) + n: results + n for n in range(len(gates))},
        compiler_params=pltpu.CompilerParams(vmem_limit_bytes=60 * MIB),
        cost_estimate=pl.CostEstimate(
            flops=int(micros * 0.517e9), bytes_accessed=10**6, transcendentals=0
        ),
    )(*scalars, *args, *deps, *gates)
    return (list(res[:results]), list(res[results:])) if gates else res


def shaped(shape, dtype=BF):
    return jax.ShapeDtypeStruct(tuple(shape), dtype)


def whole(shape):
    return pl.BlockSpec(shape, lambda *_: (0,) * len(shape), pipeline_mode=pl.Buffered(1))


def one_hot(ids, other):
    return jnp.where(ids == other, 1.0, 0.0).astype(BF)


def seq_kernel(count, ids_ref, rows_ref, *refs):
    pieces, (seq_ref, ln_ref, lnt_ref, *gain_refs) = refs[:count], refs[count:]
    gains = 0.0
    for piece in pieces:
        for z in range(piece.shape[0]):
            gains = gains + piece[z].astype(F32)
    for n, ref in enumerate(gain_refs):
        ref[...] = gains[n : n + 1]
    total = rows_ref.shape[0]
    for r in range(0, total, QB):
        lanes = lax.broadcasted_iota(jnp.int32, (QB, total), 1)
        x = dot_nn(one_hot(ids_ref[r : r + QB], lanes), rows_ref[...])
        seq_ref[r : r + QB] = x.astype(BF)
        normed, _ = norm_rows(x)
        ln = (normed * gains[0:1] + gains[1:2]).astype(BF)
        ln_ref[r : r + QB] = ln
        lnt_ref[:, r : r + QB] = jnp.transpose(ln)


def seq_norm(ids_col, rows, pieces, deps=()):
    total, width = rows.shape
    groups = pieces[0][0].shape[0]
    res = run(
        partial(seq_kernel, len(pieces)),
        (ids_col, rows, *[a for a, _ in pieces]),
        [shaped((total, width)), shaped((total, width)), shaped((width, total))]
        + [shaped((1, width), F32)] * 4,
        deps,
        specs=[whole(ids_col.shape), whole(rows.shape)]
        + [pl.BlockSpec((groups, 16, width), lambda i, n=n: (0, n, 0)) for _, n in pieces],
        micros=6,
    )
    return *res[:3], res[3:]


def place(meta, refs, full):
    groups, experts = full.shape[0], full.shape[1]
    for r in range(experts):
        for z in range(groups):
            row = lax.rem(meta[1] + (groups - z), groups)
            if len(refs) == 1:
                full[row, r] = refs[0][r, z]
            else:
                full[row, r ^ meta[0]] = refs[r][z]


def piece_specs(pieces, step):
    specs = []
    for array, n in pieces:
        shape = (*array.shape[:-2], step, array.shape[-1])
        at = (0,) * (len(shape) - 2) + (n, 0)
        specs.append(pl.BlockSpec(shape, lambda *_, at=at: at, pipeline_mode=pl.Buffered(1)))
    return specs


def stack_kernel(groups, *refs):
    ins, outs = refs[:groups], refs[groups:]
    for z in range(groups):
        row = 0
        for out in outs:
            out[z] = ins[z][row : row + out.shape[1]]
            row += out.shape[1]


def stack(blocks, rows, deps=()):
    width = blocks[0].shape[1]
    return run(
        partial(stack_kernel, len(blocks)),
        blocks,
        [shaped((len(blocks), r, width)) for r in rows],
        deps,
        micros=2,
    )


def proj_kernel(count, meta, ln_ref, *refs):
    pieces, (out_ref, full_ref) = refs[:count], refs[count:]
    place(meta, pieces, full_ref)
    width = ln_ref.shape[1]
    out_ref[...] = dot_nn(ln_ref[...], full_ref[...].reshape(width, width)).astype(BF)


def project(meta, ln, pieces, full, deps=(), gates=()):
    width = ln.shape[1]
    res = run(
        partial(proj_kernel, len(pieces)),
        (ln, *[a for a, _ in pieces]),
        [shaped(ln.shape), shaped(full)],
        deps,
        (meta,),
        specs=[whole(ln.shape)] + piece_specs(pieces, full[2]),
        gates=gates,
    )
    (out, mat), *gates = res if gates else (res,)
    return (out, mat.reshape(width, width), *gates)


def attend_kernel(flag, q_ref, k_ref, v_ref, o_ref, lse_ref, lse_cols):
    total = q_ref.shape[0]
    low = lax.broadcasted_iota(jnp.int32, (1, 2 * HDIM), 1) < HDIM
    causal = lax.broadcasted_iota(jnp.int32, (QB, QB), 1) <= lax.broadcasted_iota(
        jnp.int32, (QB, QB), 0
    )

    def run(long):
        for a in range(0, total, QB):
            b = a + QB
            q = q_ref[a:b]
            outs, logs = [], []
            for keep in (low, ~low):
                qh = jnp.where(keep, q, jnp.zeros_like(q)) * BF(HDIM**-0.5)
                near = jnp.where(causal, dot_nt(qh, k_ref[a:b]), NEG_FILL)
                top = jnp.max(near, 1, keepdims=True)
                if long and a > 0:
                    far = dot_nt(qh, k_ref[0:a])
                    top = jnp.maximum(top, jnp.max(far, 1, keepdims=True))
                near = jnp.exp(near - top)
                mass = jnp.sum(near, 1, keepdims=True)
                o = dot_nn(near.astype(BF), v_ref[a:b])
                if long and a > 0:
                    far = jnp.exp(far - top)
                    mass = mass + jnp.sum(far, 1, keepdims=True)
                    o = o + dot_nn(far.astype(BF), v_ref[0:a])
                outs.append(o * (1.0 / mass))
                logs.append(top + jnp.log(mass))
            o_ref[a:b] = jnp.where(low, outs[0], outs[1]).astype(BF)
            lse_cols[a:b] = jnp.where(low, logs[0], logs[1])

    @pl.when(flag[0] > QB)
    def _():
        run(True)

    @pl.when(flag[0] <= QB)
    def _():
        run(False)

    turned = jnp.transpose(lse_cols[...])
    lse_ref[0, 0:1] = turned[0:1]
    lse_ref[0, 1:2] = turned[HDIM : HDIM + 1]


def attend(flag, q, k, v, deps=()):
    total, width = q.shape
    pair = 2 * HDIM
    block = pl.BlockSpec((total, pair), lambda j, *_: (0, j))
    stat = pl.BlockSpec((1, 8, total), lambda j, *_: (j, 0, 0))
    return run(
        attend_kernel,
        (q, k, v),
        [shaped((total, width)), shaped((width // pair, 8, total), F32)],
        deps,
        (flag,),
        (width // pair,),
        [block] * 3,
        [block, stat],
        [pltpu.VMEM((total, pair), F32)],
        micros=30,
    )


def attend_back_kernel(
    flag, q_ref, k_ref, v_ref, o_ref, g_ref, lse_ref, dq_ref, dk_ref, dv_ref, dq_turned
):
    total = q_ref.shape[0]
    low = lax.broadcasted_iota(jnp.int32, (1, 2 * HDIM), 1) < HDIM
    causal = lax.broadcasted_iota(jnp.int32, (QB, QB), 0) <= lax.broadcasted_iota(
        jnp.int32, (QB, QB), 1
    )
    prod = jnp.transpose(g_ref[...].astype(F32) * o_ref[...].astype(F32))
    delta = [jnp.sum(prod[h * HDIM : (h + 1) * HDIM], 0, keepdims=True) for h in range(2)]
    k_turned = jnp.transpose(k_ref[...])

    def run(long):
        for a in range(0, total, QB):
            b = a + QB
            ks, vs = k_ref[a:b], v_ref[a:b]
            dks, dvs = [], []
            for h, keep in enumerate((low, ~low)):
                kh = jnp.where(keep, ks, jnp.zeros_like(ks)) * BF(HDIM**-0.5)
                vh = jnp.where(keep, vs, jnp.zeros_like(vs))
                kth = k_turned[h * HDIM : (h + 1) * HDIM, a:b]
                spans = [(a, b)]
                if long and b < total:
                    spans.append((b, total))
                dk = dv = None
                for lo, hi in spans:
                    qs, gs = q_ref[lo:hi], g_ref[lo:hi]
                    probs = jnp.exp(dot_nt(kh, qs) - lse_ref[0, h : h + 1, lo:hi])
                    if lo == a:
                        probs = jnp.where(causal, probs, 0.0)
                    dp = dot_nt(vh, gs)
                    ds = (probs * (dp - delta[h][:, lo:hi])).astype(BF)
                    dv_part, dk_part = dot_nn(probs.astype(BF), gs), dot_nn(ds, qs)
                    dk = dk_part if dk is None else dk + dk_part
                    dv = dv_part if dv is None else dv + dv_part
                    rows = slice(h * HDIM, (h + 1) * HDIM)
                    if a == 0 or not long:
                        dq_turned[rows, lo:hi] = dot_nn(kth, ds)
                    else:
                        dq_turned[rows, lo:hi] += dot_nn(kth, ds)
                dks.append(dk)
                dvs.append(dv)
            dk_ref[a:b] = (jnp.where(low, dks[0], dks[1]) * HDIM**-0.5).astype(BF)
            dv_ref[a:b] = jnp.where(low, dvs[0], dvs[1]).astype(BF)

    @pl.when(flag[0] > QB)
    def _():
        run(True)

    @pl.when(flag[0] <= QB)
    def _():
        run(False)

    dq_ref[...] = (jnp.transpose(dq_turned[...]) * HDIM**-0.5).astype(BF)


def attend_back(flag, q, k, v, o, g, lse, first, count, deps=(), gates=()):
    total = q.shape[0]
    pair = 2 * HDIM
    block = pl.BlockSpec((total, pair), lambda j, *_: (0, j + first))
    stat = pl.BlockSpec((1, 8, total), lambda j, *_: (j + first, 0, 0))
    done = pl.BlockSpec((total, pair), lambda j, *_: (0, j))
    return run(
        attend_back_kernel,
        (q, k, v, o, g, lse),
        [shaped((total, pair * count))] * 3,
        deps,
        (flag,),
        (count,),
        [block] * 5 + [stat],
        [done] * 3,
        [pltpu.VMEM((pair, total), F32)],
        micros=20,
        gates=gates,
    )


def mix_kernel(count, meta, attn_ref, seq_ref, ids_ref, *refs):
    pieces, (full_ref, out_ref, mixed) = refs[:count], refs[count:]
    place(meta, pieces, full_ref)
    total, width = mixed.shape
    mat = full_ref[...].reshape(width, width)
    for r in range(0, total, QB):
        x = seq_ref[r : r + QB].astype(F32) + dot_nn(attn_ref[r : r + QB], mat)
        mixed[r : r + QB] = x.astype(BF)
    to_experts(ids_ref, mixed, out_ref)


def to_experts(ids_ref, rows, out_ref):
    total = rows.shape[0]
    for r in range(0, total, QB):
        want = lax.broadcasted_iota(jnp.int32, (QB, total), 0) + r
        out_ref[r : r + QB] = dot_nn(one_hot(want, ids_ref[...]), rows[...]).astype(BF)


def mix(meta, attn, seq, ids_row, pieces, full, deps=()):
    width = attn.shape[1]
    mat, out = run(
        partial(mix_kernel, len(pieces)),
        (attn, seq, ids_row, *[a for a, _ in pieces]),
        [shaped(full), shaped(attn.shape)],
        deps,
        (meta,),
        specs=[whole(attn.shape)] * 2 + [whole(ids_row.shape)] + piece_specs(pieces, full[2]),
        scratch=[pltpu.VMEM(attn.shape, BF)],
        micros=9,
    )
    return mat.reshape(width, width), out


def act_grad_kernel(cot_ref, wo_ref, out_ref):
    out_ref[...] = dot_nn(cot_ref[...], wo_ref[...]).astype(BF)


def act_grad(cot, w_out, deps=()):
    total, width = cot.shape
    hidden, tile = w_out.shape[1], 512
    return run(
        act_grad_kernel,
        (cot, w_out),
        [shaped((total, hidden))],
        deps,
        (),
        (hidden // tile,),
        [whole(cot.shape), pl.BlockSpec((width, tile), lambda f: (0, f))],
        [pl.BlockSpec((total, tile), lambda f: (0, f))],
        micros=11,
    )[0]


def expert_kernel(
    steps, x_ref, cot_ref, gain_ref, bias_ref, wi_ref, dact_ref, act_ref, dx_ref, sums_ref, ln, acc
):
    f = pl.program_id(0)
    total, width = ln.shape

    @pl.when(f == 0)
    def _():
        for r in range(0, total, QB):
            normed, _ = norm_rows(x_ref[r : r + QB].astype(F32))
            ln[r : r + QB] = (normed * gain_ref[...] + bias_ref[...]).astype(BF)

    def body(first):
        for r in range(0, total, 512):
            rows = slice(r, r + 512)
            act, slope = gelu_both(dot_nn(ln[rows], wi_ref[...]))
            act_ref[rows] = act.astype(BF)
            back = (dact_ref[rows].astype(F32) * slope).astype(BF)
            if first:
                acc[rows] = dot_nt(back, wi_ref[...])
            else:
                acc[rows] += dot_nt(back, wi_ref[...])

    @pl.when(f == 0)
    def _():
        body(True)

    @pl.when(f > 0)
    def _():
        body(False)

    @pl.when(f == steps - 1)
    def _():
        gain_sum = jnp.zeros((1, width), F32)
        bias_sum = gain_sum
        for r in range(0, total, QB):
            rows = slice(r, r + QB)
            normed, inverse = norm_rows(x_ref[rows].astype(F32))
            d = acc[rows]
            gain_sum = gain_sum + jnp.sum(d * normed, 0, keepdims=True)
            bias_sum = bias_sum + jnp.sum(d, 0, keepdims=True)
            back = norm_back(d, normed, inverse, gain_ref[...])
            dx_ref[rows] = (cot_ref[rows].astype(F32) + back).astype(BF)
        sums_ref[0:1] = gain_sum
        sums_ref[1:2] = bias_sum


def expert(x, cot, gain, bias, w_in, dact, deps=()):
    total, width = x.shape
    hidden, tile = w_in.shape[1], 512
    steps = hidden // tile
    cols = pl.BlockSpec((width, tile), lambda f: (0, f))
    rows = pl.BlockSpec((total, tile), lambda f: (0, f))
    return run(
        partial(expert_kernel, steps),
        (x, cot, gain, bias, w_in, dact),
        [shaped((total, hidden)), shaped(x.shape), shaped((8, width), F32)],
        deps,
        (),
        (steps,),
        [whole(x.shape)] * 2 + [whole((1, width))] * 2 + [cols, rows],
        [rows, whole(x.shape), whole((8, width))],
        [pltpu.VMEM(x.shape, BF), pltpu.VMEM(x.shape, F32)],
        micros=34,
    )


def expert_out_kernel(x_ref, act_ref, wo_ref, out_ref):
    out = x_ref[...].astype(F32) + dot_nt(act_ref[...], wo_ref[...])
    out_ref[...] = out.astype(BF)


def expert_out(x, act, w_out, deps=()):
    total, width = x.shape
    hidden, tile = w_out.shape[1], 256
    part = pl.BlockSpec((total, tile), lambda n: (0, n))
    return run(
        expert_out_kernel,
        (x, act, w_out),
        [shaped(x.shape)],
        deps,
        (),
        (width // tile,),
        [part, whole(act.shape), pl.BlockSpec((tile, hidden), lambda n: (n, 0))],
        [part],
        micros=12,
    )[0]


def turn_kernel(meta, wi_ref, wo_ref, wit_ref, wot_ref):
    wit_ref[...] = jnp.transpose(wi_ref[...])
    wot_ref[...] = jnp.transpose(wo_ref[...])


def turn_slices(meta, w_in, w_out, hidden):
    width, tile = w_in.shape[0], min(256, hidden)
    tiles = hidden // tile
    cols = pl.BlockSpec((width, tile), lambda f, m: (0, m[1] * tiles + f))
    rows = pl.BlockSpec((tile, width), lambda f, m: (f, 0))
    return run(
        turn_kernel,
        (w_in, w_out),
        [shaped((hidden, width))] * 2,
        (),
        (meta,),
        (tiles,),
        [cols] * 2,
        [rows] * 2,
        micros=5,
    )


def slice_kernel(count, first, last, flags, *refs):
    xs, cots = refs[:count], refs[count : 2 * count]
    gain_ref, bias_ref, wi_ref, wo_ref = refs[2 * count : 2 * count + 4]
    rest = refs[2 * count + 4 :]
    if not first:
        in_prev, out_prev = rest[:2]
        rest = rest[2:]
    in_ref, out_ref, in_acc, out_acc, lns, rows, sems = rest
    f = pl.program_id(0)
    total = lns.shape[1]

    def copies(n):
        return (
            pltpu.make_async_copy(xs[n], lns.at[n], sems.at[n, 0]),
            pltpu.make_async_copy(cots[n], rows.at[n], sems.at[n, 1]),
        )

    for n in range(count):

        @pl.when((f == 0) & (flags[n] > 0))
        def _(n=n):
            for copy in copies(n):
                copy.start()

    if first:
        in_acc[...] = jnp.zeros_like(in_acc)
        out_acc[...] = jnp.zeros_like(out_acc)
    else:
        in_acc[...] = in_prev[...]
        out_acc[...] = out_prev[...]
    for n in range(count):

        @pl.when(flags[n] > 0)
        def _(n=n):
            @pl.when(f == 0)
            def _():
                for copy in copies(n):
                    copy.wait()
                for r in range(0, total, QB):
                    normed, _ = norm_rows(lns[n, r : r + QB].astype(F32))
                    lns[n, r : r + QB] = (normed * gain_ref[...] + bias_ref[...]).astype(BF)

            pre = dot_nt(wi_ref[...], lns[n])
            grad = dot_nt(wo_ref[...], rows[n])
            act, slope = gelu_both(pre)
            back = (grad * slope).astype(BF)
            in_acc[...] += dot_nn(back, lns[n])
            out_acc[...] += dot_nn(act.astype(BF), rows[n])

    if last:
        in_ref[...] = jnp.transpose(in_acc[...])
        out_ref[...] = jnp.transpose(out_acc[...])
    else:
        in_ref[...] = in_acc[...]
        out_ref[...] = out_acc[...]


def slice_grads(flags, xs, cots, gain, bias, wi_turned, wo_turned, prev, last, deps=()):
    count = len(xs)
    total, width = xs[0].shape
    hidden = wi_turned.shape[0]
    tile = min(256, hidden)
    rows = pl.BlockSpec((tile, width), lambda f, *_: (f, 0))
    cols = pl.BlockSpec((width, tile), lambda f, *_: (0, f))
    anywhere = pl.BlockSpec(memory_space=pl.ANY)
    first = prev is None
    return run(
        partial(slice_kernel, count, first, last),
        (*xs, *cots, gain, bias, wi_turned, wo_turned, *(() if first else prev)),
        [shaped((width, hidden) if last else (hidden, width), F32)] * 2,
        deps,
        (flags,),
        (hidden // tile,),
        [anywhere] * (2 * count)
        + [whole((1, width))] * 2
        + [rows] * (2 if first else 4),
        [cols if last else rows] * 2,
        [pltpu.VMEM((tile, width), F32)] * 2
        + [pltpu.VMEM((count, total, width), BF)] * 2
        + [pltpu.SemaphoreType.DMA((count, 2))],
        micros=18,
    )


def back_kernel(ids_ref, mat_ref, rows_ref, dmix_ref, dattn_ref):
    total = rows_ref.shape[0]
    for r in range(0, total, QB):
        lanes = lax.broadcasted_iota(jnp.int32, (QB, total), 1)
        x = dot_nn(one_hot(ids_ref[r : r + QB], lanes), rows_ref[...]).astype(BF)
        dmix_ref[r : r + QB] = x
        dattn_ref[r : r + QB] = dot_nt(x, mat_ref[...]).astype(BF)


def back_in(ids_col, mat, rows, deps=(), gates=()):
    return run(back_kernel, (ids_col, mat, rows), [shaped(rows.shape)] * 2, deps, gates=gates)


def shared_kernel(picks, turns, sums_in, meta, *refs):
    lefts, rights = refs[: len(turns)], refs[len(turns) : len(turns) + len(picks)]
    rest = refs[len(turns) + len(picks) :]
    small, (send, keep, sums) = rest[:sums_in], rest[sums_in:]
    half, step = send.shape[0], send.shape[2]
    turned = [jnp.transpose(l[...]) if t else l[...] for l, t in zip(lefts, turns)]

    def put(cols, size):
        for r in range(2 * half):
            row = pl.multiple_of((r ^ meta[0]) * step, step)
            ref = send if r % 2 else keep
            ref[r // 2, 0, :, cols : cols + size] = sums[pl.ds(row, step), :size].astype(BF)

    cols = 0
    for pick, right in zip(picks, rights):
        size = right.shape[1]
        sums[:, :size] = dot_nn(turned[pick], right[...])
        put(cols, size)
        cols += size
    if sums_in:
        sums[:, :128] = jnp.zeros((sums.shape[0], 128), F32)
        for n in range(sums_in):
            sums[:, 8 * n : 8 * n + 8] = jnp.transpose(small[n][...])
        put(cols, 128)


def shared_grads(meta, lefts, terms, small, experts, groups, deps=(), gates=()):
    total = terms[0][1].shape[0]
    array, is_turned = lefts[0]
    features = array.shape[0 if is_turned else 1]
    step, block = features // (experts * groups), features // groups
    width = sum(r.shape[1] for _, r in terms) + (128 if small else 0)
    as_is = pl.BlockSpec((block, total), lambda g, *_: (g, 0))
    to_turn = pl.BlockSpec((total, block), lambda g, *_: (0, g))
    sums = pl.BlockSpec((8, block), lambda g, *_: (0, g))
    shape = (experts // 2, groups, step, width)
    spec = pl.BlockSpec((shape[0], 1, step, width), lambda g, *_: (0, g, 0, 0))
    return run(
        partial(shared_kernel, [p for p, _ in terms], [not t for _, t in lefts], len(small)),
        (*[a for a, _ in lefts], *[r for _, r in terms], *small),
        [shaped(shape)] * 2,
        deps,
        (meta,),
        (groups,),
        [as_is if t else to_turn for _, t in lefts]
        + [whole(r.shape) for _, r in terms]
        + [sums] * len(small),
        [spec] * 2,
        [pltpu.VMEM((block, max(r.shape[1] for _, r in terms)), F32)],
        micros=8,
        gates=gates,
    )


def halve_kernel(keep_ref, got_ref, *outs):
    for r, out in enumerate(outs):
        both = keep_ref[r].astype(F32) + got_ref[r].astype(F32)
        out[...] = both.astype(out.dtype)


def halve(keep, got, deps=()):
    chips, tail = keep.shape[0], keep.shape[1:]
    kinds = [F32] + [BF] * (chips - 1)
    return run(halve_kernel, (keep, got), [shaped(tail, k) for k in kinds], deps, micros=2)


def total_kernel(own_ref, *refs):
    ins, (all_ref, low_ref) = refs[:-2], refs[-2:]
    total = own_ref[...]
    for ref in ins:
        total = total + ref[...].astype(F32)
    all_ref[...] = total
    low_ref[...] = total.astype(BF)


def total_of(own, others):
    return run(
        total_kernel,
        (own, *others),
        [shaped(own.shape, F32), shaped(own.shape)],
        micros=2,
    )


def final_kernel(count, heads, meta, *refs):
    owns, ins = refs[:2], refs[2 : 2 + 2 * count]
    o_ref, q_ref, k_ref, v_ref, small_ref = refs[2 + 2 * count :]
    first = owns[0][meta[1]]
    second = owns[1][meta[1]]
    for n in range(count):
        first = first + ins[2 * n][...].astype(F32)
        second = second + ins[2 * n + 1][...].astype(F32)
    width = o_ref.shape[1]
    o_ref[...] = first[:, :width]
    for n, ref in enumerate((q_ref, k_ref, v_ref)):
        ref[:, :heads] = first[:, width + n * heads : width + (n + 1) * heads]
        ref[:, heads:] = second[:, n * heads : (n + 1) * heads]
    small_ref[...] = second[:, 3 * heads :]


def final(meta, owns, pairs):
    step = owns[0].shape[1]
    heads = (owns[1].shape[2] - 128) // 3
    width = owns[0].shape[2] - 3 * heads
    return run(
        partial(final_kernel, len(pairs), heads),
        (*owns, *[a for p in pairs for a in p]),
        [shaped((step, width), F32)] * 4 + [shaped((step, 128), F32)],
        (),
        (meta,),
        micros=2,
    )


def first_kernel(steps, count, *refs):
    grads, mats = refs[: 3 * count], refs[3 * count : 3 * count + 3]
    seq_ref, dmix_ref, gain_ref, ids_ref, out_ref, sums_ref, rows = refs[3 * count + 3 :]
    r = pl.program_id(0)
    size, part = grads[0].shape
    grad = None
    for n in range(3):
        for j in range(count):
            term = dot_nt(grads[n * count + j][...], mats[n][:, j * part : (j + 1) * part])
            grad = term if grad is None else grad + term
    normed, inverse = norm_rows(seq_ref[...].astype(F32))
    gain_sum = jnp.sum(grad * normed, 0, keepdims=True)
    bias_sum = jnp.sum(grad, 0, keepdims=True)

    @pl.when(r == 0)
    def _():
        sums_ref[0:1] = gain_sum
        sums_ref[1:2] = bias_sum

    @pl.when(r > 0)
    def _():
        sums_ref[0:1] += gain_sum
        sums_ref[1:2] += bias_sum

    back = dmix_ref[...].astype(F32) + norm_back(grad, normed, inverse, gain_ref[...])
    rows[pl.ds(pl.multiple_of(r * size, size), size)] = back.astype(BF)

    @pl.when(r == steps - 1)
    def _():
        to_experts(ids_ref, rows, out_ref)


def first_back(dqs, dks, dvs, mats, seq, dmix, gain, ids_row, deps=(), gates=()):
    total, width = seq.shape
    steps, count = total // QB, len(dqs)
    block = pl.BlockSpec((QB, width), lambda r: (r, 0))
    part = pl.BlockSpec((QB, width // count), lambda r: (r, 0))
    return run(
        partial(first_kernel, steps, count),
        (*dqs, *dks, *dvs, *mats, seq, dmix, gain, ids_row),
        [shaped((total, width)), shaped((8, width), F32)],
        deps,
        (),
        (steps,),
        [part] * (3 * count)
        + [whole((width, width))] * 3
        + [block] * 2
        + [whole((1, width)), whole((1, total))],
        scratch=[pltpu.VMEM((total, width), BF)],
        micros=12,
        gates=gates,
    )


def local(
    n_grp,
    n_exp,
    tokens,
    cotangent,
    arrival,
    seq_length,
    w_q,
    w_k,
    w_v,
    w_o,
    ln1_gain,
    ln1_bias,
    ln2_gain,
    ln2_bias,
    w_in,
    w_out,
):
    me, grp = lax.axis_index("exp"), lax.axis_index("grp")
    meta = jnp.stack([me, grp]).astype(jnp.int32)
    width = tokens.shape[1]
    step = w_q.shape[0]
    hidden = w_in.shape[2] // n_grp
    both = ("grp", "exp")

    def swap(a, k):
        return lax.ppermute(a, "exp", [(i, i ^ k) for i in range(n_exp)])

    def shift(a, k):
        return lax.ppermute(a, "grp", [(i, (i + k) % n_grp) for i in range(n_grp)])

    def exchange(rows):
        return lax.all_to_all(rows, "exp", split_axis=0, concat_axis=0, tiled=True)

    bits = []
    while 2 ** len(bits) < n_exp:
        bits.append(2 ** len(bits))
    orders = [bits[:0:-1] + bits[:1], bits[1:] + bits[:1]]

    def gather_pair(own, cut):
        first = lambda a: a[0] if isinstance(a, tuple) else a[:, :cut]
        second = lambda a: a[1] if isinstance(a, tuple) else a[:, cut:]
        have = {0: own}
        for r in sorted(range(1, n_exp), key=lambda r: (bin(r).count("1"), -r)):
            b, c = (max((b for b in bits if r & b), key=order.index) for order in orders)
            if b == c and not isinstance(have[r ^ b], tuple):
                have[r] = swap(have[r ^ b], b)
            else:
                have[r] = (swap(first(have[r ^ b]), b), swap(second(have[r ^ c]), c))
        return [have[r] for r in range(n_exp)]

    def line_step(t, up, down):
        up = lax.ppermute(up, "grp", [(i, i + 1) for i in range(t - 1, n_grp - 1)])
        down = lax.ppermute(down, "grp", [(i + 1, i) for i in range(n_grp - t)])
        return up, down

    def line(a):
        steps = [(a, a)]
        for t in range(1, n_grp):
            steps.append(line_step(t, *steps[-1]))
        return steps

    ids_row = arrival
    ids_col = arrival.reshape(-1, 1)
    flag = seq_length

    gains = jnp.stack([ln1_gain, ln1_bias, ln2_gain, ln2_bias])
    mine = jnp.zeros((16, width), BF)
    mine = lax.dynamic_update_slice(mine, gains, (0, (grp * n_exp + me) * step))
    mine = jnp.concatenate([w_q, w_k, mine, w_v, w_o])
    mine = [mine] + [shift(mine, k) for k in range(1, n_grp)]
    arrived = exchange(tokens)
    w_first, w_second = w_in[0], w_out[0]
    wi_turned, wo_turned = turn_slices(meta, w_first, w_second, hidden)
    dact = act_grad(cotangent, w_second)
    pair_qk, pair_vo = stack(mine, (2 * step + 16, 2 * step), deps=(arrived, dact, wi_turned))
    pieces = gather_pair(pair_qk, step)
    all_vo = lax.all_gather(pair_vo, "exp", axis=0)

    full = (n_grp, n_exp, step, width)
    is_cut = lambda a: isinstance(a, tuple)
    pieces_q = [(a[0], 0) if is_cut(a) else (a, 0) for a in pieces]
    pieces_k = [(a[1], 0) if is_cut(a) else (a, 1) for a in pieces]
    pieces_g = [
        (a[1], step // 16) if is_cut(a) else (a, 2 * step // 16) for a in pieces
    ]
    pieces_v, pieces_o = [(all_vo, 0)], [(all_vo, 1)]

    cot_line, x_line = [(cotangent,) * 2], []

    def forward(steps, gated=None):
        if len(steps) < n_grp:
            steps.append(line_step(len(steps), *(gated or steps[-1])))
        return steps[-1]

    forward(cot_line)
    seq, ln_one, ln_turned, gains = seq_norm(ids_col, arrived, pieces_g)
    q, mat_q = project(meta, ln_one, pieces_q, full)
    k, mat_k = project(meta, ln_one, pieces_k, full)
    v, mat_v, cot_line[1] = project(meta, ln_one, pieces_v, full, deps=(q, k), gates=cot_line[1])
    forward(cot_line)
    attn, lse = attend(flag, q, k, v)
    mat_o, leaving = mix(meta, attn, seq, ids_row, pieces_o, full)
    x = exchange(leaving)

    act, dx, sums_two = expert(
        x, cotangent, gains[2], gains[3], w_first, dact, deps=cot_line[-1]
    )
    forward(cot_line)
    x_line = [(x,) * 2]
    forward(x_line)
    output = expert_out(x, act, w_second)

    def slices(t, sums, deps=()):
        flags = [(grp >= t).astype(jnp.int32), (grp + t < n_grp).astype(jnp.int32)]
        xs, cots = list(x_line[t]), list(cot_line[t])
        if t == 0:
            xs, cots, flags = xs[:1], cots[:1], flags[:1]
        return slice_grads(
            jnp.stack(flags),
            xs,
            cots,
            gains[2],
            gains[3],
            wi_turned,
            wo_turned,
            sums,
            t == n_grp - 1,
            deps,
        )

    slice_sums = slices(0, None, deps=output)
    back = exchange(dx)
    (dmix, dattn), x_line[1] = back_in(
        ids_col, mat_o, back, deps=slice_sums, gates=x_line[1]
    )
    forward(x_line)

    pairs = width // (2 * HDIM)
    early = attend_back(flag, q, k, v, attn, dattn, lse, 0, pairs // 2)
    send, keep = shared_grads(
        meta,
        [(attn, False), (ln_turned, True)],
        [(0, dmix)] + [(1, g) for g in early],
        [],
        n_exp,
        n_grp,
    )
    gates = x_line[2] if n_grp > 2 else dmix
    rest, gates = attend_back(
        flag, q, k, v, attn, dattn, lse, pairs // 2, pairs // 2, deps=send, gates=gates
    )
    if n_grp > 2:
        x_line[2] = gates
    for _ in range(3, n_grp):
        forward(cot_line)
        forward(x_line)
    first = halve(keep, swap(send, 1), deps=rest)
    dqs, dks, dvs = zip(early, rest)
    dfirst, sums_one = first_back(
        dqs, dks, dvs, (mat_q, mat_k, mat_v), seq, dmix, gains[0], ids_row, deps=first
    )
    (send, keep), dfirst = shared_grads(
        meta,
        [(ln_turned, True)],
        [(0, g) for g in rest],
        [sums_one, sums_two],
        n_exp,
        n_grp,
        gates=dfirst,
    )
    grad_x = exchange(dfirst[0])
    slice_sums = slices(1, slice_sums, send)
    second = halve(keep, swap(send, 1), deps=slice_sums)

    def over_chips(parts):
        others = [swap(parts[r], 2 * r) for r in range(1, n_exp // 2)]
        return total_of(parts[0], others)

    first = over_chips(first)
    for t in range(2, n_grp):
        deps = (first, second, x_line[-1]) if t == 2 else ()
        if t == n_grp - 1:
            second = over_chips(second)
            deps = second
        slice_sums = slices(t, slice_sums, deps)
    grad_w_in, grad_w_out = slice_sums

    parts = []
    for n in range(1, n_grp):
        at = (grp + n) % n_grp
        parts.append(
            [shift(lax.dynamic_index_in_dim(a[1], at, 0, False), n) for a in (first, second)]
        )
    *shared, small = final(meta, (first[0], second[0]), parts)
    small = [small[:, n] for n in (0, 1, 8, 9)]
    grad_w_o, *grads = shared

    return (
        output,
        grad_x,
        *grads,
        grad_w_o,
        *small,
        grad_w_in[None],
        grad_w_out[None],
    )


def solution(mesh):
    both = ("grp", "exp")
    rows, flat, mats = P(both, None), P(both), P("exp", None, None)
    split = P("exp", None, "grp")
    return jax.shard_map(
        partial(local, mesh.shape["grp"], mesh.shape["exp"]),
        mesh=mesh,
        in_specs=(rows, rows, rows, flat) + (rows,) * 4 + (flat,) * 4 + (mats, mats),
        out_specs=(rows,) * 6 + (flat,) * 4 + (split, split),
        check_vma=False,
    )
```

```python
from functools import partial

import jax
import jax.numpy as jnp
from jax import lax
from jax.experimental import pallas as pl
from jax.experimental.pallas import tpu as pltpu
from jax.sharding import PartitionSpec as P

HDIM = 64
QB = 256
EPSILON = 1e-05
NEG_FILL = -1e30
GELU_A = 0.7978845608028654
GELU_B = 0.044715
BF = jnp.bfloat16
F32 = jnp.float32
MIB = 1024 * 1024


def dot_nn(left, right):
    return lax.dot_general(left, right, (((1,), (0,)), ((), ())), preferred_element_type=F32)


def dot_nt(left, right):
    return lax.dot_general(left, right, (((1,), (1,)), ((), ())), preferred_element_type=F32)


def norm_rows(x):
    centred = x - jnp.mean(x, -1, keepdims=True)
    inverse = lax.rsqrt(jnp.mean(centred * centred, -1, keepdims=True) + EPSILON)
    return centred * inverse, inverse


def norm_back(grad, normed, inverse, gain):
    scaled = grad * gain
    return inverse * (
        scaled
        - jnp.mean(scaled, -1, keepdims=True)
        - normed * jnp.mean(scaled * normed, -1, keepdims=True)
    )


def gelu_both(u):
    sq = u * u
    half = 0.5 + 0.5 * jnp.tanh(u * (GELU_A + (GELU_A * GELU_B) * sq))
    act = u * half
    return act, half + act * (1.0 - half) * (2.0 * GELU_A + (6.0 * GELU_A * GELU_B) * sq)


def run(
    kernel,
    args,
    out_shape,
    deps=(),
    scalars=(),
    grid=(1,),
    specs=None,
    outs=None,
    scratch=(),
    micros=5,
    gates=(),
):
    specs = [whole(a.shape) for a in args] if specs is None else specs
    outs = [whole(o.shape) for o in out_shape] if outs is None else outs
    gates, deps = jax.tree.leaves(gates), jax.tree.leaves(deps)
    first, count, results = len(scalars) + len(args), len(deps) + len(gates), len(out_shape)

    def body(*refs):
        last = first + count + results
        kernel(*refs[:first], *refs[first + count : last], *refs[last + len(gates) :])

    anywhere = pl.BlockSpec(memory_space=pl.ANY)
    res = pl.pallas_call(
        body,
        grid_spec=pltpu.PrefetchScalarGridSpec(
            num_scalar_prefetch=len(scalars),
            grid=grid,
            in_specs=list(specs) + [anywhere] * count,
            out_specs=list(outs) + [anywhere] * len(gates),
            scratch_shapes=list(scratch),
        ),
        out_shape=list(out_shape) + [shaped(g.shape, g.dtype) for g in gates],
        input_output_aliases={first + len(deps) + n: results + n for n in range(len(gates))},
        compiler_params=pltpu.CompilerParams(vmem_limit_bytes=60 * MIB),
        cost_estimate=pl.CostEstimate(
            flops=int(micros * 0.517e9), bytes_accessed=10**6, transcendentals=0
        ),
    )(*scalars, *args, *deps, *gates)
    return (list(res[:results]), list(res[results:])) if gates else res


def shaped(shape, dtype=BF):
    return jax.ShapeDtypeStruct(tuple(shape), dtype)


def whole(shape):
    return pl.BlockSpec(shape, lambda *_: (0,) * len(shape), pipeline_mode=pl.Buffered(1))


def one_hot(ids, other):
    return jnp.where(ids == other, 1.0, 0.0).astype(BF)


def enter_kernel(count, meta, ids_ref, rows_ref, *refs):
    pieces, refs = [refs[n * count : (n + 1) * count] for n in range(3)], refs[3 * count :]
    seq_ref, ln_ref, lnt_ref, q_ref, k_ref, mat_q, mat_k, *gain_refs = refs
    width = rows_ref.shape[1]

    @pl.when(pl.program_id(0) == 0)
    def _():
        place(meta, pieces[0], mat_q)
        place(meta, pieces[1], mat_k)
        gains = 0.0
        for piece in pieces[2]:
            for z in range(piece.shape[0]):
                gains = gains + piece[z].astype(F32)
        for n, ref in enumerate(gain_refs):
            ref[...] = gains[n : n + 1]

    lanes = lax.broadcasted_iota(jnp.int32, (QB, rows_ref.shape[0]), 1)
    x = dot_nn(one_hot(ids_ref[...], lanes), rows_ref[...])
    seq_ref[...] = x.astype(BF)
    normed, _ = norm_rows(x)
    ln = (normed * gain_refs[0][...] + gain_refs[1][...]).astype(BF)
    ln_ref[...] = ln
    lnt_ref[...] = jnp.transpose(ln)
    q_ref[...] = dot_nn(ln, mat_q[...].reshape(width, width)).astype(BF)
    k_ref[...] = dot_nn(ln, mat_k[...].reshape(width, width)).astype(BF)


def enter(meta, ids_col, rows, pieces_q, pieces_k, pieces_g, full, deps=()):
    total, width = rows.shape
    block = pl.BlockSpec((QB, width), lambda r, *_: (r, 0))
    turned = pl.BlockSpec((width, QB), lambda r, *_: (0, r))
    rows_out, gain = shaped((total, width)), shaped((1, width), F32)
    seq, ln, lnt, q, k, mat_q, mat_k, *gains = run(
        partial(enter_kernel, len(pieces_q)),
        (ids_col, rows, *[a for a, _ in (*pieces_q, *pieces_k, *pieces_g)]),
        [rows_out, rows_out, shaped((width, total)), rows_out, rows_out]
        + [shaped(full)] * 2
        + [gain] * 4,
        deps,
        (meta,),
        (total // QB,),
        [pl.BlockSpec((QB, 1), lambda r, *_: (r, 0)), whole(rows.shape)]
        + piece_specs(pieces_q, full[2])
        + piece_specs(pieces_k, full[2])
        + piece_specs(pieces_g, 16),
        [block, block, turned, block, block] + [whole(full)] * 2 + [whole((1, width))] * 4,
        micros=14,
    )
    flat = (width, width)
    return seq, ln, lnt, q, k, mat_q.reshape(flat), mat_k.reshape(flat), gains


def place(meta, refs, full):
    groups, experts = full.shape[0], full.shape[1]
    for r in range(experts):
        for z in range(groups):
            row = lax.rem(meta[1] + (groups - z), groups)
            if len(refs) == 1:
                full[row, r] = refs[0][r, z]
            else:
                full[row, r ^ meta[0]] = refs[r][z]


def piece_specs(pieces, step):
    specs = []
    for array, n in pieces:
        shape = (*array.shape[:-2], step, array.shape[-1])
        at = (0,) * (len(shape) - 2) + (n, 0)
        specs.append(pl.BlockSpec(shape, lambda *_, at=at: at, pipeline_mode=pl.Buffered(1)))
    return specs


def stack_kernel(groups, *refs):
    ins, outs = refs[:groups], refs[groups:]
    for z in range(groups):
        row = 0
        for out in outs:
            out[z] = ins[z][row : row + out.shape[1]]
            row += out.shape[1]


def stack(blocks, rows, deps=()):
    width = blocks[0].shape[1]
    return run(
        partial(stack_kernel, len(blocks)),
        blocks,
        [shaped((len(blocks), r, width)) for r in rows],
        deps,
        micros=2,
    )


def proj_kernel(count, meta, ln_ref, *refs):
    pieces, (out_ref, full_ref) = refs[:count], refs[count:]

    @pl.when(pl.program_id(0) == 0)
    def _():
        place(meta, pieces, full_ref)

    width = ln_ref.shape[1]
    out_ref[...] = dot_nn(ln_ref[...], full_ref[...].reshape(width, width)).astype(BF)


def project(meta, ln, pieces, full, deps=(), gates=()):
    total, width = ln.shape
    block = pl.BlockSpec((QB, width), lambda r, *_: (r, 0))
    (out, mat), gates = run(
        partial(proj_kernel, len(pieces)),
        (ln, *[a for a, _ in pieces]),
        [shaped(ln.shape), shaped(full)],
        deps,
        (meta,),
        (total // QB,),
        [block] + piece_specs(pieces, full[2]),
        [block, whole(full)],
        gates=gates,
    )
    return out, mat.reshape(width, width), gates


def head_lanes(heads):
    pair = 2 * HDIM
    low = lax.broadcasted_iota(jnp.int32, (1, pair), 1) < HDIM
    cols = [slice(h // 2 * pair, (h // 2 + 1) * pair) for h in range(heads)]
    return low, cols, [~low if h % 2 else low for h in range(heads)]


def attend_kernel(flag, q_ref, k_ref, v_ref, o_ref, lse_ref, lse_cols):
    total, heads = q_ref.shape[0], q_ref.shape[1] // HDIM
    low, cols, own = head_lanes(heads)
    each = range(heads)
    causal = lax.broadcasted_iota(jnp.int32, (QB, QB), 1) <= lax.broadcasted_iota(
        jnp.int32, (QB, QB), 0
    )

    def go(long):
        for a in range(0, total, QB):
            b = a + QB
            further = long and a > 0
            q = [
                jnp.where(own[h], q_ref[a:b, cols[h]], jnp.zeros((QB, 2 * HDIM), BF))
                * BF(HDIM**-0.5)
                for h in each
            ]
            near = [jnp.where(causal, dot_nt(q[h], k_ref[a:b, cols[h]]), NEG_FILL) for h in each]
            top = [jnp.max(near[h], 1, keepdims=True) for h in each]
            if further:
                far = [dot_nt(q[h], k_ref[0:a, cols[h]]) for h in each]
                top = [jnp.maximum(top[h], jnp.max(far[h], 1, keepdims=True)) for h in each]
            near = [jnp.exp(near[h] - top[h]) for h in each]
            mass = [jnp.sum(near[h], 1, keepdims=True) for h in each]
            o = [dot_nn(near[h].astype(BF), v_ref[a:b, cols[h]]) for h in each]
            if further:
                far = [jnp.exp(far[h] - top[h]) for h in each]
                mass = [mass[h] + jnp.sum(far[h], 1, keepdims=True) for h in each]
                o = [o[h] + dot_nn(far[h].astype(BF), v_ref[0:a, cols[h]]) for h in each]
            o = [o[h] * (1.0 / mass[h]) for h in each]
            logs = [top[h] + jnp.log(mass[h]) for h in each]
            for h in range(0, heads, 2):
                o_ref[a:b, cols[h]] = jnp.where(low, o[h], o[h + 1]).astype(BF)
                lse_cols[a:b, cols[h]] = jnp.where(low, logs[h], logs[h + 1])

    @pl.when(flag[0] > QB)
    def _():
        go(True)

    @pl.when(flag[0] <= QB)
    def _():
        go(False)

    for h in range(0, heads, 2):
        turned = jnp.transpose(lse_cols[:, cols[h]])
        lse_ref[h // 2, 0:1] = turned[0:1]
        lse_ref[h // 2, 1:2] = turned[HDIM : HDIM + 1]


def attend(flag, q, k, v, deps=()):
    total, width = q.shape
    lanes = 4 * HDIM
    block = pl.BlockSpec((total, lanes), lambda j, *_: (0, j))
    stat = pl.BlockSpec((2, 8, total), lambda j, *_: (j, 0, 0))
    return run(
        attend_kernel,
        (q, k, v),
        [shaped((total, width)), shaped((width // (2 * HDIM), 8, total), F32)],
        deps,
        (flag,),
        (width // lanes,),
        [block] * 3,
        [block, stat],
        [pltpu.VMEM((total, lanes), F32)],
        micros=22,
    )


def attend_back_kernel(
    flag, q_ref, k_ref, v_ref, o_ref, g_ref, lse_ref, dq_ref, dk_ref, dv_ref, dq_turned
):
    total, heads = q_ref.shape[0], q_ref.shape[1] // HDIM
    low, cols, own = head_lanes(heads)
    each = range(heads)
    causal = lax.broadcasted_iota(jnp.int32, (QB, QB), 0) <= lax.broadcasted_iota(
        jnp.int32, (QB, QB), 1
    )
    delta, k_turned = [], []
    for h in range(0, heads, 2):
        prod = jnp.transpose(g_ref[:, cols[h]].astype(F32) * o_ref[:, cols[h]].astype(F32))
        delta.append(jnp.sum(prod[:HDIM], 0, keepdims=True))
        delta.append(jnp.sum(prod[HDIM:], 0, keepdims=True))
        turned = jnp.transpose(k_ref[:, cols[h]])
        k_turned += [turned[:HDIM], turned[HDIM:]]

    def go(long):
        for a in range(0, total, QB):
            b = a + QB
            zero = jnp.zeros((QB, 2 * HDIM), BF)
            k = [jnp.where(own[h], k_ref[a:b, cols[h]], zero) * BF(HDIM**-0.5) for h in each]
            v = [jnp.where(own[h], v_ref[a:b, cols[h]], zero) for h in each]
            dk, dv = [0.0] * heads, [0.0] * heads
            spans = [(a, b)]
            if long and b < total:
                spans.append((b, total))
            for lo, hi in spans:
                scores = [dot_nt(k[h], q_ref[lo:hi, cols[h]]) for h in each]
                dp = [dot_nt(v[h], g_ref[lo:hi, cols[h]]) for h in each]
                probs = [
                    jnp.exp(scores[h] - lse_ref[h // 2, h % 2 : h % 2 + 1, lo:hi]) for h in each
                ]
                if lo == a:
                    probs = [jnp.where(causal, p, 0.0) for p in probs]
                ds = [(probs[h] * (dp[h] - delta[h][:, lo:hi])).astype(BF) for h in each]
                probs = [p.astype(BF) for p in probs]
                for h in each:
                    dv[h] = dv[h] + dot_nn(probs[h], g_ref[lo:hi, cols[h]])
                    dk[h] = dk[h] + dot_nn(ds[h], q_ref[lo:hi, cols[h]])
                    rows = slice(h * HDIM, (h + 1) * HDIM)
                    if a == 0 or not long:
                        dq_turned[rows, lo:hi] = dot_nn(k_turned[h][:, a:b], ds[h])
                    else:
                        dq_turned[rows, lo:hi] += dot_nn(k_turned[h][:, a:b], ds[h])
            for h in range(0, heads, 2):
                both = jnp.where(low, dk[h], dk[h + 1])
                dk_ref[a:b, cols[h]] = (both * HDIM**-0.5).astype(BF)
                dv_ref[a:b, cols[h]] = jnp.where(low, dv[h], dv[h + 1]).astype(BF)

    @pl.when(flag[0] > QB)
    def _():
        go(True)

    @pl.when(flag[0] <= QB)
    def _():
        go(False)

    dq_ref[...] = (jnp.transpose(dq_turned[...]) * HDIM**-0.5).astype(BF)


def attend_back(flag, q, k, v, o, g, lse, part, parts, deps=(), gates=()):
    total, width = q.shape
    lanes = 4 * HDIM
    count = width // lanes // parts
    first = part * count
    block = pl.BlockSpec((total, lanes), lambda j, *_: (0, j + first))
    stat = pl.BlockSpec((2, 8, total), lambda j, *_: (j + first, 0, 0))
    done = pl.BlockSpec((total, lanes), lambda j, *_: (0, j))
    return run(
        attend_back_kernel,
        (q, k, v, o, g, lse),
        [shaped((total, width // parts))] * 3,
        deps,
        (flag,),
        (count,),
        [block] * 5 + [stat],
        [done] * 3,
        [pltpu.VMEM((lanes, total), F32)],
        micros=18,
        gates=gates,
    )


def mix_kernel(count, meta, attn_ref, seq_ref, ids_ref, *refs):
    pieces, (full_ref, out_ref, mixed) = refs[:count], refs[count:]
    r = pl.program_id(0)

    @pl.when(r == 0)
    def _():
        place(meta, pieces, full_ref)

    size, width = attn_ref.shape
    x = seq_ref[...].astype(F32) + dot_nn(attn_ref[...], full_ref[...].reshape(width, width))
    mixed[pl.ds(pl.multiple_of(r * size, size), size)] = x.astype(BF)

    @pl.when(r == pl.num_programs(0) - 1)
    def _():
        to_experts(ids_ref, mixed, out_ref)


def to_experts(ids_ref, rows, out_ref):
    total = rows.shape[0]
    for r in range(0, total, QB):
        want = lax.broadcasted_iota(jnp.int32, (QB, total), 0) + r
        out_ref[r : r + QB] = dot_nn(one_hot(want, ids_ref[...]), rows[...]).astype(BF)


def mix(meta, attn, seq, ids_row, pieces, full, deps=()):
    total, width = attn.shape
    block = pl.BlockSpec((QB, width), lambda r, *_: (r, 0))
    mat, out = run(
        partial(mix_kernel, len(pieces)),
        (attn, seq, ids_row, *[a for a, _ in pieces]),
        [shaped(full), shaped(attn.shape)],
        deps,
        (meta,),
        (total // QB,),
        [block, block, whole(ids_row.shape)] + piece_specs(pieces, full[2]),
        [whole(full), whole(attn.shape)],
        [pltpu.VMEM(attn.shape, BF)],
        micros=8,
    )
    return mat.reshape(width, width), out


def act_grad_kernel(cot_ref, wo_ref, out_ref):
    out_ref[...] = dot_nn(cot_ref[...], wo_ref[...]).astype(BF)


def act_grad(cot, w_out, deps=()):
    total, width = cot.shape
    hidden, tile = w_out.shape[1], 512
    return run(
        act_grad_kernel,
        (cot, w_out),
        [shaped((total, hidden))],
        deps,
        (),
        (hidden // tile,),
        [whole(cot.shape), pl.BlockSpec((width, tile), lambda f: (0, f))],
        [pl.BlockSpec((total, tile), lambda f: (0, f))],
        micros=11,
    )[0]


def expert_kernel(
    steps, x_ref, cot_ref, gain_ref, bias_ref, wi_ref, dact_ref, act_ref, dx_ref, sums_ref, ln, acc
):
    f = pl.program_id(0)
    total, width = ln.shape

    @pl.when(f == 0)
    def _():
        for r in range(0, total, QB):
            normed, _ = norm_rows(x_ref[r : r + QB].astype(F32))
            ln[r : r + QB] = (normed * gain_ref[...] + bias_ref[...]).astype(BF)

    def body(first):
        spans = [slice(r, r + QB) for r in range(0, total, QB)]
        pre = dot_nn(ln[spans[0]], wi_ref[...])
        for n, rows in enumerate(spans):
            act, slope = gelu_both(pre)
            if n + 1 < len(spans):
                pre = dot_nn(ln[spans[n + 1]], wi_ref[...])
            act_ref[rows] = act.astype(BF)
            back = (dact_ref[rows].astype(F32) * slope).astype(BF)
            if first:
                acc[rows] = dot_nt(back, wi_ref[...])
            else:
                acc[rows] += dot_nt(back, wi_ref[...])

    @pl.when(f == 0)
    def _():
        body(True)

    @pl.when(f > 0)
    def _():
        body(False)

    @pl.when(f == steps - 1)
    def _():
        gain_sum = jnp.zeros((1, width), F32)
        bias_sum = gain_sum
        for r in range(0, total, QB):
            rows = slice(r, r + QB)
            normed, inverse = norm_rows(x_ref[rows].astype(F32))
            d = acc[rows]
            gain_sum = gain_sum + jnp.sum(d * normed, 0, keepdims=True)
            bias_sum = bias_sum + jnp.sum(d, 0, keepdims=True)
            back = norm_back(d, normed, inverse, gain_ref[...])
            dx_ref[rows] = (cot_ref[rows].astype(F32) + back).astype(BF)
        sums_ref[0:1] = gain_sum
        sums_ref[1:2] = bias_sum


def expert(x, cot, gain, bias, w_in, dact, deps=()):
    total, width = x.shape
    hidden, tile = w_in.shape[1], 1024
    steps = hidden // tile
    cols = pl.BlockSpec((width, tile), lambda f: (0, f))
    rows = pl.BlockSpec((total, tile), lambda f: (0, f))
    return run(
        partial(expert_kernel, steps),
        (x, cot, gain, bias, w_in, dact),
        [shaped((total, hidden)), shaped(x.shape), shaped((8, width), F32)],
        deps,
        (),
        (steps,),
        [whole(x.shape)] * 2 + [whole((1, width))] * 2 + [cols, rows],
        [rows, whole(x.shape), whole((8, width))],
        [pltpu.VMEM(x.shape, BF), pltpu.VMEM(x.shape, F32)],
        micros=34,
    )


def expert_out_kernel(x_ref, act_ref, wo_ref, out_ref):
    out = x_ref[...].astype(F32) + dot_nt(act_ref[...], wo_ref[...])
    out_ref[...] = out.astype(BF)


def expert_out(x, act, w_out, deps=()):
    total, width = x.shape
    hidden, tile = w_out.shape[1], 256
    part = pl.BlockSpec((total, tile), lambda n: (0, n))
    return run(
        expert_out_kernel,
        (x, act, w_out),
        [shaped(x.shape)],
        deps,
        (),
        (width // tile,),
        [part, whole(act.shape), pl.BlockSpec((tile, hidden), lambda n: (n, 0))],
        [part],
        micros=12,
    )[0]


def turn_kernel(meta, wi_ref, wo_ref, wit_ref, wot_ref):
    wit_ref[...] = jnp.transpose(wi_ref[...])
    wot_ref[...] = jnp.transpose(wo_ref[...])


def turn_slices(meta, w_in, w_out, hidden):
    width, tile = w_in.shape[0], min(256, hidden)
    tiles = hidden // tile
    cols = pl.BlockSpec((width, tile), lambda f, m: (0, m[1] * tiles + f))
    rows = pl.BlockSpec((tile, width), lambda f, m: (f, 0))
    return run(
        turn_kernel,
        (w_in, w_out),
        [shaped((hidden, width))] * 2,
        (),
        (meta,),
        (tiles,),
        [cols] * 2,
        [rows] * 2,
        micros=5,
    )


def slice_kernel(t, groups, first, last, meta, *refs):
    valid = [meta[1] >= t, meta[1] + t < groups] if t else [meta[1] >= 0]
    count = len(valid)
    xs, cots = refs[:count], refs[count : 2 * count]
    gain_ref, bias_ref, wi_ref, wo_ref = refs[2 * count : 2 * count + 4]
    rest = refs[2 * count + 4 :]
    if not first:
        in_prev, out_prev = rest[:2]
        rest = rest[2:]
    in_ref, out_ref, in_acc, out_acc, lns, rows, sems = rest
    f = pl.program_id(0)
    total = lns.shape[1]

    def copies(n):
        return (
            pltpu.make_async_copy(xs[n], lns.at[n], sems.at[n, 0]),
            pltpu.make_async_copy(cots[n], rows.at[n], sems.at[n, 1]),
        )

    for n in range(count):

        @pl.when((f == 0) & valid[n])
        def _(n=n):
            for copy in copies(n):
                copy.start()

    if first:
        in_acc[...] = jnp.zeros_like(in_acc)
        out_acc[...] = jnp.zeros_like(out_acc)
    else:
        in_acc[...] = in_prev[...]
        out_acc[...] = out_prev[...]
    for n in range(count):

        @pl.when(valid[n])
        def _(n=n):
            @pl.when(f == 0)
            def _():
                for copy in copies(n):
                    copy.wait()
                for r in range(0, total, QB):
                    normed, _ = norm_rows(lns[n, r : r + QB].astype(F32))
                    lns[n, r : r + QB] = (normed * gain_ref[...] + bias_ref[...]).astype(BF)

            pre = dot_nt(wi_ref[...], lns[n])
            grad = dot_nt(wo_ref[...], rows[n])
            act, slope = gelu_both(pre)
            back = (grad * slope).astype(BF)
            in_acc[...] += dot_nn(back, lns[n])
            out_acc[...] += dot_nn(act.astype(BF), rows[n])

    if last:
        in_ref[...] = jnp.transpose(in_acc[...])
        out_ref[...] = jnp.transpose(out_acc[...])
    else:
        in_ref[...] = in_acc[...]
        out_ref[...] = out_acc[...]


def slice_grads(meta, t, groups, xs, cots, gain, bias, wi_turned, wo_turned, prev, deps=(), gates=()):
    count = len(xs)
    total, width = xs[0].shape
    hidden = wi_turned.shape[0]
    tile = min(256, hidden)
    rows = pl.BlockSpec((tile, width), lambda f, *_: (f, 0))
    cols = pl.BlockSpec((width, tile), lambda f, *_: (0, f))
    anywhere = pl.BlockSpec(memory_space=pl.ANY)
    first, last = prev is None, t == groups - 1
    return run(
        partial(slice_kernel, t, groups, first, last),
        (*xs, *cots, gain, bias, wi_turned, wo_turned, *(() if first else prev)),
        [shaped((width, hidden) if last else (hidden, width), F32)] * 2,
        deps,
        (meta,),
        (hidden // tile,),
        [anywhere] * (2 * count)
        + [whole((1, width))] * 2
        + [rows] * (2 if first else 4),
        [cols if last else rows] * 2,
        [pltpu.VMEM((tile, width), F32)] * 2
        + [pltpu.VMEM((count, total, width), BF)] * 2
        + [pltpu.SemaphoreType.DMA((count, 2))],
        micros=18,
        gates=gates,
    )


def back_kernel(ids_ref, mat_ref, rows_ref, dmix_ref, dattn_ref):
    lanes = lax.broadcasted_iota(jnp.int32, (QB, rows_ref.shape[0]), 1)
    x = dot_nn(one_hot(ids_ref[...], lanes), rows_ref[...]).astype(BF)
    dmix_ref[...] = x
    dattn_ref[...] = dot_nt(x, mat_ref[...]).astype(BF)


def back_in(ids_col, mat, rows, deps=()):
    total, width = rows.shape
    block = pl.BlockSpec((QB, width), lambda r: (r, 0))
    return run(
        back_kernel,
        (ids_col, mat, rows),
        [shaped(rows.shape)] * 2,
        deps,
        (),
        (total // QB,),
        [pl.BlockSpec((QB, 1), lambda r: (r, 0)), whole(mat.shape), whole(rows.shape)],
        [block] * 2,
        micros=7,
    )


def shared_kernel(picks, turns, sums_in, meta, *refs):
    lefts, rights = refs[: len(turns)], refs[len(turns) : len(turns) + len(picks)]
    rest = refs[len(turns) + len(picks) :]
    small, (send, keep, sums) = rest[:sums_in], rest[sums_in:]
    half, step = send.shape[0], send.shape[2]
    turned = [jnp.transpose(l[...]) if t else l[...] for l, t in zip(lefts, turns)]

    def put(cols, size):
        for r in range(2 * half):
            row = pl.multiple_of((r ^ meta[0]) * step, step)
            ref = send if r % 2 else keep
            ref[r // 2, 0, :, cols : cols + size] = sums[pl.ds(row, step), :size].astype(BF)

    cols = 0
    for pick, right in zip(picks, rights):
        size = right.shape[1]
        sums[:, :size] = dot_nn(turned[pick], right[...])
        put(cols, size)
        cols += size
    if sums_in:
        sums[:, :128] = jnp.zeros((sums.shape[0], 128), F32)
        for n in range(sums_in):
            sums[:, 8 * n : 8 * n + 8] = jnp.transpose(small[n][...])
        put(cols, 128)


def shared_grads(meta, lefts, terms, small, experts, groups, deps=(), gates=()):
    total = terms[0][1].shape[0]
    array, is_turned = lefts[0]
    features = array.shape[0 if is_turned else 1]
    step, block = features // (experts * groups), features // groups
    width = sum(r.shape[1] for _, r in terms) + (128 if small else 0)
    as_is = pl.BlockSpec((block, total), lambda g, *_: (g, 0))
    to_turn = pl.BlockSpec((total, block), lambda g, *_: (0, g))
    sums = pl.BlockSpec((8, block), lambda g, *_: (0, g))
    shape = (experts // 2, groups, step, width)
    spec = pl.BlockSpec((shape[0], 1, step, width), lambda g, *_: (0, g, 0, 0))
    return run(
        partial(shared_kernel, [p for p, _ in terms], [not t for _, t in lefts], len(small)),
        (*[a for a, _ in lefts], *[r for _, r in terms], *small),
        [shaped(shape)] * 2,
        deps,
        (meta,),
        (groups,),
        [as_is if t else to_turn for _, t in lefts]
        + [whole(r.shape) for _, r in terms]
        + [sums] * len(small),
        [spec] * 2,
        [pltpu.VMEM((block, max(r.shape[1] for _, r in terms)), F32)],
        micros=8,
        gates=gates,
    )


def halve_kernel(keep_ref, got_ref, *outs):
    for r, out in enumerate(outs):
        both = keep_ref[r].astype(F32) + got_ref[r].astype(F32)
        out[...] = both.astype(out.dtype)


def halve(keep, got, deps=()):
    chips, tail = keep.shape[0], keep.shape[1:]
    kinds = [F32] + [BF] * (chips - 1)
    return run(halve_kernel, (keep, got), [shaped(tail, k) for k in kinds], deps, micros=2)


def total_kernel(own_ref, *refs):
    ins, (all_ref, low_ref) = refs[:-2], refs[-2:]
    total = own_ref[...]
    for ref in ins:
        total = total + ref[...].astype(F32)
    all_ref[...] = total
    low_ref[...] = total.astype(BF)


def total_of(own, others):
    return run(
        total_kernel,
        (own, *others),
        [shaped(own.shape, F32), shaped(own.shape)],
        micros=2,
    )


def final_kernel(count, heads, meta, *refs):
    owns, ins = refs[:2], refs[2 : 2 + 2 * count]
    o_ref, q_ref, k_ref, v_ref, small_ref = refs[2 + 2 * count :]
    first = owns[0][meta[1]]
    second = owns[1][meta[1]]
    for n in range(count):
        first = first + ins[2 * n][...].astype(F32)
        second = second + ins[2 * n + 1][...].astype(F32)
    width = o_ref.shape[1]
    o_ref[...] = first[:, :width]
    for n, ref in enumerate((q_ref, k_ref, v_ref)):
        ref[:, :heads] = first[:, width + n * heads : width + (n + 1) * heads]
        ref[:, heads:] = second[:, n * heads : (n + 1) * heads]
    small_ref[...] = second[:, 3 * heads :]


def final(meta, owns, pairs):
    step = owns[0].shape[1]
    heads = (owns[1].shape[2] - 128) // 3
    width = owns[0].shape[2] - 3 * heads
    return run(
        partial(final_kernel, len(pairs), heads),
        (*owns, *[a for p in pairs for a in p]),
        [shaped((step, width), F32)] * 4 + [shaped((step, 128), F32)],
        (),
        (meta,),
        micros=2,
    )


def first_kernel(steps, count, *refs):
    grads, mats = refs[: 3 * count], refs[3 * count : 3 * count + 3]
    seq_ref, dmix_ref, gain_ref, ids_ref, out_ref, sums_ref, rows = refs[3 * count + 3 :]
    r = pl.program_id(0)
    size, part = grads[0].shape
    grad = None
    for n in range(3):
        for j in range(count):
            term = dot_nt(grads[n * count + j][...], mats[n][:, j * part : (j + 1) * part])
            grad = term if grad is None else grad + term
    normed, inverse = norm_rows(seq_ref[...].astype(F32))
    gain_sum = jnp.sum(grad * normed, 0, keepdims=True)
    bias_sum = jnp.sum(grad, 0, keepdims=True)

    @pl.when(r == 0)
    def _():
        sums_ref[0:1] = gain_sum
        sums_ref[1:2] = bias_sum

    @pl.when(r > 0)
    def _():
        sums_ref[0:1] += gain_sum
        sums_ref[1:2] += bias_sum

    back = dmix_ref[...].astype(F32) + norm_back(grad, normed, inverse, gain_ref[...])
    rows[pl.ds(pl.multiple_of(r * size, size), size)] = back.astype(BF)

    @pl.when(r == steps - 1)
    def _():
        to_experts(ids_ref, rows, out_ref)


def first_back(dqs, dks, dvs, mats, seq, dmix, gain, ids_row, deps=(), gates=()):
    total, width = seq.shape
    steps, count = total // QB, len(dqs)
    block = pl.BlockSpec((QB, width), lambda r: (r, 0))
    part = pl.BlockSpec((QB, width // count), lambda r: (r, 0))
    return run(
        partial(first_kernel, steps, count),
        (*dqs, *dks, *dvs, *mats, seq, dmix, gain, ids_row),
        [shaped((total, width)), shaped((8, width), F32)],
        deps,
        (),
        (steps,),
        [part] * (3 * count)
        + [whole((width, width))] * 3
        + [block] * 2
        + [whole((1, width)), whole((1, total))],
        scratch=[pltpu.VMEM((total, width), BF)],
        micros=12,
        gates=gates,
    )


def local(
    n_grp,
    n_exp,
    tokens,
    cotangent,
    arrival,
    seq_length,
    w_q,
    w_k,
    w_v,
    w_o,
    ln1_gain,
    ln1_bias,
    ln2_gain,
    ln2_bias,
    w_in,
    w_out,
):
    me, grp = lax.axis_index("exp"), lax.axis_index("grp")
    meta = jnp.stack([me, grp]).astype(jnp.int32)
    width = tokens.shape[1]
    step = w_q.shape[0]
    hidden = w_in.shape[2] // n_grp
    both = ("grp", "exp")

    def swap(a, k):
        return lax.ppermute(a, "exp", [(i, i ^ k) for i in range(n_exp)])

    def shift(a, k):
        return lax.ppermute(a, "grp", [(i, (i + k) % n_grp) for i in range(n_grp)])

    def exchange(rows):
        return lax.all_to_all(rows, "exp", split_axis=0, concat_axis=0, tiled=True)

    bits = []
    while 2 ** len(bits) < n_exp:
        bits.append(2 ** len(bits))
    orders = [bits[:0:-1] + bits[:1], bits[1:] + bits[:1]]

    def gather_pair(own, cut):
        first = lambda a: a[0] if isinstance(a, tuple) else a[:, :cut]
        second = lambda a: a[1] if isinstance(a, tuple) else a[:, cut:]
        have = {0: own}
        for r in sorted(range(1, n_exp), key=lambda r: (bin(r).count("1"), -r)):
            b, c = (max((b for b in bits if r & b), key=order.index) for order in orders)
            if b == c and not isinstance(have[r ^ b], tuple):
                have[r] = swap(have[r ^ b], b)
            else:
                have[r] = (swap(first(have[r ^ b]), b), swap(second(have[r ^ c]), c))
        return [have[r] for r in range(n_exp)]

    def line_step(t, up, down):
        up = lax.ppermute(up, "grp", [(i, i + 1) for i in range(t - 1, n_grp - 1)])
        down = lax.ppermute(down, "grp", [(i + 1, i) for i in range(n_grp - t)])
        return up, down

    def line(a):
        steps = [(a, a)]
        for t in range(1, n_grp):
            steps.append(line_step(t, *steps[-1]))
        return steps

    ids_row = arrival
    ids_col = arrival.reshape(-1, 1)
    flag = seq_length

    gains = jnp.stack([ln1_gain, ln1_bias, ln2_gain, ln2_bias])
    mine = jnp.zeros((16, width), BF)
    mine = lax.dynamic_update_slice(mine, gains, (0, (grp * n_exp + me) * step))
    mine = jnp.concatenate([w_q, w_k, mine, w_v, w_o])
    mine = [mine] + [shift(mine, k) for k in range(1, n_grp)]
    arrived = exchange(tokens)
    w_first, w_second = w_in[0], w_out[0]
    wi_turned, wo_turned = turn_slices(meta, w_first, w_second, hidden)
    dact = act_grad(cotangent, w_second)
    pair_qk, pair_vo = stack(mine, (2 * step + 16, 2 * step), deps=(arrived, dact, wi_turned))
    pieces = gather_pair(pair_qk, step)
    all_vo = lax.all_gather(pair_vo, "exp", axis=0)

    full = (n_grp, n_exp, step, width)
    is_cut = lambda a: isinstance(a, tuple)
    pieces_q = [(a[0], 0) if is_cut(a) else (a, 0) for a in pieces]
    pieces_k = [(a[1], 0) if is_cut(a) else (a, 1) for a in pieces]
    pieces_g = [
        (a[1], step // 16) if is_cut(a) else (a, 2 * step // 16) for a in pieces
    ]
    pieces_v, pieces_o = [(all_vo, 0)], [(all_vo, 1)]

    cot_line, x_line = [(cotangent,) * 2], []

    def forward(steps, gated=None):
        if len(steps) < n_grp:
            steps.append(line_step(len(steps), *(gated or steps[-1])))
        return steps[-1]

    forward(cot_line)
    seq, ln_one, ln_turned, q, k, mat_q, mat_k, gains = enter(
        meta, ids_col, arrived, pieces_q, pieces_k, pieces_g, full
    )
    v, mat_v, cot_line[1] = project(meta, ln_one, pieces_v, full, gates=cot_line[1])
    forward(cot_line)
    attn, lse = attend(flag, q, k, v)
    mat_o, leaving = mix(meta, attn, seq, ids_row, pieces_o, full)
    x = exchange(leaving)

    act, dx, sums_two = expert(
        x, cotangent, gains[2], gains[3], w_first, dact, deps=cot_line[-1]
    )
    forward(cot_line)
    x_line = [(x,) * 2]
    forward(x_line)
    output = expert_out(x, act, w_second)

    def slices(t, sums, deps=(), gates=()):
        xs, cots = (list(line[t])[: 2 if t else 1] for line in (x_line, cot_line))
        last = (gains[2], gains[3], wi_turned, wo_turned, sums, deps, gates)
        return slice_grads(meta, t, n_grp, xs, cots, *last)

    slice_sums, x_line[1] = slices(0, None, deps=output, gates=x_line[1])
    back = exchange(dx)
    dmix, dattn = back_in(ids_col, mat_o, back, deps=slice_sums)
    forward(x_line)

    early = attend_back(flag, q, k, v, attn, dattn, lse, 0, 2)
    send, keep = shared_grads(
        meta,
        [(attn, False), (ln_turned, True)],
        [(0, dmix)] + [(1, g) for g in early],
        [],
        n_exp,
        n_grp,
    )
    gates = x_line[2] if n_grp > 2 else dmix
    rest, gates = attend_back(
        flag, q, k, v, attn, dattn, lse, 1, 2, deps=send, gates=gates
    )
    if n_grp > 2:
        x_line[2] = gates
    for _ in range(3, n_grp):
        forward(cot_line)
        forward(x_line)
    first = halve(keep, swap(send, 1), deps=rest)
    dqs, dks, dvs = zip(early, rest)
    dfirst, sums_one = first_back(
        dqs, dks, dvs, (mat_q, mat_k, mat_v), seq, dmix, gains[0], ids_row, deps=first
    )
    (send, keep), dfirst = shared_grads(
        meta,
        [(ln_turned, True)],
        [(0, g) for g in rest],
        [sums_one, sums_two],
        n_exp,
        n_grp,
        gates=dfirst,
    )
    grad_x = exchange(dfirst[0])
    slice_sums = slices(1, slice_sums, send)
    second = halve(keep, swap(send, 1), deps=slice_sums)

    def over_chips(parts):
        others = [swap(parts[r], 2 * r) for r in range(1, n_exp // 2)]
        return total_of(parts[0], others)

    first = over_chips(first)
    for t in range(2, n_grp):
        deps = (first, second, x_line[-1]) if t == 2 else ()
        if t == n_grp - 1:
            second = over_chips(second)
            deps = second
        slice_sums = slices(t, slice_sums, deps)
    grad_w_in, grad_w_out = slice_sums

    parts = []
    for n in range(1, n_grp):
        at = (grp + n) % n_grp
        parts.append(
            [shift(lax.dynamic_index_in_dim(a[1], at, 0, False), n) for a in (first, second)]
        )
    *shared, small = final(meta, (first[0], second[0]), parts)
    small = [small[:, n] for n in (0, 1, 8, 9)]
    grad_w_o, *grads = shared

    return (
        output,
        grad_x,
        *grads,
        grad_w_o,
        *small,
        grad_w_in[None],
        grad_w_out[None],
    )


def solution(mesh):
    both = ("grp", "exp")
    rows, flat, mats = P(both, None), P(both), P("exp", None, None)
    split = P("exp", None, "grp")
    return jax.shard_map(
        partial(local, mesh.shape["grp"], mesh.shape["exp"]),
        mesh=mesh,
        in_specs=(rows, rows, rows, flat) + (rows,) * 4 + (flat,) * 4 + (mats, mats),
        out_specs=(rows,) * 6 + (flat,) * 4 + (split, split),
        check_vma=False,
    )
```

```python
from functools import partial

import jax
import jax.numpy as jnp
from jax import lax
from jax.experimental import pallas as pl
from jax.experimental.pallas import tpu as pltpu
from jax.sharding import PartitionSpec as P

HDIM = 64
QB = 256
EPSILON = 1e-05
NEG_FILL = -1e30
GELU_A = 0.7978845608028654
GELU_B = 0.044715
BF = jnp.bfloat16
F32 = jnp.float32
MIB = 1024 * 1024


def dot_nn(left, right):
    return lax.dot_general(left, right, (((1,), (0,)), ((), ())), preferred_element_type=F32)


def dot_nt(left, right):
    return lax.dot_general(left, right, (((1,), (1,)), ((), ())), preferred_element_type=F32)


def norm_rows(x):
    centred = x - jnp.mean(x, -1, keepdims=True)
    inverse = lax.rsqrt(jnp.mean(centred * centred, -1, keepdims=True) + EPSILON)
    return centred * inverse, inverse


def norm_back(grad, normed, inverse, gain):
    scaled = grad * gain
    return inverse * (
        scaled
        - jnp.mean(scaled, -1, keepdims=True)
        - normed * jnp.mean(scaled * normed, -1, keepdims=True)
    )


def gelu_both(u):
    sq = u * u
    half = 0.5 + 0.5 * jnp.tanh(u * (GELU_A + (GELU_A * GELU_B) * sq))
    act = u * half
    return act, half + act * (1.0 - half) * (2.0 * GELU_A + (6.0 * GELU_A * GELU_B) * sq)


def run(
    kernel,
    args,
    out_shape,
    deps=(),
    scalars=(),
    grid=(1,),
    specs=None,
    outs=None,
    scratch=(),
    micros=5,
    gates=(),
):
    specs = [whole(a.shape) for a in args] if specs is None else specs
    outs = [whole(o.shape) for o in out_shape] if outs is None else outs
    gates, deps = jax.tree.leaves(gates), jax.tree.leaves(deps)
    first, count, results = len(scalars) + len(args), len(deps) + len(gates), len(out_shape)

    def body(*refs):
        last = first + count + results
        kernel(*refs[:first], *refs[first + count : last], *refs[last + len(gates) :])

    anywhere = pl.BlockSpec(memory_space=pl.ANY)
    res = pl.pallas_call(
        body,
        grid_spec=pltpu.PrefetchScalarGridSpec(
            num_scalar_prefetch=len(scalars),
            grid=grid,
            in_specs=list(specs) + [anywhere] * count,
            out_specs=list(outs) + [anywhere] * len(gates),
            scratch_shapes=list(scratch),
        ),
        out_shape=list(out_shape) + [shaped(g.shape, g.dtype) for g in gates],
        input_output_aliases={first + len(deps) + n: results + n for n in range(len(gates))},
        compiler_params=pltpu.CompilerParams(vmem_limit_bytes=60 * MIB),
        cost_estimate=pl.CostEstimate(
            flops=int(micros * 0.517e9), bytes_accessed=10**6, transcendentals=0
        ),
    )(*scalars, *args, *deps, *gates)
    return (list(res[:results]), list(res[results:])) if gates else res


def shaped(shape, dtype=BF):
    return jax.ShapeDtypeStruct(tuple(shape), dtype)


def whole(shape):
    return pl.BlockSpec(shape, lambda *_: (0,) * len(shape), pipeline_mode=pl.Buffered(1))


def one_hot(ids, other):
    return jnp.where(ids == other, 1.0, 0.0).astype(BF)


def enter_kernel(count, meta, ids_ref, rows_ref, *refs):
    pieces, refs = [refs[n * count : (n + 1) * count] for n in range(3)], refs[3 * count :]
    seq_ref, ln_ref, lnt_ref, q_ref, k_ref, mat_q, mat_k, *gain_refs = refs
    width = rows_ref.shape[1]

    @pl.when(pl.program_id(0) == 0)
    def _():
        place(meta, pieces[0], mat_q)
        place(meta, pieces[1], mat_k)
        gains = 0.0
        for piece in pieces[2]:
            for z in range(piece.shape[0]):
                gains = gains + piece[z].astype(F32)
        for n, ref in enumerate(gain_refs[:-1]):
            ref[...] = gains[n : n + 1]
        gain_refs[-1][...] = jnp.transpose(gains)

    lanes = lax.broadcasted_iota(jnp.int32, (QB, rows_ref.shape[0]), 1)
    x = dot_nn(one_hot(ids_ref[...], lanes), rows_ref[...])
    seq_ref[...] = x.astype(BF)
    normed, _ = norm_rows(x)
    ln = (normed * gain_refs[0][...] + gain_refs[1][...]).astype(BF)
    ln_ref[...] = ln
    lnt_ref[...] = jnp.transpose(ln)
    q_ref[...] = dot_nn(ln, mat_q[...].reshape(width, width)).astype(BF)
    k_ref[...] = dot_nn(ln, mat_k[...].reshape(width, width)).astype(BF)


def enter(meta, ids_col, rows, pieces_q, pieces_k, pieces_g, full, deps=()):
    total, width = rows.shape
    block = pl.BlockSpec((QB, width), lambda r, *_: (r, 0))
    turned = pl.BlockSpec((width, QB), lambda r, *_: (0, r))
    rows_out, gain = shaped((total, width)), shaped((1, width), F32)
    seq, ln, lnt, q, k, mat_q, mat_k, *gains = run(
        partial(enter_kernel, len(pieces_q)),
        (ids_col, rows, *[a for a, _ in (*pieces_q, *pieces_k, *pieces_g)]),
        [rows_out, rows_out, shaped((width, total)), rows_out, rows_out]
        + [shaped(full)] * 2
        + [gain] * 4
        + [shaped((width, 16), F32)],
        deps,
        (meta,),
        (total // QB,),
        [pl.BlockSpec((QB, 1), lambda r, *_: (r, 0)), whole(rows.shape)]
        + piece_specs(pieces_q, full[2])
        + piece_specs(pieces_k, full[2])
        + piece_specs(pieces_g, 16),
        [block, block, turned, block, block]
        + [whole(full)] * 2
        + [whole((1, width))] * 4
        + [whole((width, 16))],
        micros=14,
    )
    flat = (width, width)
    return seq, ln, lnt, q, k, mat_q.reshape(flat), mat_k.reshape(flat), gains


def place(meta, refs, full):
    groups, experts = full.shape[0], full.shape[1]
    for r in range(experts):
        for z in range(groups):
            row = lax.rem(meta[1] + (groups - z), groups)
            if len(refs) == 1:
                full[row, r] = refs[0][r, z]
            else:
                full[row, r ^ meta[0]] = refs[r][z]


def piece_specs(pieces, step):
    specs = []
    for array, n in pieces:
        shape = (*array.shape[:-2], step, array.shape[-1])
        at = (0,) * (len(shape) - 2) + (n, 0)
        specs.append(pl.BlockSpec(shape, lambda *_, at=at: at, pipeline_mode=pl.Buffered(1)))
    return specs


def stack_kernel(groups, *refs):
    ins, outs = refs[:groups], refs[groups:]
    for z in range(groups):
        row = 0
        for out in outs:
            out[z] = ins[z][row : row + out.shape[1]]
            row += out.shape[1]


def stack(blocks, rows, deps=()):
    width = blocks[0].shape[1]
    return run(
        partial(stack_kernel, len(blocks)),
        blocks,
        [shaped((len(blocks), r, width)) for r in rows],
        deps,
        micros=2,
    )


def proj_kernel(count, meta, ln_ref, *refs):
    pieces, (out_ref, full_ref) = refs[:count], refs[count:]

    @pl.when(pl.program_id(0) == 0)
    def _():
        place(meta, pieces, full_ref)

    width = ln_ref.shape[1]
    out_ref[...] = dot_nn(ln_ref[...], full_ref[...].reshape(width, width)).astype(BF)


def project(meta, ln, pieces, full, deps=(), gates=()):
    total, width = ln.shape
    block = pl.BlockSpec((QB, width), lambda r, *_: (r, 0))
    (out, mat), gates = run(
        partial(proj_kernel, len(pieces)),
        (ln, *[a for a, _ in pieces]),
        [shaped(ln.shape), shaped(full)],
        deps,
        (meta,),
        (total // QB,),
        [block] + piece_specs(pieces, full[2]),
        [block, whole(full)],
        gates=gates,
    )
    return out, mat.reshape(width, width), gates


def head_lanes(heads):
    pair = 2 * HDIM
    low = lax.broadcasted_iota(jnp.int32, (1, pair), 1) < HDIM
    cols = [slice(h // 2 * pair, (h // 2 + 1) * pair) for h in range(heads)]
    return low, cols, [~low if h % 2 else low for h in range(heads)]


def attend_kernel(flag, q_ref, k_ref, v_ref, o_ref, lse_ref, lse_cols):
    total, heads = q_ref.shape[0], q_ref.shape[1] // HDIM
    low, cols, own = head_lanes(heads)
    each = range(heads)
    causal = lax.broadcasted_iota(jnp.int32, (QB, QB), 1) <= lax.broadcasted_iota(
        jnp.int32, (QB, QB), 0
    )

    def go(long):
        for a in range(0, total, QB):
            b = a + QB
            further = long and a > 0
            q = [
                jnp.where(own[h], q_ref[a:b, cols[h]], jnp.zeros((QB, 2 * HDIM), BF))
                * BF(HDIM**-0.5)
                for h in each
            ]
            near = [jnp.where(causal, dot_nt(q[h], k_ref[a:b, cols[h]]), NEG_FILL) for h in each]
            top = [jnp.max(near[h], 1, keepdims=True) for h in each]
            if further:
                far = [dot_nt(q[h], k_ref[0:a, cols[h]]) for h in each]
                top = [jnp.maximum(top[h], jnp.max(far[h], 1, keepdims=True)) for h in each]
            near = [jnp.exp(near[h] - top[h]) for h in each]
            mass = [jnp.sum(near[h], 1, keepdims=True) for h in each]
            o = [dot_nn(near[h].astype(BF), v_ref[a:b, cols[h]]) for h in each]
            if further:
                far = [jnp.exp(far[h] - top[h]) for h in each]
                mass = [mass[h] + jnp.sum(far[h], 1, keepdims=True) for h in each]
                o = [o[h] + dot_nn(far[h].astype(BF), v_ref[0:a, cols[h]]) for h in each]
            o = [o[h] * (1.0 / mass[h]) for h in each]
            logs = [top[h] + jnp.log(mass[h]) for h in each]
            for h in range(0, heads, 2):
                o_ref[a:b, cols[h]] = jnp.where(low, o[h], o[h + 1]).astype(BF)
                lse_cols[a:b, cols[h]] = jnp.where(low, logs[h], logs[h + 1])

    @pl.when(flag[0] > QB)
    def _():
        go(True)

    @pl.when(flag[0] <= QB)
    def _():
        go(False)

    for h in range(0, heads, 2):
        turned = jnp.transpose(lse_cols[:, cols[h]])
        lse_ref[h // 2, 0:1] = turned[0:1]
        lse_ref[h // 2, 1:2] = turned[HDIM : HDIM + 1]


def attend(flag, q, k, v, deps=()):
    total, width = q.shape
    lanes = 4 * HDIM
    block = pl.BlockSpec((total, lanes), lambda j, *_: (0, j))
    stat = pl.BlockSpec((2, 8, total), lambda j, *_: (j, 0, 0))
    return run(
        attend_kernel,
        (q, k, v),
        [shaped((total, width)), shaped((width // (2 * HDIM), 8, total), F32)],
        deps,
        (flag,),
        (width // lanes,),
        [block] * 3,
        [block, stat],
        [pltpu.VMEM((total, lanes), F32)],
        micros=22,
    )


def attend_back_kernel(
    flag, q_ref, k_ref, v_ref, o_ref, g_ref, lse_ref, dq_ref, dk_ref, dv_ref, dq_turned
):
    total, heads = q_ref.shape[0], q_ref.shape[1] // HDIM
    low, cols, own = head_lanes(heads)
    each = range(heads)
    causal = lax.broadcasted_iota(jnp.int32, (QB, QB), 0) <= lax.broadcasted_iota(
        jnp.int32, (QB, QB), 1
    )
    delta, k_turned = [], []
    for h in range(0, heads, 2):
        prod = jnp.transpose(g_ref[:, cols[h]].astype(F32) * o_ref[:, cols[h]].astype(F32))
        delta.append(jnp.sum(prod[:HDIM], 0, keepdims=True))
        delta.append(jnp.sum(prod[HDIM:], 0, keepdims=True))
        turned = jnp.transpose(k_ref[:, cols[h]])
        k_turned += [turned[:HDIM], turned[HDIM:]]

    def go(long):
        for a in range(0, total, QB):
            b = a + QB
            zero = jnp.zeros((QB, 2 * HDIM), BF)
            k = [jnp.where(own[h], k_ref[a:b, cols[h]], zero) * BF(HDIM**-0.5) for h in each]
            v = [jnp.where(own[h], v_ref[a:b, cols[h]], zero) for h in each]
            dk, dv = [0.0] * heads, [0.0] * heads
            spans = [(a, b)]
            if long and b < total:
                spans.append((b, total))
            for lo, hi in spans:
                scores = [dot_nt(k[h], q_ref[lo:hi, cols[h]]) for h in each]
                dp = [dot_nt(v[h], g_ref[lo:hi, cols[h]]) for h in each]
                probs = [
                    jnp.exp(scores[h] - lse_ref[h // 2, h % 2 : h % 2 + 1, lo:hi]) for h in each
                ]
                if lo == a:
                    probs = [jnp.where(causal, p, 0.0) for p in probs]
                ds = [(probs[h] * (dp[h] - delta[h][:, lo:hi])).astype(BF) for h in each]
                probs = [p.astype(BF) for p in probs]
                for h in each:
                    dv[h] = dv[h] + dot_nn(probs[h], g_ref[lo:hi, cols[h]])
                    dk[h] = dk[h] + dot_nn(ds[h], q_ref[lo:hi, cols[h]])
                    rows = slice(h * HDIM, (h + 1) * HDIM)
                    if a == 0 or not long:
                        dq_turned[rows, lo:hi] = dot_nn(k_turned[h][:, a:b], ds[h])
                    else:
                        dq_turned[rows, lo:hi] += dot_nn(k_turned[h][:, a:b], ds[h])
            for h in range(0, heads, 2):
                both = jnp.where(low, dk[h], dk[h + 1])
                dk_ref[a:b, cols[h]] = (both * HDIM**-0.5).astype(BF)
                dv_ref[a:b, cols[h]] = jnp.where(low, dv[h], dv[h + 1]).astype(BF)

    @pl.when(flag[0] > QB)
    def _():
        go(True)

    @pl.when(flag[0] <= QB)
    def _():
        go(False)

    dq_ref[...] = (jnp.transpose(dq_turned[...]) * HDIM**-0.5).astype(BF)


def attend_back(flag, q, k, v, o, g, lse, part, parts, deps=(), gates=()):
    total, width = q.shape
    lanes = 4 * HDIM
    count = width // lanes // parts
    first = part * count
    block = pl.BlockSpec((total, lanes), lambda j, *_: (0, j + first))
    stat = pl.BlockSpec((2, 8, total), lambda j, *_: (j + first, 0, 0))
    done = pl.BlockSpec((total, lanes), lambda j, *_: (0, j))
    return run(
        attend_back_kernel,
        (q, k, v, o, g, lse),
        [shaped((total, width // parts))] * 3,
        deps,
        (flag,),
        (count,),
        [block] * 5 + [stat],
        [done] * 3,
        [pltpu.VMEM((lanes, total), F32)],
        micros=18,
        gates=gates,
    )


def mix_kernel(count, meta, attn_ref, seq_ref, ids_ref, *refs):
    pieces, (full_ref, out_ref, mixed) = refs[:count], refs[count:]
    r = pl.program_id(0)

    @pl.when(r == 0)
    def _():
        place(meta, pieces, full_ref)

    size, width = attn_ref.shape
    x = seq_ref[...].astype(F32) + dot_nn(attn_ref[...], full_ref[...].reshape(width, width))
    mixed[pl.ds(pl.multiple_of(r * size, size), size)] = x.astype(BF)

    @pl.when(r == pl.num_programs(0) - 1)
    def _():
        to_experts(ids_ref, mixed, out_ref)


def to_experts(ids_ref, rows, out_ref):
    total = rows.shape[0]
    for r in range(0, total, QB):
        want = lax.broadcasted_iota(jnp.int32, (QB, total), 0) + r
        out_ref[r : r + QB] = dot_nn(one_hot(want, ids_ref[...]), rows[...]).astype(BF)


def mix(meta, attn, seq, ids_row, pieces, full, deps=()):
    total, width = attn.shape
    block = pl.BlockSpec((QB, width), lambda r, *_: (r, 0))
    mat, out = run(
        partial(mix_kernel, len(pieces)),
        (attn, seq, ids_row, *[a for a, _ in pieces]),
        [shaped(full), shaped(attn.shape)],
        deps,
        (meta,),
        (total // QB,),
        [block, block, whole(ids_row.shape)] + piece_specs(pieces, full[2]),
        [whole(full), whole(attn.shape)],
        [pltpu.VMEM(attn.shape, BF)],
        micros=8,
    )
    return mat.reshape(width, width), out


def act_grad_kernel(cot_ref, wo_ref, out_ref):
    out_ref[...] = dot_nn(cot_ref[...], wo_ref[...]).astype(BF)


def act_grad(cot, w_out, deps=()):
    total, width = cot.shape
    hidden, tile = w_out.shape[1], 512
    return run(
        act_grad_kernel,
        (cot, w_out),
        [shaped((total, hidden))],
        deps,
        (),
        (hidden // tile,),
        [whole(cot.shape), pl.BlockSpec((width, tile), lambda f: (0, f))],
        [pl.BlockSpec((total, tile), lambda f: (0, f))],
        micros=11,
    )[0]


def expert_kernel(
    steps, x_ref, cot_ref, gain_ref, bias_ref, wi_ref, dact_ref, act_ref, dx_ref, sums_ref, ln, acc
):
    f = pl.program_id(0)
    total, width = ln.shape

    @pl.when(f == 0)
    def _():
        for r in range(0, total, QB):
            normed, _ = norm_rows(x_ref[r : r + QB].astype(F32))
            ln[r : r + QB] = (normed * gain_ref[...] + bias_ref[...]).astype(BF)

    def body(first):
        spans = [slice(r, r + QB) for r in range(0, total, QB)]
        pre = dot_nn(ln[spans[0]], wi_ref[...])
        for n, rows in enumerate(spans):
            act, slope = gelu_both(pre)
            if n + 1 < len(spans):
                pre = dot_nn(ln[spans[n + 1]], wi_ref[...])
            act_ref[rows] = act.astype(BF)
            back = (dact_ref[rows].astype(F32) * slope).astype(BF)
            if first:
                acc[rows] = dot_nt(back, wi_ref[...])
            else:
                acc[rows] += dot_nt(back, wi_ref[...])

    @pl.when(f == 0)
    def _():
        body(True)

    @pl.when(f > 0)
    def _():
        body(False)

    @pl.when(f == steps - 1)
    def _():
        gain_sum = jnp.zeros((1, width), F32)
        bias_sum = gain_sum
        for r in range(0, total, QB):
            rows = slice(r, r + QB)
            normed, inverse = norm_rows(x_ref[rows].astype(F32))
            d = acc[rows]
            gain_sum = gain_sum + jnp.sum(d * normed, 0, keepdims=True)
            bias_sum = bias_sum + jnp.sum(d, 0, keepdims=True)
            back = norm_back(d, normed, inverse, gain_ref[...])
            dx_ref[rows] = (cot_ref[rows].astype(F32) + back).astype(BF)
        sums_ref[0:1] = gain_sum
        sums_ref[1:2] = bias_sum


def expert(x, cot, gain, bias, w_in, dact, deps=()):
    total, width = x.shape
    hidden, tile = w_in.shape[1], 1024
    steps = hidden // tile
    cols = pl.BlockSpec((width, tile), lambda f: (0, f))
    rows = pl.BlockSpec((total, tile), lambda f: (0, f))
    return run(
        partial(expert_kernel, steps),
        (x, cot, gain, bias, w_in, dact),
        [shaped((total, hidden)), shaped(x.shape), shaped((8, width), F32)],
        deps,
        (),
        (steps,),
        [whole(x.shape)] * 2 + [whole((1, width))] * 2 + [cols, rows],
        [rows, whole(x.shape), whole((8, width))],
        [pltpu.VMEM(x.shape, BF), pltpu.VMEM(x.shape, F32)],
        micros=34,
    )


def expert_out_kernel(x_ref, act_ref, wo_ref, out_ref):
    out = x_ref[...].astype(F32) + dot_nt(act_ref[...], wo_ref[...])
    out_ref[...] = out.astype(BF)


def expert_out(x, act, w_out, deps=()):
    total, width = x.shape
    hidden, tile = w_out.shape[1], 256
    part = pl.BlockSpec((total, tile), lambda n: (0, n))
    return run(
        expert_out_kernel,
        (x, act, w_out),
        [shaped(x.shape)],
        deps,
        (),
        (width // tile,),
        [part, whole(act.shape), pl.BlockSpec((tile, hidden), lambda n: (n, 0))],
        [part],
        micros=12,
    )[0]


def turn_kernel(meta, wi_ref, wo_ref, wit_ref, wot_ref):
    wit_ref[...] = jnp.transpose(wi_ref[...])
    wot_ref[...] = jnp.transpose(wo_ref[...])


def turn_slices(meta, w_in, w_out, hidden):
    width, tile = w_in.shape[0], min(256, hidden)
    tiles = hidden // tile
    cols = pl.BlockSpec((width, tile), lambda f, m: (0, m[1] * tiles + f))
    rows = pl.BlockSpec((tile, width), lambda f, m: (f, 0))
    return run(
        turn_kernel,
        (w_in, w_out),
        [shaped((hidden, width))] * 2,
        (),
        (meta,),
        (tiles,),
        [cols] * 2,
        [rows] * 2,
        micros=5,
    )


def slice_kernel(t, groups, first, last, meta, *refs):
    valid = [meta[1] >= t, meta[1] + t < groups] if t else [meta[1] >= 0]
    count = len(valid)
    xs, cots = refs[:count], refs[count : 2 * count]
    gain_ref, bias_ref, wi_ref, wo_ref = refs[2 * count : 2 * count + 4]
    rest = refs[2 * count + 4 :]
    if not first:
        in_prev, out_prev = rest[:2]
        rest = rest[2:]
    in_ref, out_ref, in_acc, out_acc, lns, rows, sems = rest
    f = pl.program_id(0)
    total = lns.shape[1]

    def copies(n):
        return (
            pltpu.make_async_copy(xs[n], lns.at[n], sems.at[n, 0]),
            pltpu.make_async_copy(cots[n], rows.at[n], sems.at[n, 1]),
        )

    for n in range(count):

        @pl.when((f == 0) & valid[n])
        def _(n=n):
            for copy in copies(n):
                copy.start()

    if first:
        in_acc[...] = jnp.zeros_like(in_acc)
        out_acc[...] = jnp.zeros_like(out_acc)
    else:
        in_acc[...] = in_prev[...]
        out_acc[...] = out_prev[...]
    for n in range(count):

        @pl.when(valid[n])
        def _(n=n):
            @pl.when(f == 0)
            def _():
                for copy in copies(n):
                    copy.wait()
                for r in range(0, total, QB):
                    normed, _ = norm_rows(lns[n, r : r + QB].astype(F32))
                    lns[n, r : r + QB] = (normed * gain_ref[...] + bias_ref[...]).astype(BF)

            pre = dot_nt(wi_ref[...], lns[n])
            grad = dot_nt(wo_ref[...], rows[n])
            act, slope = gelu_both(pre)
            back = (grad * slope).astype(BF)
            in_acc[...] += dot_nn(back, lns[n])
            out_acc[...] += dot_nn(act.astype(BF), rows[n])

    if last:
        in_ref[...] = jnp.transpose(in_acc[...])
        out_ref[...] = jnp.transpose(out_acc[...])
    else:
        in_ref[...] = in_acc[...]
        out_ref[...] = out_acc[...]


def slice_grads(meta, t, groups, xs, cots, gain, bias, wi_turned, wo_turned, prev, deps=(), gates=()):
    count = len(xs)
    total, width = xs[0].shape
    hidden = wi_turned.shape[0]
    tile = min(256, hidden)
    rows = pl.BlockSpec((tile, width), lambda f, *_: (f, 0))
    cols = pl.BlockSpec((width, tile), lambda f, *_: (0, f))
    anywhere = pl.BlockSpec(memory_space=pl.ANY)
    first, last = prev is None, t == groups - 1
    return run(
        partial(slice_kernel, t, groups, first, last),
        (*xs, *cots, gain, bias, wi_turned, wo_turned, *(() if first else prev)),
        [shaped((width, hidden) if last else (hidden, width), F32)] * 2,
        deps,
        (meta,),
        (hidden // tile,),
        [anywhere] * (2 * count)
        + [whole((1, width))] * 2
        + [rows] * (2 if first else 4),
        [cols if last else rows] * 2,
        [pltpu.VMEM((tile, width), F32)] * 2
        + [pltpu.VMEM((count, total, width), BF)] * 2
        + [pltpu.SemaphoreType.DMA((count, 2))],
        micros=18,
        gates=gates,
    )


def back_kernel(ids_ref, mat_ref, rows_ref, dmix_ref, dattn_ref):
    lanes = lax.broadcasted_iota(jnp.int32, (QB, rows_ref.shape[0]), 1)
    x = dot_nn(one_hot(ids_ref[...], lanes), rows_ref[...]).astype(BF)
    dmix_ref[...] = x
    dattn_ref[...] = dot_nt(x, mat_ref[...]).astype(BF)


def back_in(ids_col, mat, rows, deps=()):
    total, width = rows.shape
    block = pl.BlockSpec((QB, width), lambda r: (r, 0))
    return run(
        back_kernel,
        (ids_col, mat, rows),
        [shaped(rows.shape)] * 2,
        deps,
        (),
        (total // QB,),
        [pl.BlockSpec((QB, 1), lambda r: (r, 0)), whole(mat.shape), whole(rows.shape)],
        [block] * 2,
        micros=7,
    )


def shared_kernel(turn, count, norm, left_ref, *refs):
    rights, refs = refs[:count], refs[count:]
    if norm:
        mats, (gains_ref, small_ref, out, tops) = refs[:count], refs[count:]
    else:
        (out,) = refs
    experts, step = out.shape[0], out.shape[2]
    left = jnp.transpose(left_ref[...]) if turn else left_ref[...]

    def put(values, cols):
        values = values.astype(BF)
        for e in range(experts):
            part = values[e * step : (e + 1) * step]
            out[e, 0, :, cols : cols + values.shape[1]] = part

    if norm:

        @pl.when(pl.program_id(0) == 0)
        def _():
            for n, right in enumerate(rights):
                tops[n : n + 1] = jnp.sum(right[...].astype(F32), 0, keepdims=True)

    cols, with_gain, with_bias = 0, 0.0, 0.0
    for n, right in enumerate(rights):
        sums = dot_nn(left, right[...])
        if norm:
            mat = mats[n][...].astype(F32)
            with_gain = with_gain + jnp.sum(mat * sums, -1, keepdims=True)
            with_bias = with_bias + jnp.sum(mat * tops[n : n + 1], -1, keepdims=True)
        put(sums, cols)
        cols += right.shape[1]
    if norm:
        with_gain = (with_gain - gains_ref[:, 1:2] * with_bias) / gains_ref[:, 0:1]
        rest = jnp.zeros((sums.shape[0], 120), F32)
        extra = jnp.concatenate([jnp.transpose(small_ref[...]), rest], -1)
        lane = lax.broadcasted_iota(jnp.int32, (1, 128), 1)
        extra = jnp.where(lane == 8, with_gain, jnp.where(lane == 9, with_bias, extra))
        put(extra, cols)


def shared_grads(left, turned, rights, experts, groups, norm=(), deps=(), gates=()):
    total = rights[0].shape[0]
    features = left.shape[0 if turned else 1]
    step, block = features // (experts * groups), features // groups
    width = sum(r.shape[1] for r in rights) + (128 if norm else 0)
    rows = pl.BlockSpec((block, total), lambda g: (g, 0))
    specs = [rows if turned else pl.BlockSpec((total, block), lambda g: (0, g))]
    specs += [whole(r.shape) for r in rights]
    args, scratch = [left, *rights], []
    if norm:
        mats, gains, small = norm
        args += [*mats, gains, small]
        specs += [pl.BlockSpec((block, m.shape[1]), lambda g: (g, 0)) for m in mats]
        specs += [pl.BlockSpec((block, 16), lambda g: (g, 0))]
        specs += [pl.BlockSpec((8, block), lambda g: (0, g))]
        scratch = [pltpu.VMEM((8, rights[0].shape[1]), F32)]
    shape = (experts, groups, step, width)
    return run(
        partial(shared_kernel, not turned, len(rights), bool(norm)),
        args,
        [shaped(shape)],
        deps,
        (),
        (groups,),
        specs,
        [pl.BlockSpec((experts, 1, step, width), lambda g: (0, g, 0, 0))],
        scratch,
        micros=4 * len(rights),
        gates=gates,
    )


def total_kernel(meta, first_ref, second_ref, *outs):
    groups = len(outs)
    g = pl.program_id(0)
    for s in range(groups):

        @pl.when(g == lax.rem(meta[1] + s, groups))
        def _(out=outs[s]):
            col = 0
            for ref in (first_ref, second_ref):
                total = ref[0, 0].astype(F32)
                for e in range(1, ref.shape[0]):
                    total = total + ref[e, 0].astype(F32)
                out[:, col : col + total.shape[1]] = total.astype(out.dtype)
                col += total.shape[1]


def total_over(meta, first, second, deps=(), gates=()):
    groups, step = first.shape[1:3]
    width = first.shape[3] + second.shape[3]
    specs = []
    for a in (first, second):
        block = (a.shape[0], 1, *a.shape[2:])
        specs.append(pl.BlockSpec(block, lambda g, *_: (0, g, 0, 0)))
    return run(
        total_kernel,
        (first, second),
        [shaped((step, width), F32)] + [shaped((step, width))] * (groups - 1),
        deps,
        (meta,),
        (groups,),
        specs,
        [whole((step, width))] * groups,
        micros=5,
        gates=gates,
    )


def final_kernel(*refs):
    ins, (o_ref, q_ref, k_ref, v_ref, *small) = refs[:-8], refs[-8:]
    total = ins[0][...]
    for ref in ins[1:]:
        total = total + ref[...].astype(F32)
    width = o_ref.shape[1]
    for n, ref in enumerate((o_ref, q_ref, k_ref, v_ref)):
        ref[...] = total[:, n * width : (n + 1) * width]
    turned = jnp.transpose(total[:, 4 * width :])
    for n, ref in zip((8, 9, 0, 1), small):
        ref[...] = turned[n : n + 1]


def final(parts, width):
    step = parts[0].shape[0]
    return run(
        final_kernel,
        parts,
        [shaped((step, width), F32)] * 4 + [shaped((1, step), F32)] * 4,
        micros=2,
    )


def first_kernel(*refs):
    grads, mats = refs[:3], refs[3:6]
    seq_ref, dmix_ref, gain_ref, ids_ref, out_ref, rows = refs[6:]
    r = pl.program_id(0)
    size = seq_ref.shape[0]
    grad = dot_nt(grads[0][...], mats[0][...])
    for n in (1, 2):
        grad = grad + dot_nt(grads[n][...], mats[n][...])
    normed, inverse = norm_rows(seq_ref[...].astype(F32))
    back = dmix_ref[...].astype(F32) + norm_back(grad, normed, inverse, gain_ref[...])
    rows[pl.ds(pl.multiple_of(r * size, size), size)] = back.astype(BF)

    @pl.when(r == pl.num_programs(0) - 1)
    def _():
        to_experts(ids_ref, rows, out_ref)


def first_back(grads, mats, seq, dmix, gain, ids_row, deps=()):
    total, width = seq.shape
    block = pl.BlockSpec((QB, width), lambda r: (r, 0))
    return run(
        first_kernel,
        (*grads, *mats, seq, dmix, gain, ids_row),
        [shaped((total, width))],
        deps,
        (),
        (total // QB,),
        [block] * 3
        + [whole((width, width))] * 3
        + [block] * 2
        + [whole((1, width)), whole((1, total))],
        [whole((total, width))],
        [pltpu.VMEM((total, width), BF)],
        micros=16,
    )[0]


def local(
    n_grp,
    n_exp,
    tokens,
    cotangent,
    arrival,
    seq_length,
    w_q,
    w_k,
    w_v,
    w_o,
    ln1_gain,
    ln1_bias,
    ln2_gain,
    ln2_bias,
    w_in,
    w_out,
):
    me, grp = lax.axis_index("exp"), lax.axis_index("grp")
    meta = jnp.stack([me, grp]).astype(jnp.int32)
    width = tokens.shape[1]
    step = w_q.shape[0]
    hidden = w_in.shape[2] // n_grp
    both = ("grp", "exp")

    def swap(a, k):
        return lax.ppermute(a, "exp", [(i, i ^ k) for i in range(n_exp)])

    def shift(a, k):
        return lax.ppermute(a, "grp", [(i, (i + k) % n_grp) for i in range(n_grp)])

    def exchange(rows):
        return lax.all_to_all(rows, "exp", split_axis=0, concat_axis=0, tiled=True)

    bits = []
    while 2 ** len(bits) < n_exp:
        bits.append(2 ** len(bits))
    orders = [bits[:0:-1] + bits[:1], bits[1:] + bits[:1]]

    def gather_pair(own, cut):
        first = lambda a: a[0] if isinstance(a, tuple) else a[:, :cut]
        second = lambda a: a[1] if isinstance(a, tuple) else a[:, cut:]
        have = {0: own}
        for r in sorted(range(1, n_exp), key=lambda r: (bin(r).count("1"), -r)):
            b, c = (max((b for b in bits if r & b), key=order.index) for order in orders)
            if b == c and not isinstance(have[r ^ b], tuple):
                have[r] = swap(have[r ^ b], b)
            else:
                have[r] = (swap(first(have[r ^ b]), b), swap(second(have[r ^ c]), c))
        return [have[r] for r in range(n_exp)]

    def line_step(t, up, down):
        up = lax.ppermute(up, "grp", [(i, i + 1) for i in range(t - 1, n_grp - 1)])
        down = lax.ppermute(down, "grp", [(i + 1, i) for i in range(n_grp - t)])
        return up, down

    def line(a):
        steps = [(a, a)]
        for t in range(1, n_grp):
            steps.append(line_step(t, *steps[-1]))
        return steps

    ids_row = arrival
    ids_col = arrival.reshape(-1, 1)
    flag = seq_length

    gains = jnp.stack([ln1_gain, ln1_bias, ln2_gain, ln2_bias])
    mine = jnp.zeros((16, width), BF)
    mine = lax.dynamic_update_slice(mine, gains, (0, (grp * n_exp + me) * step))
    mine = jnp.concatenate([w_q, w_k, mine, w_v, w_o])
    mine = [mine] + [shift(mine, k) for k in range(1, n_grp)]
    arrived = exchange(tokens)
    w_first, w_second = w_in[0], w_out[0]
    wi_turned, wo_turned = turn_slices(meta, w_first, w_second, hidden)
    dact = act_grad(cotangent, w_second)
    pair_qk, pair_vo = stack(mine, (2 * step + 16, 2 * step), deps=(arrived, dact, wi_turned))
    pieces = gather_pair(pair_qk, step)
    all_vo = lax.all_gather(pair_vo, "exp", axis=0)

    full = (n_grp, n_exp, step, width)
    is_cut = lambda a: isinstance(a, tuple)
    pieces_q = [(a[0], 0) if is_cut(a) else (a, 0) for a in pieces]
    pieces_k = [(a[1], 0) if is_cut(a) else (a, 1) for a in pieces]
    pieces_g = [
        (a[1], step // 16) if is_cut(a) else (a, 2 * step // 16) for a in pieces
    ]
    pieces_v, pieces_o = [(all_vo, 0)], [(all_vo, 1)]

    cot_line, x_line = [(cotangent,) * 2], []

    def forward(steps, gated=None):
        if len(steps) < n_grp:
            steps.append(line_step(len(steps), *(gated or steps[-1])))
        return steps[-1]

    forward(cot_line)
    seq, ln_one, ln_turned, q, k, mat_q, mat_k, gains = enter(
        meta, ids_col, arrived, pieces_q, pieces_k, pieces_g, full
    )
    v, mat_v, cot_line[1] = project(meta, ln_one, pieces_v, full, gates=cot_line[1])
    forward(cot_line)
    attn, lse = attend(flag, q, k, v)
    mat_o, leaving = mix(meta, attn, seq, ids_row, pieces_o, full)
    x = exchange(leaving)

    act, dx, sums_two = expert(
        x, cotangent, gains[2], gains[3], w_first, dact, deps=cot_line[-1]
    )
    x_line = [(x,) * 2]
    forward(x_line)
    output = expert_out(x, act, w_second)

    def slices(t, sums, deps=(), gates=()):
        xs, cots = (list(line[t])[: 2 if t else 1] for line in (x_line, cot_line))
        last = (gains[2], gains[3], wi_turned, wo_turned, sums, deps, gates)
        return slice_grads(meta, t, n_grp, xs, cots, *last)

    slice_sums, x_line[1] = slices(0, None, deps=output, gates=x_line[1])
    back = exchange(dx)
    dmix, dattn = back_in(ids_col, mat_o, back, deps=slice_sums)
    forward(x_line)

    (first,) = shared_grads(attn, False, [dmix], n_exp, n_grp)
    grads, cot_line[-1] = attend_back(
        flag, q, k, v, attn, dattn, lse, 0, 1, deps=first, gates=cot_line[-1]
    )
    while len(cot_line) < n_grp:
        forward(cot_line)
    first = exchange(first)
    (second,), x_line[-1] = shared_grads(
        ln_turned,
        True,
        grads,
        n_exp,
        n_grp,
        ((mat_q, mat_k, mat_v), gains[4], sums_two),
        gates=x_line[-1],
    )
    while len(x_line) < n_grp:
        forward(x_line)
    dfirst = first_back(
        grads, (mat_q, mat_k, mat_v), seq, dmix, gains[0], ids_row, deps=(first, second)
    )
    second = exchange(second)
    for t in range(1, n_grp):
        deps = (dfirst,) if t == 1 else ()
        if t == n_grp - 1:
            deps = (deps, slice_sums, cot_line[-1])
            parts, (dfirst,) = total_over(meta, first, second, deps, dfirst)
            deps = parts
            parts = [parts[0]] + [shift(a, n + 1) for n, a in enumerate(parts[1:])]
        slice_sums = slices(t, slice_sums, deps)
    grad_x = exchange(dfirst)
    grad_w_in, grad_w_out = slice_sums
    grad_w_o, *grads = final(parts, width)
    grads, small = grads[:3], [a[0] for a in grads[3:]]

    return (
        output,
        grad_x,
        *grads,
        grad_w_o,
        *small,
        grad_w_in[None],
        grad_w_out[None],
    )


def solution(mesh):
    both = ("grp", "exp")
    rows, flat, mats = P(both, None), P(both), P("exp", None, None)
    split = P("exp", None, "grp")
    return jax.shard_map(
        partial(local, mesh.shape["grp"], mesh.shape["exp"]),
        mesh=mesh,
        in_specs=(rows, rows, rows, flat) + (rows,) * 4 + (flat,) * 4 + (mats, mats),
        out_specs=(rows,) * 6 + (flat,) * 4 + (split, split),
        check_vma=False,
    )
```

```python
from functools import partial

import jax
import jax.numpy as jnp
from jax import lax
from jax.experimental import pallas as pl
from jax.experimental.pallas import tpu as pltpu
from jax.sharding import PartitionSpec as P

HDIM = 64
QB = 256
EPSILON = 1e-05
NEG_FILL = -1e30
GELU_A = 0.7978845608028654
GELU_B = 0.044715
BF = jnp.bfloat16
F32 = jnp.float32
MIB = 1024 * 1024


def dot_nn(left, right):
    return lax.dot_general(left, right, (((1,), (0,)), ((), ())), preferred_element_type=F32)


def dot_nt(left, right):
    return lax.dot_general(left, right, (((1,), (1,)), ((), ())), preferred_element_type=F32)


def norm_rows(x):
    centred = x - jnp.mean(x, -1, keepdims=True)
    inverse = lax.rsqrt(jnp.mean(centred * centred, -1, keepdims=True) + EPSILON)
    return centred * inverse, inverse


def norm_back(grad, normed, inverse, gain):
    scaled = grad * gain
    return inverse * (
        scaled
        - jnp.mean(scaled, -1, keepdims=True)
        - normed * jnp.mean(scaled * normed, -1, keepdims=True)
    )


def gelu_both(u):
    sq = u * u
    half = 0.5 + 0.5 * jnp.tanh(u * (GELU_A + (GELU_A * GELU_B) * sq))
    act = u * half
    return act, half + act * (1.0 - half) * (2.0 * GELU_A + (6.0 * GELU_A * GELU_B) * sq)


def run(
    kernel,
    args,
    out_shape,
    deps=(),
    scalars=(),
    grid=(1,),
    specs=None,
    outs=None,
    scratch=(),
    micros=5,
    gates=(),
):
    specs = [whole(a.shape) for a in args] if specs is None else specs
    outs = [whole(o.shape) for o in out_shape] if outs is None else outs
    gates, deps = jax.tree.leaves(gates), jax.tree.leaves(deps)
    first, count, results = len(scalars) + len(args), len(deps) + len(gates), len(out_shape)

    def body(*refs):
        last = first + count + results
        kernel(*refs[:first], *refs[first + count : last], *refs[last + len(gates) :])

    anywhere = pl.BlockSpec(memory_space=pl.ANY)
    res = pl.pallas_call(
        body,
        grid_spec=pltpu.PrefetchScalarGridSpec(
            num_scalar_prefetch=len(scalars),
            grid=grid,
            in_specs=list(specs) + [anywhere] * count,
            out_specs=list(outs) + [anywhere] * len(gates),
            scratch_shapes=list(scratch),
        ),
        out_shape=list(out_shape) + [shaped(g.shape, g.dtype) for g in gates],
        input_output_aliases={first + len(deps) + n: results + n for n in range(len(gates))},
        compiler_params=pltpu.CompilerParams(vmem_limit_bytes=60 * MIB),
        cost_estimate=pl.CostEstimate(
            flops=int(micros * 0.517e9), bytes_accessed=10**6, transcendentals=0
        ),
    )(*scalars, *args, *deps, *gates)
    return (list(res[:results]), list(res[results:])) if gates else res


def shaped(shape, dtype=BF):
    return jax.ShapeDtypeStruct(tuple(shape), dtype)


def whole(shape):
    return pl.BlockSpec(shape, lambda *_: (0,) * len(shape), pipeline_mode=pl.Buffered(1))


def one_hot(ids, other):
    return jnp.where(ids == other, 1.0, 0.0).astype(BF)


def enter_kernel(count, meta, ids_ref, rows_ref, *refs):
    pieces, refs = [refs[n * count : (n + 1) * count] for n in range(3)], refs[3 * count :]
    seq_ref, ln_ref, lnt_ref, q_ref, k_ref, mat_q, mat_k, *gain_refs = refs
    width = rows_ref.shape[1]

    @pl.when(pl.program_id(0) == 0)
    def _():
        place(meta, pieces[0], mat_q)
        place(meta, pieces[1], mat_k)
        gains = 0.0
        for piece in pieces[2]:
            for z in range(piece.shape[0]):
                gains = gains + piece[z].astype(F32)
        for n, ref in enumerate(gain_refs[:-1]):
            ref[...] = gains[n : n + 1]
        gain_refs[-1][...] = jnp.transpose(gains)

    lanes = lax.broadcasted_iota(jnp.int32, (QB, rows_ref.shape[0]), 1)
    x = dot_nn(one_hot(ids_ref[...], lanes), rows_ref[...])
    seq_ref[...] = x.astype(BF)
    normed, _ = norm_rows(x)
    ln = (normed * gain_refs[0][...] + gain_refs[1][...]).astype(BF)
    ln_ref[...] = ln
    lnt_ref[...] = jnp.transpose(ln)
    q_ref[...] = dot_nn(ln, mat_q[...].reshape(width, width)).astype(BF)
    k_ref[...] = dot_nn(ln, mat_k[...].reshape(width, width)).astype(BF)


def enter(meta, ids_col, rows, pieces_q, pieces_k, pieces_g, full, deps=()):
    total, width = rows.shape
    block = pl.BlockSpec((QB, width), lambda r, *_: (r, 0))
    turned = pl.BlockSpec((width, QB), lambda r, *_: (0, r))
    rows_out, gain = shaped((total, width)), shaped((1, width), F32)
    seq, ln, lnt, q, k, mat_q, mat_k, *gains = run(
        partial(enter_kernel, len(pieces_q)),
        (ids_col, rows, *[a for a, _ in (*pieces_q, *pieces_k, *pieces_g)]),
        [rows_out, rows_out, shaped((width, total)), rows_out, rows_out]
        + [shaped(full)] * 2
        + [gain] * 4
        + [shaped((width, 16), F32)],
        deps,
        (meta,),
        (total // QB,),
        [pl.BlockSpec((QB, 1), lambda r, *_: (r, 0)), whole(rows.shape)]
        + piece_specs(pieces_q, full[2])
        + piece_specs(pieces_k, full[2])
        + piece_specs(pieces_g, 16),
        [block, block, turned, block, block]
        + [whole(full)] * 2
        + [whole((1, width))] * 4
        + [whole((width, 16))],
        micros=14,
    )
    flat = (width, width)
    return seq, ln, lnt, q, k, mat_q.reshape(flat), mat_k.reshape(flat), gains


def place(meta, refs, full):
    groups, experts = full.shape[0], full.shape[1]
    for r in range(experts):
        for z in range(groups):
            row = lax.rem(meta[1] + (groups - z), groups)
            if len(refs) == 1:
                full[row, r] = refs[0][r, z]
            else:
                full[row, r ^ meta[0]] = refs[r][z]


def piece_specs(pieces, step):
    specs = []
    for array, n in pieces:
        shape = (*array.shape[:-2], step, array.shape[-1])
        at = (0,) * (len(shape) - 2) + (n, 0)
        specs.append(pl.BlockSpec(shape, lambda *_, at=at: at, pipeline_mode=pl.Buffered(1)))
    return specs


def stack_kernel(groups, *refs):
    ins, outs = refs[:groups], refs[groups:]
    for z in range(groups):
        row = 0
        for out in outs:
            out[z] = ins[z][row : row + out.shape[1]]
            row += out.shape[1]


def stack(blocks, rows, deps=()):
    width = blocks[0].shape[1]
    return run(
        partial(stack_kernel, len(blocks)),
        blocks,
        [shaped((len(blocks), r, width)) for r in rows],
        deps,
        micros=2,
    )


def proj_kernel(count, meta, ln_ref, *refs):
    pieces, (out_ref, full_ref) = refs[:count], refs[count:]

    @pl.when(pl.program_id(0) == 0)
    def _():
        place(meta, pieces, full_ref)

    width = ln_ref.shape[1]
    out_ref[...] = dot_nn(ln_ref[...], full_ref[...].reshape(width, width)).astype(BF)


def project(meta, ln, pieces, full, deps=(), gates=()):
    total, width = ln.shape
    block = pl.BlockSpec((QB, width), lambda r, *_: (r, 0))
    (out, mat), gates = run(
        partial(proj_kernel, len(pieces)),
        (ln, *[a for a, _ in pieces]),
        [shaped(ln.shape), shaped(full)],
        deps,
        (meta,),
        (total // QB,),
        [block] + piece_specs(pieces, full[2]),
        [block, whole(full)],
        gates=gates,
    )
    return out, mat.reshape(width, width), gates


def head_lanes(heads):
    pair = 2 * HDIM
    low = lax.broadcasted_iota(jnp.int32, (1, pair), 1) < HDIM
    cols = [slice(h // 2 * pair, (h // 2 + 1) * pair) for h in range(heads)]
    return low, cols, [~low if h % 2 else low for h in range(heads)]


def attend_kernel(flag, q_ref, k_ref, v_ref, o_ref, lse_ref, lse_cols):
    total, heads = q_ref.shape[0], q_ref.shape[1] // HDIM
    low, cols, own = head_lanes(heads)
    each = range(heads)
    causal = lax.broadcasted_iota(jnp.int32, (QB, QB), 1) <= lax.broadcasted_iota(
        jnp.int32, (QB, QB), 0
    )

    def go(long):
        for a in range(0, total, QB):
            b = a + QB
            further = long and a > 0
            q = [
                jnp.where(own[h], q_ref[a:b, cols[h]], jnp.zeros((QB, 2 * HDIM), BF))
                * BF(HDIM**-0.5)
                for h in each
            ]
            near = [jnp.where(causal, dot_nt(q[h], k_ref[a:b, cols[h]]), NEG_FILL) for h in each]
            top = [jnp.max(near[h], 1, keepdims=True) for h in each]
            if further:
                far = [dot_nt(q[h], k_ref[0:a, cols[h]]) for h in each]
                top = [jnp.maximum(top[h], jnp.max(far[h], 1, keepdims=True)) for h in each]
            near = [jnp.exp(near[h] - top[h]) for h in each]
            mass = [jnp.sum(near[h], 1, keepdims=True) for h in each]
            o = [dot_nn(near[h].astype(BF), v_ref[a:b, cols[h]]) for h in each]
            if further:
                far = [jnp.exp(far[h] - top[h]) for h in each]
                mass = [mass[h] + jnp.sum(far[h], 1, keepdims=True) for h in each]
                o = [o[h] + dot_nn(far[h].astype(BF), v_ref[0:a, cols[h]]) for h in each]
            o = [o[h] * (1.0 / mass[h]) for h in each]
            logs = [top[h] + jnp.log(mass[h]) for h in each]
            for h in range(0, heads, 2):
                o_ref[a:b, cols[h]] = jnp.where(low, o[h], o[h + 1]).astype(BF)
                lse_cols[a:b, cols[h]] = jnp.where(low, logs[h], logs[h + 1])

    @pl.when(flag[0] > QB)
    def _():
        go(True)

    @pl.when(flag[0] <= QB)
    def _():
        go(False)

    for h in range(0, heads, 2):
        turned = jnp.transpose(lse_cols[:, cols[h]])
        lse_ref[h // 2, 0:1] = turned[0:1]
        lse_ref[h // 2, 1:2] = turned[HDIM : HDIM + 1]


def attend(flag, q, k, v, deps=()):
    total, width = q.shape
    lanes = 4 * HDIM
    block = pl.BlockSpec((total, lanes), lambda j, *_: (0, j))
    stat = pl.BlockSpec((2, 8, total), lambda j, *_: (j, 0, 0))
    return run(
        attend_kernel,
        (q, k, v),
        [shaped((total, width)), shaped((width // (2 * HDIM), 8, total), F32)],
        deps,
        (flag,),
        (width // lanes,),
        [block] * 3,
        [block, stat],
        [pltpu.VMEM((total, lanes), F32)],
        micros=22,
    )


def attend_back_kernel(
    flag, q_ref, k_ref, v_ref, o_ref, g_ref, lse_ref, dq_ref, dk_ref, dv_ref, dq_turned
):
    total, heads = q_ref.shape[0], q_ref.shape[1] // HDIM
    low, cols, own = head_lanes(heads)
    each = range(heads)
    causal = lax.broadcasted_iota(jnp.int32, (QB, QB), 0) <= lax.broadcasted_iota(
        jnp.int32, (QB, QB), 1
    )
    delta, k_turned = [], []
    for h in range(0, heads, 2):
        prod = jnp.transpose(g_ref[:, cols[h]].astype(F32) * o_ref[:, cols[h]].astype(F32))
        delta.append(jnp.sum(prod[:HDIM], 0, keepdims=True))
        delta.append(jnp.sum(prod[HDIM:], 0, keepdims=True))
        turned = jnp.transpose(k_ref[:, cols[h]])
        k_turned += [turned[:HDIM], turned[HDIM:]]

    def go(long):
        for a in range(0, total, QB):
            b = a + QB
            zero = jnp.zeros((QB, 2 * HDIM), BF)
            k = [jnp.where(own[h], k_ref[a:b, cols[h]], zero) * BF(HDIM**-0.5) for h in each]
            v = [jnp.where(own[h], v_ref[a:b, cols[h]], zero) for h in each]
            dk, dv = [0.0] * heads, [0.0] * heads
            spans = [(a, b)]
            if long and b < total:
                spans.append((b, total))
            for lo, hi in spans:
                scores = [dot_nt(k[h], q_ref[lo:hi, cols[h]]) for h in each]
                dp = [dot_nt(v[h], g_ref[lo:hi, cols[h]]) for h in each]
                probs = [
                    jnp.exp(scores[h] - lse_ref[h // 2, h % 2 : h % 2 + 1, lo:hi]) for h in each
                ]
                if lo == a:
                    probs = [jnp.where(causal, p, 0.0) for p in probs]
                ds = [(probs[h] * (dp[h] - delta[h][:, lo:hi])).astype(BF) for h in each]
                probs = [p.astype(BF) for p in probs]
                for h in each:
                    dv[h] = dv[h] + dot_nn(probs[h], g_ref[lo:hi, cols[h]])
                    dk[h] = dk[h] + dot_nn(ds[h], q_ref[lo:hi, cols[h]])
                    rows = slice(h * HDIM, (h + 1) * HDIM)
                    if a == 0 or not long:
                        dq_turned[rows, lo:hi] = dot_nn(k_turned[h][:, a:b], ds[h])
                    else:
                        dq_turned[rows, lo:hi] += dot_nn(k_turned[h][:, a:b], ds[h])
            for h in range(0, heads, 2):
                both = jnp.where(low, dk[h], dk[h + 1])
                dk_ref[a:b, cols[h]] = (both * HDIM**-0.5).astype(BF)
                dv_ref[a:b, cols[h]] = jnp.where(low, dv[h], dv[h + 1]).astype(BF)

    @pl.when(flag[0] > QB)
    def _():
        go(True)

    @pl.when(flag[0] <= QB)
    def _():
        go(False)

    dq_ref[...] = (jnp.transpose(dq_turned[...]) * HDIM**-0.5).astype(BF)


def attend_back(flag, q, k, v, o, g, lse, part, parts, deps=(), gates=()):
    total, width = q.shape
    lanes = 4 * HDIM
    count = width // lanes // parts
    first = part * count
    block = pl.BlockSpec((total, lanes), lambda j, *_: (0, j + first))
    stat = pl.BlockSpec((2, 8, total), lambda j, *_: (j + first, 0, 0))
    done = pl.BlockSpec((total, lanes), lambda j, *_: (0, j))
    return run(
        attend_back_kernel,
        (q, k, v, o, g, lse),
        [shaped((total, width // parts))] * 3,
        deps,
        (flag,),
        (count,),
        [block] * 5 + [stat],
        [done] * 3,
        [pltpu.VMEM((lanes, total), F32)],
        micros=18,
        gates=gates,
    )


def mix_kernel(count, meta, attn_ref, seq_ref, ids_ref, *refs):
    pieces, (full_ref, out_ref, mixed) = refs[:count], refs[count:]
    r = pl.program_id(0)

    @pl.when(r == 0)
    def _():
        place(meta, pieces, full_ref)

    size, width = attn_ref.shape
    x = seq_ref[...].astype(F32) + dot_nn(attn_ref[...], full_ref[...].reshape(width, width))
    mixed[pl.ds(pl.multiple_of(r * size, size), size)] = x.astype(BF)

    @pl.when(r == pl.num_programs(0) - 1)
    def _():
        to_experts(ids_ref, mixed, out_ref)


def to_experts(ids_ref, rows, out_ref):
    total = rows.shape[0]
    for r in range(0, total, QB):
        want = lax.broadcasted_iota(jnp.int32, (QB, total), 0) + r
        out_ref[r : r + QB] = dot_nn(one_hot(want, ids_ref[...]), rows[...]).astype(BF)


def mix(meta, attn, seq, ids_row, pieces, full, deps=()):
    total, width = attn.shape
    block = pl.BlockSpec((QB, width), lambda r, *_: (r, 0))
    mat, out = run(
        partial(mix_kernel, len(pieces)),
        (attn, seq, ids_row, *[a for a, _ in pieces]),
        [shaped(full), shaped(attn.shape)],
        deps,
        (meta,),
        (total // QB,),
        [block, block, whole(ids_row.shape)] + piece_specs(pieces, full[2]),
        [whole(full), whole(attn.shape)],
        [pltpu.VMEM(attn.shape, BF)],
        micros=8,
    )
    return mat.reshape(width, width), out


def act_grad_kernel(cot_ref, wo_ref, out_ref):
    out_ref[...] = dot_nn(cot_ref[...], wo_ref[...]).astype(BF)


def act_grad(cot, w_out, deps=()):
    total, width = cot.shape
    hidden, tile = w_out.shape[1], 512
    return run(
        act_grad_kernel,
        (cot, w_out),
        [shaped((total, hidden))],
        deps,
        (),
        (hidden // tile,),
        [whole(cot.shape), pl.BlockSpec((width, tile), lambda f: (0, f))],
        [pl.BlockSpec((total, tile), lambda f: (0, f))],
        micros=11,
    )[0]


def expert_kernel(
    steps, x_ref, cot_ref, gain_ref, bias_ref, wi_ref, dact_ref, act_ref, dx_ref, sums_ref, ln, acc
):
    f = pl.program_id(0)
    total, width = ln.shape

    @pl.when(f == 0)
    def _():
        for r in range(0, total, QB):
            normed, _ = norm_rows(x_ref[r : r + QB].astype(F32))
            ln[r : r + QB] = (normed * gain_ref[...] + bias_ref[...]).astype(BF)

    def body(first):
        spans = [slice(r, r + QB) for r in range(0, total, QB)]
        pre = dot_nn(ln[spans[0]], wi_ref[...])
        for n, rows in enumerate(spans):
            act, slope = gelu_both(pre)
            if n + 1 < len(spans):
                pre = dot_nn(ln[spans[n + 1]], wi_ref[...])
            act_ref[rows] = act.astype(BF)
            back = (dact_ref[rows].astype(F32) * slope).astype(BF)
            if first:
                acc[rows] = dot_nt(back, wi_ref[...])
            else:
                acc[rows] += dot_nt(back, wi_ref[...])

    @pl.when(f == 0)
    def _():
        body(True)

    @pl.when(f > 0)
    def _():
        body(False)

    @pl.when(f == steps - 1)
    def _():
        gain_sum = jnp.zeros((1, width), F32)
        bias_sum = gain_sum
        for r in range(0, total, QB):
            rows = slice(r, r + QB)
            normed, inverse = norm_rows(x_ref[rows].astype(F32))
            d = acc[rows]
            gain_sum = gain_sum + jnp.sum(d * normed, 0, keepdims=True)
            bias_sum = bias_sum + jnp.sum(d, 0, keepdims=True)
            back = norm_back(d, normed, inverse, gain_ref[...])
            dx_ref[rows] = (cot_ref[rows].astype(F32) + back).astype(BF)
        sums_ref[0:1] = gain_sum
        sums_ref[1:2] = bias_sum


def expert(x, cot, gain, bias, w_in, dact, deps=()):
    total, width = x.shape
    hidden, tile = w_in.shape[1], 1024
    steps = hidden // tile
    cols = pl.BlockSpec((width, tile), lambda f: (0, f))
    rows = pl.BlockSpec((total, tile), lambda f: (0, f))
    return run(
        partial(expert_kernel, steps),
        (x, cot, gain, bias, w_in, dact),
        [shaped((total, hidden)), shaped(x.shape), shaped((8, width), F32)],
        deps,
        (),
        (steps,),
        [whole(x.shape)] * 2 + [whole((1, width))] * 2 + [cols, rows],
        [rows, whole(x.shape), whole((8, width))],
        [pltpu.VMEM(x.shape, BF), pltpu.VMEM(x.shape, F32)],
        micros=34,
    )


def expert_out_kernel(x_ref, act_ref, wo_ref, out_ref):
    out = x_ref[...].astype(F32) + dot_nt(act_ref[...], wo_ref[...])
    out_ref[...] = out.astype(BF)


def expert_out(x, act, w_out, deps=()):
    total, width = x.shape
    hidden, tile = w_out.shape[1], 256
    part = pl.BlockSpec((total, tile), lambda n: (0, n))
    return run(
        expert_out_kernel,
        (x, act, w_out),
        [shaped(x.shape)],
        deps,
        (),
        (width // tile,),
        [part, whole(act.shape), pl.BlockSpec((tile, hidden), lambda n: (n, 0))],
        [part],
        micros=12,
    )[0]


def turn_kernel(meta, wi_ref, wo_ref, wit_ref, wot_ref):
    wit_ref[...] = jnp.transpose(wi_ref[...])
    wot_ref[...] = jnp.transpose(wo_ref[...])


def turn_slices(meta, w_in, w_out, hidden):
    width, tile = w_in.shape[0], min(256, hidden)
    tiles = hidden // tile
    cols = pl.BlockSpec((width, tile), lambda f, m: (0, m[1] * tiles + f))
    rows = pl.BlockSpec((tile, width), lambda f, m: (f, 0))
    return run(
        turn_kernel,
        (w_in, w_out),
        [shaped((hidden, width))] * 2,
        (),
        (meta,),
        (tiles,),
        [cols] * 2,
        [rows] * 2,
        micros=5,
    )


def slice_kernel(t, groups, first, last, meta, *refs):
    valid = [meta[1] >= t, meta[1] + t < groups] if t else [meta[1] >= 0]
    count = len(valid)
    xs, cots = refs[:count], refs[count : 2 * count]
    gain_ref, bias_ref, wi_ref, wo_ref = refs[2 * count : 2 * count + 4]
    rest = refs[2 * count + 4 :]
    if not first:
        in_prev, out_prev = rest[:2]
        rest = rest[2:]
    in_ref, out_ref, in_acc, out_acc, lns, rows, sems = rest
    f = pl.program_id(0)
    total = lns.shape[1]

    def copies(n):
        return (
            pltpu.make_async_copy(xs[n], lns.at[n], sems.at[n, 0]),
            pltpu.make_async_copy(cots[n], rows.at[n], sems.at[n, 1]),
        )

    for n in range(count):

        @pl.when((f == 0) & valid[n])
        def _(n=n):
            for copy in copies(n):
                copy.start()

    if first:
        in_acc[...] = jnp.zeros_like(in_acc)
        out_acc[...] = jnp.zeros_like(out_acc)
    else:
        in_acc[...] = in_prev[...]
        out_acc[...] = out_prev[...]
    for n in range(count):

        @pl.when(valid[n])
        def _(n=n):
            @pl.when(f == 0)
            def _():
                for copy in copies(n):
                    copy.wait()
                for r in range(0, total, QB):
                    normed, _ = norm_rows(lns[n, r : r + QB].astype(F32))
                    lns[n, r : r + QB] = (normed * gain_ref[...] + bias_ref[...]).astype(BF)

            pre = dot_nt(wi_ref[...], lns[n])
            grad = dot_nt(wo_ref[...], rows[n])
            act, slope = gelu_both(pre)
            back = (grad * slope).astype(BF)
            in_acc[...] += dot_nn(back, lns[n])
            out_acc[...] += dot_nn(act.astype(BF), rows[n])

    if last:
        in_ref[...] = jnp.transpose(in_acc[...])
        out_ref[...] = jnp.transpose(out_acc[...])
    else:
        in_ref[...] = in_acc[...]
        out_ref[...] = out_acc[...]


def slice_grads(meta, t, groups, xs, cots, gain, bias, wi_turned, wo_turned, prev, deps=(), gates=()):
    count = len(xs)
    total, width = xs[0].shape
    hidden = wi_turned.shape[0]
    tile = min(256, hidden)
    rows = pl.BlockSpec((tile, width), lambda f, *_: (f, 0))
    cols = pl.BlockSpec((width, tile), lambda f, *_: (0, f))
    anywhere = pl.BlockSpec(memory_space=pl.ANY)
    first, last = prev is None, t == groups - 1
    return run(
        partial(slice_kernel, t, groups, first, last),
        (*xs, *cots, gain, bias, wi_turned, wo_turned, *(() if first else prev)),
        [shaped((width, hidden) if last else (hidden, width), F32)] * 2,
        deps,
        (meta,),
        (hidden // tile,),
        [anywhere] * (2 * count)
        + [whole((1, width))] * 2
        + [rows] * (2 if first else 4),
        [cols if last else rows] * 2,
        [pltpu.VMEM((tile, width), F32)] * 2
        + [pltpu.VMEM((count, total, width), BF)] * 2
        + [pltpu.SemaphoreType.DMA((count, 2))],
        micros=18,
        gates=gates,
    )


def back_kernel(ids_ref, mat_ref, rows_ref, dmix_ref, dattn_ref):
    lanes = lax.broadcasted_iota(jnp.int32, (QB, rows_ref.shape[0]), 1)
    x = dot_nn(one_hot(ids_ref[...], lanes), rows_ref[...]).astype(BF)
    dmix_ref[...] = x
    dattn_ref[...] = dot_nt(x, mat_ref[...]).astype(BF)


def back_in(ids_col, mat, rows, deps=()):
    total, width = rows.shape
    block = pl.BlockSpec((QB, width), lambda r: (r, 0))
    return run(
        back_kernel,
        (ids_col, mat, rows),
        [shaped(rows.shape)] * 2,
        deps,
        (),
        (total // QB,),
        [pl.BlockSpec((QB, 1), lambda r: (r, 0)), whole(mat.shape), whole(rows.shape)],
        [block] * 2,
        micros=7,
    )


def shared_kernel(turn, count, norm, left_ref, *refs):
    rights, refs = refs[:count], refs[count:]
    if norm:
        mats, (gains_ref, small_ref, out, tops) = refs[:count], refs[count:]
    else:
        (out,) = refs
    experts, step = out.shape[0], out.shape[2]
    left = jnp.transpose(left_ref[...]) if turn else left_ref[...]

    def put(values, cols):
        values = values.astype(BF)
        for e in range(experts):
            part = values[e * step : (e + 1) * step]
            out[e, 0, :, cols : cols + values.shape[1]] = part

    if norm:

        @pl.when(pl.program_id(0) == 0)
        def _():
            for n, right in enumerate(rights):
                tops[n : n + 1] = jnp.sum(right[...].astype(F32), 0, keepdims=True)

    cols, with_gain, with_bias = 0, 0.0, 0.0
    for n, right in enumerate(rights):
        sums = dot_nn(left, right[...])
        if norm:
            mat = mats[n][...].astype(F32)
            with_gain = with_gain + jnp.sum(mat * sums, -1, keepdims=True)
            with_bias = with_bias + jnp.sum(mat * tops[n : n + 1], -1, keepdims=True)
        put(sums, cols)
        cols += right.shape[1]
    if norm:
        with_gain = (with_gain - gains_ref[:, 1:2] * with_bias) / gains_ref[:, 0:1]
        rest = jnp.zeros((sums.shape[0], 120), F32)
        extra = jnp.concatenate([jnp.transpose(small_ref[...]), rest], -1)
        lane = lax.broadcasted_iota(jnp.int32, (1, 128), 1)
        extra = jnp.where(lane == 8, with_gain, jnp.where(lane == 9, with_bias, extra))
        put(extra, cols)


def shared_grads(left, turned, rights, experts, groups, norm=(), deps=(), gates=()):
    total = rights[0].shape[0]
    features = left.shape[0 if turned else 1]
    step, block = features // (experts * groups), features // groups
    width = sum(r.shape[1] for r in rights) + (128 if norm else 0)
    rows = pl.BlockSpec((block, total), lambda g: (g, 0))
    specs = [rows if turned else pl.BlockSpec((total, block), lambda g: (0, g))]
    specs += [whole(r.shape) for r in rights]
    args, scratch = [left, *rights], []
    if norm:
        mats, gains, small = norm
        args += [*mats, gains, small]
        specs += [pl.BlockSpec((block, m.shape[1]), lambda g: (g, 0)) for m in mats]
        specs += [pl.BlockSpec((block, 16), lambda g: (g, 0))]
        specs += [pl.BlockSpec((8, block), lambda g: (0, g))]
        scratch = [pltpu.VMEM((8, rights[0].shape[1]), F32)]
    shape = (experts, groups, step, width)
    return run(
        partial(shared_kernel, not turned, len(rights), bool(norm)),
        args,
        [shaped(shape)],
        deps,
        (),
        (groups,),
        specs,
        [pl.BlockSpec((experts, 1, step, width), lambda g: (0, g, 0, 0))],
        scratch,
        micros=4 * len(rights),
        gates=gates,
    )


def total_kernel(meta, first_ref, second_ref, *outs):
    groups = len(outs)
    g = pl.program_id(0)
    for s in range(groups):

        @pl.when(g == lax.rem(meta[1] + s, groups))
        def _(out=outs[s]):
            col = 0
            for ref in (first_ref, second_ref):
                total = ref[0, 0].astype(F32)
                for e in range(1, ref.shape[0]):
                    total = total + ref[e, 0].astype(F32)
                out[:, col : col + total.shape[1]] = total.astype(out.dtype)
                col += total.shape[1]


def total_over(meta, first, second, deps=(), gates=()):
    groups, step = first.shape[1:3]
    width = first.shape[3] + second.shape[3]
    specs = []
    for a in (first, second):
        block = (a.shape[0], 1, *a.shape[2:])
        specs.append(pl.BlockSpec(block, lambda g, *_: (0, g, 0, 0)))
    return run(
        total_kernel,
        (first, second),
        [shaped((step, width), F32)] + [shaped((step, width))] * (groups - 1),
        deps,
        (meta,),
        (groups,),
        specs,
        [whole((step, width))] * groups,
        micros=5,
        gates=gates,
    )


def final_kernel(*refs):
    ins, (o_ref, q_ref, k_ref, v_ref, *small) = refs[:-8], refs[-8:]
    total = ins[0][...]
    for ref in ins[1:]:
        total = total + ref[...].astype(F32)
    width = o_ref.shape[1]
    for n, ref in enumerate((o_ref, q_ref, k_ref, v_ref)):
        ref[...] = total[:, n * width : (n + 1) * width]
    turned = jnp.transpose(total[:, 4 * width :])
    for n, ref in zip((8, 9, 0, 1), small):
        ref[...] = turned[n : n + 1]


def final(parts, width):
    step = parts[0].shape[0]
    return run(
        final_kernel,
        parts,
        [shaped((step, width), F32)] * 4 + [shaped((1, step), F32)] * 4,
        micros=2,
    )


def first_kernel(*refs):
    grads, mats = refs[:3], refs[3:6]
    seq_ref, dmix_ref, gain_ref, ids_ref, out_ref, rows = refs[6:]
    r = pl.program_id(0)
    size = seq_ref.shape[0]
    grad = dot_nt(grads[0][...], mats[0][...])
    for n in (1, 2):
        grad = grad + dot_nt(grads[n][...], mats[n][...])
    normed, inverse = norm_rows(seq_ref[...].astype(F32))
    back = dmix_ref[...].astype(F32) + norm_back(grad, normed, inverse, gain_ref[...])
    rows[pl.ds(pl.multiple_of(r * size, size), size)] = back.astype(BF)

    @pl.when(r == pl.num_programs(0) - 1)
    def _():
        to_experts(ids_ref, rows, out_ref)


def first_back(grads, mats, seq, dmix, gain, ids_row, deps=()):
    total, width = seq.shape
    block = pl.BlockSpec((QB, width), lambda r: (r, 0))
    return run(
        first_kernel,
        (*grads, *mats, seq, dmix, gain, ids_row),
        [shaped((total, width))],
        deps,
        (),
        (total // QB,),
        [block] * 3
        + [whole((width, width))] * 3
        + [block] * 2
        + [whole((1, width)), whole((1, total))],
        [whole((total, width))],
        [pltpu.VMEM((total, width), BF)],
        micros=1,
    )[0]


def local(
    n_grp,
    n_exp,
    tokens,
    cotangent,
    arrival,
    seq_length,
    w_q,
    w_k,
    w_v,
    w_o,
    ln1_gain,
    ln1_bias,
    ln2_gain,
    ln2_bias,
    w_in,
    w_out,
):
    me, grp = lax.axis_index("exp"), lax.axis_index("grp")
    meta = jnp.stack([me, grp]).astype(jnp.int32)
    width = tokens.shape[1]
    step = w_q.shape[0]
    hidden = w_in.shape[2] // n_grp
    both = ("grp", "exp")

    def swap(a, k):
        return lax.ppermute(a, "exp", [(i, i ^ k) for i in range(n_exp)])

    def shift(a, k):
        return lax.ppermute(a, "grp", [(i, (i + k) % n_grp) for i in range(n_grp)])

    def exchange(rows):
        return lax.all_to_all(rows, "exp", split_axis=0, concat_axis=0, tiled=True)

    bits = []
    while 2 ** len(bits) < n_exp:
        bits.append(2 ** len(bits))
    orders = [bits[:0:-1] + bits[:1], bits[1:] + bits[:1]]

    def gather_pair(own, cut):
        first = lambda a: a[0] if isinstance(a, tuple) else a[:, :cut]
        second = lambda a: a[1] if isinstance(a, tuple) else a[:, cut:]
        have = {0: own}
        for r in sorted(range(1, n_exp), key=lambda r: (bin(r).count("1"), -r)):
            b, c = (max((b for b in bits if r & b), key=order.index) for order in orders)
            if b == c and not isinstance(have[r ^ b], tuple):
                have[r] = swap(have[r ^ b], b)
            else:
                have[r] = (swap(first(have[r ^ b]), b), swap(second(have[r ^ c]), c))
        return [have[r] for r in range(n_exp)]

    def line_step(t, up, down):
        up = lax.ppermute(up, "grp", [(i, i + 1) for i in range(t - 1, n_grp - 1)])
        down = lax.ppermute(down, "grp", [(i + 1, i) for i in range(n_grp - t)])
        return up, down

    def line(a):
        steps = [(a, a)]
        for t in range(1, n_grp):
            steps.append(line_step(t, *steps[-1]))
        return steps

    ids_row = arrival
    ids_col = arrival.reshape(-1, 1)
    flag = seq_length

    gains = jnp.stack([ln1_gain, ln1_bias, ln2_gain, ln2_bias])
    mine = jnp.zeros((16, width), BF)
    mine = lax.dynamic_update_slice(mine, gains, (0, (grp * n_exp + me) * step))
    mine = jnp.concatenate([w_q, w_k, mine, w_v, w_o])
    mine = [mine] + [shift(mine, k) for k in range(1, n_grp)]
    arrived = exchange(tokens)
    w_first, w_second = w_in[0], w_out[0]
    wi_turned, wo_turned = turn_slices(meta, w_first, w_second, hidden)
    dact = act_grad(cotangent, w_second)
    pair_qk, pair_vo = stack(mine, (2 * step + 16, 2 * step), deps=(arrived, dact, wi_turned))
    pieces = gather_pair(pair_qk, step)
    all_vo = lax.all_gather(pair_vo, "exp", axis=0)

    full = (n_grp, n_exp, step, width)
    is_cut = lambda a: isinstance(a, tuple)
    pieces_q = [(a[0], 0) if is_cut(a) else (a, 0) for a in pieces]
    pieces_k = [(a[1], 0) if is_cut(a) else (a, 1) for a in pieces]
    pieces_g = [
        (a[1], step // 16) if is_cut(a) else (a, 2 * step // 16) for a in pieces
    ]
    pieces_v, pieces_o = [(all_vo, 0)], [(all_vo, 1)]

    cot_line, x_line = [(cotangent,) * 2], []

    def forward(steps, gated=None):
        if len(steps) < n_grp:
            steps.append(line_step(len(steps), *(gated or steps[-1])))
        return steps[-1]

    forward(cot_line)
    seq, ln_one, ln_turned, q, k, mat_q, mat_k, gains = enter(
        meta, ids_col, arrived, pieces_q, pieces_k, pieces_g, full
    )
    v, mat_v, cot_line[1] = project(meta, ln_one, pieces_v, full, gates=cot_line[1])
    forward(cot_line)
    attn, lse = attend(flag, q, k, v)
    mat_o, leaving = mix(meta, attn, seq, ids_row, pieces_o, full)
    x = exchange(leaving)

    act, dx, sums_two = expert(
        x, cotangent, gains[2], gains[3], w_first, dact, deps=cot_line[-1]
    )
    x_line = [(x,) * 2]
    forward(x_line)
    output = expert_out(x, act, w_second)

    def slices(t, sums, deps=(), gates=()):
        xs, cots = (list(line[t])[: 2 if t else 1] for line in (x_line, cot_line))
        last = (gains[2], gains[3], wi_turned, wo_turned, sums, deps, gates)
        return slice_grads(meta, t, n_grp, xs, cots, *last)

    slice_sums, x_line[1] = slices(0, None, deps=output, gates=x_line[1])
    back = exchange(dx)
    dmix, dattn = back_in(ids_col, mat_o, back, deps=slice_sums)
    forward(x_line)

    (first,), cot_line[-1] = shared_grads(
        attn, False, [dmix], n_exp, n_grp, gates=cot_line[-1]
    )
    while len(cot_line) < n_grp:
        forward(cot_line)
    grads = attend_back(flag, q, k, v, attn, dattn, lse, 0, 1, deps=first)
    first = exchange(first)
    (second,), x_line[-1] = shared_grads(
        ln_turned,
        True,
        grads,
        n_exp,
        n_grp,
        ((mat_q, mat_k, mat_v), gains[4], sums_two),
        gates=x_line[-1],
    )
    while len(x_line) < n_grp:
        forward(x_line)
    dfirst = first_back(
        grads, (mat_q, mat_k, mat_v), seq, dmix, gains[0], ids_row, deps=(first, second)
    )
    second = exchange(second)
    for t in range(1, n_grp):
        deps = (dfirst, cot_line[-1]) if t == 1 else ()
        if t == n_grp - 1:
            deps = (deps, slice_sums)
            parts, (dfirst,) = total_over(meta, first, second, deps, dfirst)
            deps = parts
            parts = [parts[0]] + [shift(a, n + 1) for n, a in enumerate(parts[1:])]
        slice_sums = slices(t, slice_sums, deps)
    grad_x = exchange(dfirst)
    grad_w_in, grad_w_out = slice_sums
    grad_w_o, *grads = final(parts, width)
    grads, small = grads[:3], [a[0] for a in grads[3:]]

    return (
        output,
        grad_x,
        *grads,
        grad_w_o,
        *small,
        grad_w_in[None],
        grad_w_out[None],
    )


def solution(mesh):
    both = ("grp", "exp")
    rows, flat, mats = P(both, None), P(both), P("exp", None, None)
    split = P("exp", None, "grp")
    return jax.shard_map(
        partial(local, mesh.shape["grp"], mesh.shape["exp"]),
        mesh=mesh,
        in_specs=(rows, rows, rows, flat) + (rows,) * 4 + (flat,) * 4 + (mats, mats),
        out_specs=(rows,) * 6 + (flat,) * 4 + (split, split),
        check_vma=False,
    )
```

```python
from functools import partial

import jax
import jax.numpy as jnp
from jax import lax
from jax.experimental import pallas as pl
from jax.experimental.pallas import tpu as pltpu
from jax.sharding import PartitionSpec as P

HDIM = 64
QB = 256
EPSILON = 1e-05
NEG_FILL = -1e30
GELU_A = 0.7978845608028654
GELU_B = 0.044715
BF = jnp.bfloat16
F32 = jnp.float32
MIB = 1024 * 1024


def dot_nn(left, right):
    return lax.dot_general(left, right, (((1,), (0,)), ((), ())), preferred_element_type=F32)


def dot_nt(left, right):
    return lax.dot_general(left, right, (((1,), (1,)), ((), ())), preferred_element_type=F32)


def norm_rows(x):
    centred = x - jnp.mean(x, -1, keepdims=True)
    inverse = lax.rsqrt(jnp.mean(centred * centred, -1, keepdims=True) + EPSILON)
    return centred * inverse, inverse


def norm_back(grad, normed, inverse, gain):
    scaled = grad * gain
    return inverse * (
        scaled
        - jnp.mean(scaled, -1, keepdims=True)
        - normed * jnp.mean(scaled * normed, -1, keepdims=True)
    )


def gelu_both(u):
    sq = u * u
    half = 0.5 + 0.5 * jnp.tanh(u * (GELU_A + (GELU_A * GELU_B) * sq))
    act = u * half
    return act, half + act * (1.0 - half) * (2.0 * GELU_A + (6.0 * GELU_A * GELU_B) * sq)


def run(
    kernel,
    args,
    out_shape,
    deps=(),
    scalars=(),
    grid=(1,),
    specs=None,
    outs=None,
    scratch=(),
    micros=5,
    gates=(),
):
    specs = [whole(a.shape) for a in args] if specs is None else specs
    outs = [whole(o.shape) for o in out_shape] if outs is None else outs
    gates, deps = jax.tree.leaves(gates), jax.tree.leaves(deps)
    first, count, results = len(scalars) + len(args), len(deps) + len(gates), len(out_shape)

    def body(*refs):
        last = first + count + results
        kernel(*refs[:first], *refs[first + count : last], *refs[last + len(gates) :])

    anywhere = pl.BlockSpec(memory_space=pl.ANY)
    res = pl.pallas_call(
        body,
        grid_spec=pltpu.PrefetchScalarGridSpec(
            num_scalar_prefetch=len(scalars),
            grid=grid,
            in_specs=list(specs) + [anywhere] * count,
            out_specs=list(outs) + [anywhere] * len(gates),
            scratch_shapes=list(scratch),
        ),
        out_shape=list(out_shape) + [shaped(g.shape, g.dtype) for g in gates],
        input_output_aliases={first + len(deps) + n: results + n for n in range(len(gates))},
        compiler_params=pltpu.CompilerParams(vmem_limit_bytes=60 * MIB),
        cost_estimate=pl.CostEstimate(
            flops=int(micros * 0.517e9), bytes_accessed=10**6, transcendentals=0
        ),
    )(*scalars, *args, *deps, *gates)
    return (list(res[:results]), list(res[results:])) if gates else res


def shaped(shape, dtype=BF):
    return jax.ShapeDtypeStruct(tuple(shape), dtype)


def whole(shape):
    return pl.BlockSpec(shape, lambda *_: (0,) * len(shape), pipeline_mode=pl.Buffered(1))


def one_hot(ids, other):
    return jnp.where(ids == other, 1.0, 0.0).astype(BF)


def enter_kernel(count, meta, ids_ref, rows_ref, *refs):
    pieces, refs = [refs[n * count : (n + 1) * count] for n in range(3)], refs[3 * count :]
    seq_ref, ln_ref, lnt_ref, q_ref, k_ref, mat_q, mat_k, *gain_refs = refs
    width = rows_ref.shape[1]

    @pl.when(pl.program_id(0) == 0)
    def _():
        place(meta, pieces[0], mat_q)
        place(meta, pieces[1], mat_k)
        gains = 0.0
        for piece in pieces[2]:
            for z in range(piece.shape[0]):
                gains = gains + piece[z].astype(F32)
        for n, ref in enumerate(gain_refs[:-1]):
            ref[...] = gains[n : n + 1]
        gain_refs[-1][...] = jnp.transpose(gains)

    lanes = lax.broadcasted_iota(jnp.int32, (QB, rows_ref.shape[0]), 1)
    x = dot_nn(one_hot(ids_ref[...], lanes), rows_ref[...])
    seq_ref[...] = x.astype(BF)
    normed, _ = norm_rows(x)
    ln = (normed * gain_refs[0][...] + gain_refs[1][...]).astype(BF)
    ln_ref[...] = ln
    lnt_ref[...] = jnp.transpose(ln)
    q_ref[...] = dot_nn(ln, mat_q[...].reshape(width, width)).astype(BF)
    k_ref[...] = dot_nn(ln, mat_k[...].reshape(width, width)).astype(BF)


def enter(meta, ids_col, rows, pieces_q, pieces_k, pieces_g, full, deps=()):
    total, width = rows.shape
    block = pl.BlockSpec((QB, width), lambda r, *_: (r, 0))
    turned = pl.BlockSpec((width, QB), lambda r, *_: (0, r))
    rows_out, gain = shaped((total, width)), shaped((1, width), F32)
    seq, ln, lnt, q, k, mat_q, mat_k, *gains = run(
        partial(enter_kernel, len(pieces_q)),
        (ids_col, rows, *[a for a, _ in (*pieces_q, *pieces_k, *pieces_g)]),
        [rows_out, rows_out, shaped((width, total)), rows_out, rows_out]
        + [shaped(full)] * 2
        + [gain] * 4
        + [shaped((width, 16), F32)],
        deps,
        (meta,),
        (total // QB,),
        [pl.BlockSpec((QB, 1), lambda r, *_: (r, 0)), whole(rows.shape)]
        + piece_specs(pieces_q, full[2])
        + piece_specs(pieces_k, full[2])
        + piece_specs(pieces_g, 16),
        [block, block, turned, block, block]
        + [whole(full)] * 2
        + [whole((1, width))] * 4
        + [whole((width, 16))],
        micros=14,
    )
    flat = (width, width)
    return seq, ln, lnt, q, k, mat_q.reshape(flat), mat_k.reshape(flat), gains


def place(meta, refs, full):
    groups, experts = full.shape[0], full.shape[1]
    for r in range(experts):
        for z in range(groups):
            row = lax.rem(meta[1] + (groups - z), groups)
            if len(refs) == 1:
                full[row, r] = refs[0][r, z]
            else:
                full[row, r ^ meta[0]] = refs[r][z]


def piece_specs(pieces, step):
    specs = []
    for array, n in pieces:
        shape = (*array.shape[:-2], step, array.shape[-1])
        at = (0,) * (len(shape) - 2) + (n, 0)
        specs.append(pl.BlockSpec(shape, lambda *_, at=at: at, pipeline_mode=pl.Buffered(1)))
    return specs


def stack_kernel(groups, *refs):
    ins, outs = refs[:groups], refs[groups:]
    for z in range(groups):
        row = 0
        for out in outs:
            out[z] = ins[z][row : row + out.shape[1]]
            row += out.shape[1]


def stack(blocks, rows, deps=()):
    width = blocks[0].shape[1]
    return run(
        partial(stack_kernel, len(blocks)),
        blocks,
        [shaped((len(blocks), r, width)) for r in rows],
        deps,
        micros=2,
    )


def proj_kernel(count, meta, ln_ref, *refs):
    pieces, (out_ref, full_ref) = refs[:count], refs[count:]

    @pl.when(pl.program_id(0) == 0)
    def _():
        place(meta, pieces, full_ref)

    width = ln_ref.shape[1]
    out_ref[...] = dot_nn(ln_ref[...], full_ref[...].reshape(width, width)).astype(BF)


def project(meta, ln, pieces, full, deps=(), gates=()):
    total, width = ln.shape
    block = pl.BlockSpec((QB, width), lambda r, *_: (r, 0))
    (out, mat), gates = run(
        partial(proj_kernel, len(pieces)),
        (ln, *[a for a, _ in pieces]),
        [shaped(ln.shape), shaped(full)],
        deps,
        (meta,),
        (total // QB,),
        [block] + piece_specs(pieces, full[2]),
        [block, whole(full)],
        gates=gates,
    )
    return out, mat.reshape(width, width), gates


def head_lanes(heads):
    pair = 2 * HDIM
    low = lax.broadcasted_iota(jnp.int32, (1, pair), 1) < HDIM
    cols = [slice(h // 2 * pair, (h // 2 + 1) * pair) for h in range(heads)]
    return low, cols, [~low if h % 2 else low for h in range(heads)]


def attend_kernel(flag, q_ref, k_ref, v_ref, o_ref, lse_ref, lse_cols):
    total, heads = q_ref.shape[0], q_ref.shape[1] // HDIM
    low, cols, own = head_lanes(heads)
    each = range(heads)
    causal = lax.broadcasted_iota(jnp.int32, (QB, QB), 1) <= lax.broadcasted_iota(
        jnp.int32, (QB, QB), 0
    )

    def go(long):
        for a in range(0, total, QB):
            b = a + QB
            further = long and a > 0
            q = [
                jnp.where(own[h], q_ref[a:b, cols[h]], jnp.zeros((QB, 2 * HDIM), BF))
                * BF(HDIM**-0.5)
                for h in each
            ]
            near = [jnp.where(causal, dot_nt(q[h], k_ref[a:b, cols[h]]), NEG_FILL) for h in each]
            top = [jnp.max(near[h], 1, keepdims=True) for h in each]
            if further:
                far = [dot_nt(q[h], k_ref[0:a, cols[h]]) for h in each]
                top = [jnp.maximum(top[h], jnp.max(far[h], 1, keepdims=True)) for h in each]
            near = [jnp.exp(near[h] - top[h]) for h in each]
            mass = [jnp.sum(near[h], 1, keepdims=True) for h in each]
            o = [dot_nn(near[h].astype(BF), v_ref[a:b, cols[h]]) for h in each]
            if further:
                far = [jnp.exp(far[h] - top[h]) for h in each]
                mass = [mass[h] + jnp.sum(far[h], 1, keepdims=True) for h in each]
                o = [o[h] + dot_nn(far[h].astype(BF), v_ref[0:a, cols[h]]) for h in each]
            o = [o[h] * (1.0 / mass[h]) for h in each]
            logs = [top[h] + jnp.log(mass[h]) for h in each]
            for h in range(0, heads, 2):
                o_ref[a:b, cols[h]] = jnp.where(low, o[h], o[h + 1]).astype(BF)
                lse_cols[a:b, cols[h]] = jnp.where(low, logs[h], logs[h + 1])

    @pl.when(flag[0] > QB)
    def _():
        go(True)

    @pl.when(flag[0] <= QB)
    def _():
        go(False)

    for h in range(0, heads, 2):
        turned = jnp.transpose(lse_cols[:, cols[h]])
        lse_ref[h // 2, 0:1] = turned[0:1]
        lse_ref[h // 2, 1:2] = turned[HDIM : HDIM + 1]


def attend(flag, q, k, v, deps=()):
    total, width = q.shape
    lanes = 4 * HDIM
    block = pl.BlockSpec((total, lanes), lambda j, *_: (0, j))
    stat = pl.BlockSpec((2, 8, total), lambda j, *_: (j, 0, 0))
    return run(
        attend_kernel,
        (q, k, v),
        [shaped((total, width)), shaped((width // (2 * HDIM), 8, total), F32)],
        deps,
        (flag,),
        (width // lanes,),
        [block] * 3,
        [block, stat],
        [pltpu.VMEM((total, lanes), F32)],
        micros=22,
    )


def attend_back_kernel(
    flag, q_ref, k_ref, v_ref, o_ref, g_ref, lse_ref, dq_ref, dk_ref, dv_ref, dq_turned
):
    total, heads = q_ref.shape[0], q_ref.shape[1] // HDIM
    low, cols, own = head_lanes(heads)
    each = range(heads)
    causal = lax.broadcasted_iota(jnp.int32, (QB, QB), 0) <= lax.broadcasted_iota(
        jnp.int32, (QB, QB), 1
    )
    delta, k_turned = [], []
    for h in range(0, heads, 2):
        prod = jnp.transpose(g_ref[:, cols[h]].astype(F32) * o_ref[:, cols[h]].astype(F32))
        delta.append(jnp.sum(prod[:HDIM], 0, keepdims=True))
        delta.append(jnp.sum(prod[HDIM:], 0, keepdims=True))
        turned = jnp.transpose(k_ref[:, cols[h]])
        k_turned += [turned[:HDIM], turned[HDIM:]]

    def go(long):
        for a in range(0, total, QB):
            b = a + QB
            zero = jnp.zeros((QB, 2 * HDIM), BF)
            k = [jnp.where(own[h], k_ref[a:b, cols[h]], zero) * BF(HDIM**-0.5) for h in each]
            v = [jnp.where(own[h], v_ref[a:b, cols[h]], zero) for h in each]
            dk, dv = [0.0] * heads, [0.0] * heads
            spans = [(a, b)]
            if long and b < total:
                spans.append((b, total))
            for lo, hi in spans:
                scores = [dot_nt(k[h], q_ref[lo:hi, cols[h]]) for h in each]
                dp = [dot_nt(v[h], g_ref[lo:hi, cols[h]]) for h in each]
                probs = [
                    jnp.exp(scores[h] - lse_ref[h // 2, h % 2 : h % 2 + 1, lo:hi]) for h in each
                ]
                if lo == a:
                    probs = [jnp.where(causal, p, 0.0) for p in probs]
                ds = [(probs[h] * (dp[h] - delta[h][:, lo:hi])).astype(BF) for h in each]
                probs = [p.astype(BF) for p in probs]
                for h in each:
                    dv[h] = dv[h] + dot_nn(probs[h], g_ref[lo:hi, cols[h]])
                    dk[h] = dk[h] + dot_nn(ds[h], q_ref[lo:hi, cols[h]])
                    rows = slice(h * HDIM, (h + 1) * HDIM)
                    if a == 0 or not long:
                        dq_turned[rows, lo:hi] = dot_nn(k_turned[h][:, a:b], ds[h])
                    else:
                        dq_turned[rows, lo:hi] += dot_nn(k_turned[h][:, a:b], ds[h])
            for h in range(0, heads, 2):
                both = jnp.where(low, dk[h], dk[h + 1])
                dk_ref[a:b, cols[h]] = (both * HDIM**-0.5).astype(BF)
                dv_ref[a:b, cols[h]] = jnp.where(low, dv[h], dv[h + 1]).astype(BF)

    @pl.when(flag[0] > QB)
    def _():
        go(True)

    @pl.when(flag[0] <= QB)
    def _():
        go(False)

    dq_ref[...] = (jnp.transpose(dq_turned[...]) * HDIM**-0.5).astype(BF)


def attend_back(flag, q, k, v, o, g, lse, part, parts, deps=(), gates=()):
    total, width = q.shape
    lanes = 4 * HDIM
    count = width // lanes // parts
    first = part * count
    block = pl.BlockSpec((total, lanes), lambda j, *_: (0, j + first))
    stat = pl.BlockSpec((2, 8, total), lambda j, *_: (j + first, 0, 0))
    done = pl.BlockSpec((total, lanes), lambda j, *_: (0, j))
    return run(
        attend_back_kernel,
        (q, k, v, o, g, lse),
        [shaped((total, width // parts))] * 3,
        deps,
        (flag,),
        (count,),
        [block] * 5 + [stat],
        [done] * 3,
        [pltpu.VMEM((lanes, total), F32)],
        micros=18,
        gates=gates,
    )


def mix_kernel(count, meta, attn_ref, seq_ref, ids_ref, *refs):
    pieces, (full_ref, out_ref, mixed) = refs[:count], refs[count:]
    r = pl.program_id(0)

    @pl.when(r == 0)
    def _():
        place(meta, pieces, full_ref)

    size, width = attn_ref.shape
    x = seq_ref[...].astype(F32) + dot_nn(attn_ref[...], full_ref[...].reshape(width, width))
    mixed[pl.ds(pl.multiple_of(r * size, size), size)] = x.astype(BF)

    @pl.when(r == pl.num_programs(0) - 1)
    def _():
        to_experts(ids_ref, mixed, out_ref)


def to_experts(ids_ref, rows, out_ref):
    total = rows.shape[0]
    for r in range(0, total, QB):
        want = lax.broadcasted_iota(jnp.int32, (QB, total), 0) + r
        out_ref[r : r + QB] = dot_nn(one_hot(want, ids_ref[...]), rows[...]).astype(BF)


def mix(meta, attn, seq, ids_row, pieces, full, deps=()):
    total, width = attn.shape
    block = pl.BlockSpec((QB, width), lambda r, *_: (r, 0))
    mat, out = run(
        partial(mix_kernel, len(pieces)),
        (attn, seq, ids_row, *[a for a, _ in pieces]),
        [shaped(full), shaped(attn.shape)],
        deps,
        (meta,),
        (total // QB,),
        [block, block, whole(ids_row.shape)] + piece_specs(pieces, full[2]),
        [whole(full), whole(attn.shape)],
        [pltpu.VMEM(attn.shape, BF)],
        micros=8,
    )
    return mat.reshape(width, width), out


def act_grad_kernel(cot_ref, wo_ref, out_ref):
    out_ref[...] = dot_nn(cot_ref[...], wo_ref[...]).astype(BF)


def act_grad(cot, w_out, deps=()):
    total, width = cot.shape
    hidden, tile = w_out.shape[1], 512
    return run(
        act_grad_kernel,
        (cot, w_out),
        [shaped((total, hidden))],
        deps,
        (),
        (hidden // tile,),
        [whole(cot.shape), pl.BlockSpec((width, tile), lambda f: (0, f))],
        [pl.BlockSpec((total, tile), lambda f: (0, f))],
        micros=11,
    )[0]


def expert_kernel(
    steps, x_ref, cot_ref, gain_ref, bias_ref, wi_ref, dact_ref, act_ref, dx_ref, sums_ref, ln, acc
):
    f = pl.program_id(0)
    total, width = ln.shape

    @pl.when(f == 0)
    def _():
        for r in range(0, total, QB):
            normed, _ = norm_rows(x_ref[r : r + QB].astype(F32))
            ln[r : r + QB] = (normed * gain_ref[...] + bias_ref[...]).astype(BF)

    def body(first):
        spans = [slice(r, r + QB) for r in range(0, total, QB)]
        pre = dot_nn(ln[spans[0]], wi_ref[...])
        for n, rows in enumerate(spans):
            act, slope = gelu_both(pre)
            if n + 1 < len(spans):
                pre = dot_nn(ln[spans[n + 1]], wi_ref[...])
            act_ref[rows] = act.astype(BF)
            back = (dact_ref[rows].astype(F32) * slope).astype(BF)
            if first:
                acc[rows] = dot_nt(back, wi_ref[...])
            else:
                acc[rows] += dot_nt(back, wi_ref[...])

    @pl.when(f == 0)
    def _():
        body(True)

    @pl.when(f > 0)
    def _():
        body(False)

    @pl.when(f == steps - 1)
    def _():
        gain_sum = jnp.zeros((1, width), F32)
        bias_sum = gain_sum
        for r in range(0, total, QB):
            rows = slice(r, r + QB)
            normed, inverse = norm_rows(x_ref[rows].astype(F32))
            d = acc[rows]
            gain_sum = gain_sum + jnp.sum(d * normed, 0, keepdims=True)
            bias_sum = bias_sum + jnp.sum(d, 0, keepdims=True)
            back = norm_back(d, normed, inverse, gain_ref[...])
            dx_ref[rows] = (cot_ref[rows].astype(F32) + back).astype(BF)
        sums_ref[0:1] = gain_sum
        sums_ref[1:2] = bias_sum


def expert(x, cot, gain, bias, w_in, dact, deps=()):
    total, width = x.shape
    hidden, tile = w_in.shape[1], 1024
    steps = hidden // tile
    cols = pl.BlockSpec((width, tile), lambda f: (0, f))
    rows = pl.BlockSpec((total, tile), lambda f: (0, f))
    return run(
        partial(expert_kernel, steps),
        (x, cot, gain, bias, w_in, dact),
        [shaped((total, hidden)), shaped(x.shape), shaped((8, width), F32)],
        deps,
        (),
        (steps,),
        [whole(x.shape)] * 2 + [whole((1, width))] * 2 + [cols, rows],
        [rows, whole(x.shape), whole((8, width))],
        [pltpu.VMEM(x.shape, BF), pltpu.VMEM(x.shape, F32)],
        micros=34,
    )


def expert_out_kernel(x_ref, act_ref, wo_ref, out_ref):
    out = x_ref[...].astype(F32) + dot_nt(act_ref[...], wo_ref[...])
    out_ref[...] = out.astype(BF)


def expert_out(x, act, w_out, deps=()):
    total, width = x.shape
    hidden, tile = w_out.shape[1], 256
    part = pl.BlockSpec((total, tile), lambda n: (0, n))
    return run(
        expert_out_kernel,
        (x, act, w_out),
        [shaped(x.shape)],
        deps,
        (),
        (width // tile,),
        [part, whole(act.shape), pl.BlockSpec((tile, hidden), lambda n: (n, 0))],
        [part],
        micros=12,
    )[0]


def turn_kernel(meta, wi_ref, wo_ref, wit_ref, wot_ref):
    wit_ref[...] = jnp.transpose(wi_ref[...])
    wot_ref[...] = jnp.transpose(wo_ref[...])


def turn_slices(meta, w_in, w_out, hidden):
    width, tile = w_in.shape[0], min(256, hidden)
    tiles = hidden // tile
    cols = pl.BlockSpec((width, tile), lambda f, m: (0, m[1] * tiles + f))
    rows = pl.BlockSpec((tile, width), lambda f, m: (f, 0))
    return run(
        turn_kernel,
        (w_in, w_out),
        [shaped((hidden, width))] * 2,
        (),
        (meta,),
        (tiles,),
        [cols] * 2,
        [rows] * 2,
        micros=5,
    )


def slice_kernel(t, groups, first, last, meta, *refs):
    valid = [meta[1] >= t, meta[1] + t < groups] if t else [meta[1] >= 0]
    count = len(valid)
    xs, cots = refs[:count], refs[count : 2 * count]
    froms = [lax.max(meta[1] - t, 0), lax.min(meta[1] + t, groups - 1)]
    cots = [c.at[f] if t > 1 else c for c, f in zip(cots, froms)]
    gain_ref, bias_ref, wi_ref, wo_ref = refs[2 * count : 2 * count + 4]
    rest = refs[2 * count + 4 :]
    if not first:
        in_prev, out_prev = rest[:2]
        rest = rest[2:]
    in_ref, out_ref, in_acc, out_acc, lns, rows, sems = rest
    f = pl.program_id(0)
    total = lns.shape[1]

    def copies(n):
        return (
            pltpu.make_async_copy(xs[n], lns.at[n], sems.at[n, 0]),
            pltpu.make_async_copy(cots[n], rows.at[n], sems.at[n, 1]),
        )

    for n in range(count):

        @pl.when((f == 0) & valid[n])
        def _(n=n):
            for copy in copies(n):
                copy.start()

    if first:
        in_acc[...] = jnp.zeros_like(in_acc)
        out_acc[...] = jnp.zeros_like(out_acc)
    else:
        in_acc[...] = in_prev[...]
        out_acc[...] = out_prev[...]
    for n in range(count):

        @pl.when(valid[n])
        def _(n=n):
            @pl.when(f == 0)
            def _():
                for copy in copies(n):
                    copy.wait()
                for r in range(0, total, QB):
                    normed, _ = norm_rows(lns[n, r : r + QB].astype(F32))
                    lns[n, r : r + QB] = (normed * gain_ref[...] + bias_ref[...]).astype(BF)

            pre = dot_nt(wi_ref[...], lns[n])
            grad = dot_nt(wo_ref[...], rows[n])
            act, slope = gelu_both(pre)
            back = (grad * slope).astype(BF)
            in_acc[...] += dot_nn(back, lns[n])
            out_acc[...] += dot_nn(act.astype(BF), rows[n])

    if last:
        in_ref[...] = jnp.transpose(in_acc[...])
        out_ref[...] = jnp.transpose(out_acc[...])
    else:
        in_ref[...] = in_acc[...]
        out_ref[...] = out_acc[...]


def slice_grads(meta, t, groups, xs, cots, gain, bias, wi_turned, wo_turned, prev, deps=(), gates=()):
    count = len(xs)
    total, width = xs[0].shape
    hidden = wi_turned.shape[0]
    tile = min(256, hidden)
    rows = pl.BlockSpec((tile, width), lambda f, *_: (f, 0))
    cols = pl.BlockSpec((width, tile), lambda f, *_: (0, f))
    anywhere = pl.BlockSpec(memory_space=pl.ANY)
    first, last = prev is None, t == groups - 1
    return run(
        partial(slice_kernel, t, groups, first, last),
        (*xs, *cots, gain, bias, wi_turned, wo_turned, *(() if first else prev)),
        [shaped((width, hidden) if last else (hidden, width), F32)] * 2,
        deps,
        (meta,),
        (hidden // tile,),
        [anywhere] * (2 * count)
        + [whole((1, width))] * 2
        + [rows] * (2 if first else 4),
        [cols if last else rows] * 2,
        [pltpu.VMEM((tile, width), F32)] * 2
        + [pltpu.VMEM((count, total, width), BF)] * 2
        + [pltpu.SemaphoreType.DMA((count, 2))],
        micros=18,
        gates=gates,
    )


def back_kernel(ids_ref, mat_ref, rows_ref, dmix_ref, dattn_ref):
    lanes = lax.broadcasted_iota(jnp.int32, (QB, rows_ref.shape[0]), 1)
    x = dot_nn(one_hot(ids_ref[...], lanes), rows_ref[...]).astype(BF)
    dmix_ref[...] = x
    dattn_ref[...] = dot_nt(x, mat_ref[...]).astype(BF)


def back_in(ids_col, mat, rows, deps=()):
    total, width = rows.shape
    block = pl.BlockSpec((QB, width), lambda r: (r, 0))
    return run(
        back_kernel,
        (ids_col, mat, rows),
        [shaped(rows.shape)] * 2,
        deps,
        (),
        (total // QB,),
        [pl.BlockSpec((QB, 1), lambda r: (r, 0)), whole(mat.shape), whole(rows.shape)],
        [block] * 2,
        micros=7,
    )


def shared_kernel(turn, count, norm, left_ref, *refs):
    rights, refs = refs[:count], refs[count:]
    if norm:
        mats, (gains_ref, small_ref, out, tops) = refs[:count], refs[count:]
    else:
        (out,) = refs
    experts, step = out.shape[0], out.shape[2]
    left = jnp.transpose(left_ref[...]) if turn else left_ref[...]

    def put(values, cols):
        values = values.astype(BF)
        for e in range(experts):
            part = values[e * step : (e + 1) * step]
            out[e, 0, :, cols : cols + values.shape[1]] = part

    if norm:

        @pl.when(pl.program_id(0) == 0)
        def _():
            for n, right in enumerate(rights):
                tops[n : n + 1] = jnp.sum(right[...].astype(F32), 0, keepdims=True)

    cols, with_gain, with_bias = 0, 0.0, 0.0
    for n, right in enumerate(rights):
        sums = dot_nn(left, right[...])
        if norm:
            mat = mats[n][...].astype(F32)
            with_gain = with_gain + jnp.sum(mat * sums, -1, keepdims=True)
            with_bias = with_bias + jnp.sum(mat * tops[n : n + 1], -1, keepdims=True)
        put(sums, cols)
        cols += right.shape[1]
    if norm:
        with_gain = (with_gain - gains_ref[:, 1:2] * with_bias) / gains_ref[:, 0:1]
        rest = jnp.zeros((sums.shape[0], 120), F32)
        extra = jnp.concatenate([jnp.transpose(small_ref[...]), rest], -1)
        lane = lax.broadcasted_iota(jnp.int32, (1, 128), 1)
        extra = jnp.where(lane == 8, with_gain, jnp.where(lane == 9, with_bias, extra))
        put(extra, cols)


def shared_grads(left, turned, rights, experts, groups, norm=(), deps=(), gates=()):
    total = rights[0].shape[0]
    features = left.shape[0 if turned else 1]
    step, block = features // (experts * groups), features // groups
    width = sum(r.shape[1] for r in rights) + (128 if norm else 0)
    rows = pl.BlockSpec((block, total), lambda g: (g, 0))
    specs = [rows if turned else pl.BlockSpec((total, block), lambda g: (0, g))]
    specs += [whole(r.shape) for r in rights]
    args, scratch = [left, *rights], []
    if norm:
        mats, gains, small = norm
        args += [*mats, gains, small]
        specs += [pl.BlockSpec((block, m.shape[1]), lambda g: (g, 0)) for m in mats]
        specs += [pl.BlockSpec((block, 16), lambda g: (g, 0))]
        specs += [pl.BlockSpec((8, block), lambda g: (0, g))]
        scratch = [pltpu.VMEM((8, rights[0].shape[1]), F32)]
    shape = (experts, groups, step, width)
    return run(
        partial(shared_kernel, not turned, len(rights), bool(norm)),
        args,
        [shaped(shape)],
        deps,
        (),
        (groups,),
        specs,
        [pl.BlockSpec((experts, 1, step, width), lambda g: (0, g, 0, 0))],
        scratch,
        micros=4 * len(rights),
        gates=gates,
    )


def total_kernel(meta, first_ref, second_ref, *outs):
    groups = len(outs)
    g = pl.program_id(0)
    for s in range(groups):

        @pl.when(g == lax.rem(meta[1] + s, groups))
        def _(out=outs[s]):
            col = 0
            for ref in (first_ref, second_ref):
                total = ref[0, 0].astype(F32)
                for e in range(1, ref.shape[0]):
                    total = total + ref[e, 0].astype(F32)
                out[:, col : col + total.shape[1]] = total.astype(out.dtype)
                col += total.shape[1]


def total_over(meta, first, second, deps=(), gates=()):
    groups, step = first.shape[1:3]
    width = first.shape[3] + second.shape[3]
    specs = []
    for a in (first, second):
        block = (a.shape[0], 1, *a.shape[2:])
        specs.append(pl.BlockSpec(block, lambda g, *_: (0, g, 0, 0)))
    return run(
        total_kernel,
        (first, second),
        [shaped((step, width), F32)] + [shaped((step, width))] * (groups - 1),
        deps,
        (meta,),
        (groups,),
        specs,
        [whole((step, width))] * groups,
        micros=5,
        gates=gates,
    )


def final_kernel(*refs):
    ins, (o_ref, q_ref, k_ref, v_ref, *small) = refs[:-8], refs[-8:]
    total = ins[0][...]
    for ref in ins[1:]:
        total = total + ref[...].astype(F32)
    width = o_ref.shape[1]
    for n, ref in enumerate((o_ref, q_ref, k_ref, v_ref)):
        ref[...] = total[:, n * width : (n + 1) * width]
    turned = jnp.transpose(total[:, 4 * width :])
    for n, ref in zip((8, 9, 0, 1), small):
        ref[...] = turned[n : n + 1]


def final(parts, width):
    step = parts[0].shape[0]
    return run(
        final_kernel,
        parts,
        [shaped((step, width), F32)] * 4 + [shaped((1, step), F32)] * 4,
        micros=2,
    )


def first_kernel(*refs):
    grads, mats = refs[:3], refs[3:6]
    seq_ref, dmix_ref, gain_ref, ids_ref, out_ref, rows = refs[6:]
    r = pl.program_id(0)
    size = seq_ref.shape[0]
    grad = dot_nt(grads[0][...], mats[0][...])
    for n in (1, 2):
        grad = grad + dot_nt(grads[n][...], mats[n][...])
    normed, inverse = norm_rows(seq_ref[...].astype(F32))
    back = dmix_ref[...].astype(F32) + norm_back(grad, normed, inverse, gain_ref[...])
    rows[pl.ds(pl.multiple_of(r * size, size), size)] = back.astype(BF)

    @pl.when(r == pl.num_programs(0) - 1)
    def _():
        to_experts(ids_ref, rows, out_ref)


def first_back(grads, mats, seq, dmix, gain, ids_row, deps=()):
    total, width = seq.shape
    block = pl.BlockSpec((QB, width), lambda r: (r, 0))
    return run(
        first_kernel,
        (*grads, *mats, seq, dmix, gain, ids_row),
        [shaped((total, width))],
        deps,
        (),
        (total // QB,),
        [block] * 3
        + [whole((width, width))] * 3
        + [block] * 2
        + [whole((1, width)), whole((1, total))],
        [whole((total, width))],
        [pltpu.VMEM((total, width), BF)],
        micros=16,
    )[0]


def local(
    n_grp,
    n_exp,
    tokens,
    cotangent,
    arrival,
    seq_length,
    w_q,
    w_k,
    w_v,
    w_o,
    ln1_gain,
    ln1_bias,
    ln2_gain,
    ln2_bias,
    w_in,
    w_out,
):
    me, grp = lax.axis_index("exp"), lax.axis_index("grp")
    meta = jnp.stack([me, grp]).astype(jnp.int32)
    width = tokens.shape[1]
    step = w_q.shape[0]
    hidden = w_in.shape[2] // n_grp
    both = ("grp", "exp")

    def swap(a, k):
        return lax.ppermute(a, "exp", [(i, i ^ k) for i in range(n_exp)])

    def shift(a, k):
        return lax.ppermute(a, "grp", [(i, (i + k) % n_grp) for i in range(n_grp)])

    def exchange(rows):
        return lax.all_to_all(rows, "exp", split_axis=0, concat_axis=0, tiled=True)

    bits = []
    while 2 ** len(bits) < n_exp:
        bits.append(2 ** len(bits))
    orders = [bits[:0:-1] + bits[:1], bits[1:] + bits[:1]]

    def gather_pair(own, cut):
        first = lambda a: a[0] if isinstance(a, tuple) else a[:, :cut]
        second = lambda a: a[1] if isinstance(a, tuple) else a[:, cut:]
        have = {0: own}
        for r in sorted(range(1, n_exp), key=lambda r: (bin(r).count("1"), -r)):
            b, c = (max((b for b in bits if r & b), key=order.index) for order in orders)
            if b == c and not isinstance(have[r ^ b], tuple):
                have[r] = swap(have[r ^ b], b)
            else:
                have[r] = (swap(first(have[r ^ b]), b), swap(second(have[r ^ c]), c))
        return [have[r] for r in range(n_exp)]

    def line_step(t, up, down):
        up = lax.ppermute(up, "grp", [(i, i + 1) for i in range(t - 1, n_grp - 1)])
        down = lax.ppermute(down, "grp", [(i + 1, i) for i in range(n_grp - t)])
        return up, down

    def line(a):
        steps = [(a, a)]
        for t in range(1, n_grp):
            steps.append(line_step(t, *steps[-1]))
        return steps

    ids_row = arrival
    ids_col = arrival.reshape(-1, 1)
    flag = seq_length

    gains = jnp.stack([ln1_gain, ln1_bias, ln2_gain, ln2_bias])
    mine = jnp.zeros((16, width), BF)
    mine = lax.dynamic_update_slice(mine, gains, (0, (grp * n_exp + me) * step))
    mine = jnp.concatenate([w_q, w_k, mine, w_v, w_o])
    mine = [mine] + [shift(mine, k) for k in range(1, n_grp)]
    arrived = exchange(tokens)
    w_first, w_second = w_in[0], w_out[0]
    wi_turned, wo_turned = turn_slices(meta, w_first, w_second, hidden)
    dact = act_grad(cotangent, w_second)
    pair_qk, pair_vo = stack(mine, (2 * step + 16, 2 * step), deps=(arrived, dact, wi_turned))
    pieces = gather_pair(pair_qk, step)
    all_vo = lax.all_gather(pair_vo, "exp", axis=0)

    full = (n_grp, n_exp, step, width)
    is_cut = lambda a: isinstance(a, tuple)
    pieces_q = [(a[0], 0) if is_cut(a) else (a, 0) for a in pieces]
    pieces_k = [(a[1], 0) if is_cut(a) else (a, 1) for a in pieces]
    pieces_g = [
        (a[1], step // 16) if is_cut(a) else (a, 2 * step // 16) for a in pieces
    ]
    pieces_v, pieces_o = [(all_vo, 0)], [(all_vo, 1)]

    cot_line, x_line = [(cotangent,) * 2], []

    def forward(steps, gated=None):
        if len(steps) < n_grp:
            steps.append(line_step(len(steps), *(gated or steps[-1])))
        return steps[-1]

    forward(cot_line)
    seq, ln_one, ln_turned, q, k, mat_q, mat_k, gains = enter(
        meta, ids_col, arrived, pieces_q, pieces_k, pieces_g, full
    )
    v, mat_v, (cot_gated,) = project(meta, ln_one, pieces_v, full, gates=cotangent)
    cot_all = lax.all_gather(cot_gated, "grp", axis=0)
    attn, lse = attend(flag, q, k, v)
    mat_o, leaving = mix(meta, attn, seq, ids_row, pieces_o, full)
    x = exchange(leaving)

    act, dx, sums_two = expert(
        x, cotangent, gains[2], gains[3], w_first, dact
    )
    x_line = [(x,) * 2]
    forward(x_line)
    output = expert_out(x, act, w_second)

    def slices(t, sums, deps=(), gates=()):
        xs = list(x_line[t])[: 2 if t else 1]
        cots = [cot_all] * 2 if t > 1 else list(cot_line[t])[: len(xs)]
        last = (gains[2], gains[3], wi_turned, wo_turned, sums, deps, gates)
        return slice_grads(meta, t, n_grp, xs, cots, *last)

    slice_sums, x_line[1] = slices(0, None, deps=output, gates=x_line[1])
    back = exchange(dx)
    dmix, dattn = back_in(ids_col, mat_o, back, deps=slice_sums)
    forward(x_line)

    (first,) = shared_grads(attn, False, [dmix], n_exp, n_grp)
    grads = attend_back(flag, q, k, v, attn, dattn, lse, 0, 1, deps=first)
    first = exchange(first)
    (second,), x_line[-1] = shared_grads(
        ln_turned,
        True,
        grads,
        n_exp,
        n_grp,
        ((mat_q, mat_k, mat_v), gains[4], sums_two),
        gates=x_line[-1],
    )
    while len(x_line) < n_grp:
        forward(x_line)
    dfirst = first_back(
        grads, (mat_q, mat_k, mat_v), seq, dmix, gains[0], ids_row, deps=(first, second)
    )
    second = exchange(second)
    for t in range(1, n_grp):
        deps = (dfirst,) if t == 1 else ()
        if t == n_grp - 1:
            deps = (deps, slice_sums)
            parts, (dfirst,) = total_over(meta, first, second, deps, dfirst)
            deps = parts
            parts = [parts[0]] + [shift(a, n + 1) for n, a in enumerate(parts[1:])]
        slice_sums = slices(t, slice_sums, deps)
    grad_x = exchange(dfirst)
    grad_w_in, grad_w_out = slice_sums
    grad_w_o, *grads = final(parts, width)
    grads, small = grads[:3], [a[0] for a in grads[3:]]

    return (
        output,
        grad_x,
        *grads,
        grad_w_o,
        *small,
        grad_w_in[None],
        grad_w_out[None],
    )


def solution(mesh):
    both = ("grp", "exp")
    rows, flat, mats = P(both, None), P(both), P("exp", None, None)
    split = P("exp", None, "grp")
    return jax.shard_map(
        partial(local, mesh.shape["grp"], mesh.shape["exp"]),
        mesh=mesh,
        in_specs=(rows, rows, rows, flat) + (rows,) * 4 + (flat,) * 4 + (mats, mats),
        out_specs=(rows,) * 6 + (flat,) * 4 + (split, split),
        check_vma=False,
    )
```
